32 devices in a mesh: dp: 16 (over z, x, core), space: 2 (over y).
Axes of the slice: x: 2, y: 2, z: 4, core: 2. Of those that a mesh axis runs over, the one named last changes fastest.
Arguments:
- field_in: bfloat16 [1, 512, 512, 128], P(None, 'space', 'dp'), may hold values from -6 to 6
- pre_act: bfloat16 [1, 512, 512, 128], P(None, 'space', 'dp'), may hold values from -8 to 8
- cotangent: bfloat16 [1, 512, 512, 128], P(None, 'space', 'dp'), may hold values from -6 to 6
- spec_weight: bfloat16 [64, 64, 2, 128, 128], P('dp', 'space'), may hold values from -0.25 to 0.25
- local_weight: bfloat16 [128, 128], replicated, may hold values from -0.5 to 0.5
Outputs:
- grad_input: bfloat16 [1, 512, 512, 128], P(None, 'space', 'dp')
- grad_spectral: bfloat16 [64, 64, 2, 128, 128], P('dp', 'space')
- grad_local: float32 [128, 128], replicated
- grad_bias: float32 [128], replicated
The draws below stay inside these ranges and needn't reach their ends.
All inputs are finite; a program needn't handle non-finite values.
Results may differ from the reference program's by a relative error of at most 0.0075.
The reference program's roundings to bfloat16 on the way (of `delta_field`, `y_table`, `x_table`, `along_y`, `mode_back`, `along_x` and `spectral_part`) count: a program that leaves them out, or rounds other values in their place, can miss the bound.
Values may be sent and summed in bfloat16 or wider, within the bound.
No kernel may reach another device: no remote copies, remote signals or barrier semaphores. Data moves between devices by JAX's collectives and lax.ppermute only.
A program may use at most 128 MiB of HBM per device.

```python
import math
import jax
import jax.numpy as jnp
from jax import lax

C = 128
KX = 64
KY = 64
NX = 512
NY = 512
BATCH = 1


def shard_levels(stream_key, extent, cuts, smallest, high):
    gain, own = 1.0, jax.random.fold_in(stream_key, 6)
    for dim, shards_of in cuts:
        draws = jnp.exp(jax.random.uniform(jax.random.fold_in(own, dim), (shards_of,), jnp.float32, smallest / len(cuts), high / len(cuts)))
        gain = gain * jnp.repeat(draws, extent[dim] // shards_of).reshape([-1 if axis == dim else 1 for axis in range(len(extent))])
    return gain


def noise(own_key, shape, spread, bound, pieces=(), kind=jnp.bfloat16):
    loudness = shard_levels(own_key, shape, pieces, -0.22, 0.18) if pieces else 1.0
    drawn = jax.random.normal(own_key, shape, jnp.float32) * spread * loudness
    return jnp.minimum(jnp.maximum(drawn, -bound), bound).astype(kind)


def setup_inputs(seed: int = 0) -> dict:
    splits = jax.random.split(jax.random.key(seed), 6)
    return {
        "field_in": noise(splits[0], (BATCH, NX, NY, C), 1.0, 6.0, ((1, 2), (2, 16))),
        "pre_act": noise(splits[1], (BATCH, NX, NY, C), 1.5, 8.0, ((1, 2), (2, 16))),
        "cotangent": noise(splits[2], (BATCH, NX, NY, C), 1.0, 6.0, ((1, 2), (2, 16))),
        "spec_weight": noise(splits[3], (KX, KY, 2, C, C), (4 * C) ** -0.5, 0.25, ((0, 16), (1, 2))),
        "local_weight": noise(splits[4], (C, C), C ** -0.5, 0.5),
    }


highest = lax.Precision.HIGHEST
root_two_pi = 0.7978845608028654
cubic_coef = 0.044715

def gelu_slope(values):
    tangent = jnp.tanh(root_two_pi * (values + cubic_coef * values * values * values))
    return 0.5 * (1.0 + tangent) + 0.5 * values * (1.0 - tangent * tangent) * root_two_pi * (1.0 + 3.0 * cubic_coef * values * values)

def y_basis(grid_cols, ky_count):
    positions = jnp.arange(grid_cols, dtype=jnp.int32)
    frequency = jnp.arange(ky_count, dtype=jnp.int32)
    phases = positions[:, None] * frequency[None, :] % grid_cols
    angles = phases.astype(jnp.float32) * (2.0 * math.pi / grid_cols)
    basis_table = jnp.stack([jnp.cos(angles), -jnp.sin(angles)], axis=2).reshape(grid_cols, 2 * ky_count)
    return basis_table.astype(jnp.bfloat16)

def x_basis(grid_rows, kx_count):
    positions = jnp.arange(grid_rows, dtype=jnp.int32)
    mode_index = jnp.arange(kx_count, dtype=jnp.int32)
    frequency = jnp.where(mode_index < kx_count // 2, mode_index, mode_index - kx_count)
    phases = frequency[:, None] * positions[None, :] % grid_rows
    angles = phases.astype(jnp.float32) * (2.0 * math.pi / grid_rows)
    cosine = jnp.cos(angles)
    sine = jnp.sin(angles)
    upper_rows = jnp.stack([cosine, sine], axis=1)
    lower_rows = jnp.stack([-sine, cosine], axis=1)
    return jnp.stack([upper_rows, lower_rows], axis=0).astype(jnp.bfloat16)

def rounded(values):
    return lax.optimization_barrier(values.astype(jnp.bfloat16)).astype(jnp.float32)

def reference(field_in, pre_act, cotangent, spec_weight, local_weight):
    y_table = y_basis(NY, KY).astype(jnp.float32)
    x_table = x_basis(NX, KX).astype(jnp.float32)
    local_float = local_weight.astype(jnp.float32)

    def forward_sample(inputs):
        sample, pre_sample, cot_sample = inputs
        delta_field = (cot_sample.astype(jnp.float32) * gelu_slope(pre_sample.astype(jnp.float32))).astype(jnp.bfloat16)
        stacked = jnp.stack([sample, delta_field]).astype(jnp.float32)
        along_y = rounded(jnp.einsum('fxyc,yr->fxrc', stacked, y_table, precision=highest))
        along_y = along_y.reshape(2, NX, KY, 2, C)
        spectra = jnp.einsum('qjpx,fxkpc->fjkqc', x_table, along_y, precision=highest).astype(jnp.bfloat16)
        local_term = jnp.einsum('xyc,xyo->co', sample.astype(jnp.float32), delta_field.astype(jnp.float32), precision=highest)
        bias_term = lax.optimization_barrier(jnp.sum(delta_field.astype(jnp.float32), axis=(0, 1)))
        return (spectra, delta_field, local_term, bias_term)
    spectra, deltas, local_terms, bias_terms = lax.map(forward_sample, (field_in, pre_act, cotangent))
    ky_scale = jnp.where(jnp.arange(KY, dtype=jnp.int32) == 0, 1.0, 2.0).astype(jnp.float32) / (NX * NY)
    per_mode = jnp.moveaxis(spectra, 2, 0)

    def mode_column(inputs):
        column, weights = inputs
        input_part = column[:, 0].astype(jnp.float32)
        delta_part = column[:, 1].astype(jnp.float32)
        products = jnp.einsum('bkqc,bkpo->kqpco', input_part, delta_part, precision=highest)
        grad_real = products[:, 0, 0] + products[:, 1, 1]
        grad_imag = products[:, 0, 1] - products[:, 1, 0]
        grad_mode = (jnp.stack([grad_real, grad_imag], axis=1) * (ky_scale / BATCH)[:, None, None, None]).astype(jnp.bfloat16)
        adjoint = jnp.einsum('bkpo,kqco->bkpqc', delta_part, weights.astype(jnp.float32), precision=highest)
        back_real = adjoint[:, :, 0, 0] + adjoint[:, :, 1, 1]
        back_imag = adjoint[:, :, 1, 0] - adjoint[:, :, 0, 1]
        mode_grad = (jnp.stack([back_real, back_imag], axis=2) * ky_scale[None, :, None, None]).astype(jnp.bfloat16)
        return (grad_mode, mode_grad)
    grad_spectral, mode_back = lax.map(mode_column, (per_mode, spec_weight))
    back_per_sample = jnp.moveaxis(mode_back, 1, 0)

    def input_grad(inputs):
        modes, delta_field = inputs
        along_x = rounded(jnp.einsum('qjpx,jkqc->xkpc', x_table, modes.astype(jnp.float32), precision=highest))
        along_x = along_x.reshape(NX, 2 * KY, C)
        spectral_part = rounded(jnp.einsum('xrc,yr->xyc', along_x, y_table, precision=highest))
        local_part = jnp.einsum('xyo,co->xyc', delta_field.astype(jnp.float32), local_float, precision=highest)
        return (spectral_part + local_part).astype(jnp.bfloat16)
    grad_input = lax.map(input_grad, (back_per_sample, deltas))
    grad_local = lax.optimization_barrier(jnp.sum(local_terms, axis=0)) / BATCH
    grad_bias = lax.optimization_barrier(jnp.sum(bias_terms, axis=0)) / BATCH
    return (grad_input, grad_spectral, grad_local, grad_bias)
```

```python
import math

import jax
import jax.numpy as jnp
from jax import lax
from jax.experimental import pallas as pl
from jax.experimental.pallas import tpu as pltpu
from jax.sharding import PartitionSpec as P

root_two_pi = 0.7978845608028654
cubic_coef = 0.044715
f32 = jnp.float32
bf16 = jnp.bfloat16
vmem_bytes = 40 * 1024 * 1024


def gelu_slope(values):
    square = values * values
    tangent = jnp.tanh(root_two_pi * (values + cubic_coef * square * values))
    return 0.5 * (1.0 + tangent) + 0.5 * values * (1.0 - tangent * tangent) * root_two_pi * (
        1.0 + 3.0 * cubic_coef * square
    )


def params(steps=1):
    return pltpu.CompilerParams(
        vmem_limit_bytes=vmem_bytes, dimension_semantics=("arbitrary",) * steps
    )


def whole(shape):
    return pl.BlockSpec(shape, lambda *_: (0,) * len(shape))


def x_transform(table, wide, narrow, out_ref):
    rows, columns, channels = out_ref.shape
    grid_rows = table.shape[1]
    for y in range(0, columns, 2):
        pair = [
            wide[pl.ds(y + i, grid_rows, stride=columns), :].astype(bf16) for i in range(2)
        ]
        sums = jnp.dot(table, jnp.concatenate(pair, axis=1), preferred_element_type=f32)
        for i in range(2):
            narrow[pl.ds(y + i, rows, stride=columns), :] = sums[:, i * channels : (i + 1) * channels]
    out_ref[...] = narrow[...].reshape(rows, columns, channels).astype(bf16)


def delta_kernel(table_ref, pre_ref, cot_ref, delta_ref, out_ref, wide, narrow):
    grid_rows, columns, channels = pre_ref.shape
    step = 8

    def slab(i, carry):
        rows = pl.ds(pl.multiple_of(i * step, step), step)
        slope = gelu_slope(pre_ref[rows].astype(f32))
        delta = (cot_ref[rows].astype(f32) * slope).astype(bf16)
        delta_ref[rows] = delta
        wide[pl.ds(pl.multiple_of(i * step * columns, step * columns), step * columns), :] = (
            delta.astype(f32).reshape(step * columns, channels)
        )
        return carry

    lax.fori_loop(0, grid_rows // step, slab, 0, unroll=2)
    x_transform(table_ref[...], wide, narrow, out_ref)


def delta_call(table, pre_act, cotangent):
    grid_rows, columns, channels = pre_act.shape
    rows = table.shape[0]
    block = min(16, columns)
    field = pl.BlockSpec((grid_rows, block, channels), lambda i: (0, i, 0))
    return pl.pallas_call(
        delta_kernel,
        grid=(columns // block,),
        in_specs=[whole(table.shape), field, field],
        out_specs=[field, pl.BlockSpec((rows, block, channels), lambda i: (0, i, 0))],
        out_shape=[
            jax.ShapeDtypeStruct(pre_act.shape, bf16),
            jax.ShapeDtypeStruct((rows, columns, channels), bf16),
        ],
        scratch_shapes=[
            pltpu.VMEM((grid_rows * block, channels), f32),
            pltpu.VMEM((rows * block, channels), f32),
        ],
        compiler_params=params(),
        cost_estimate=pl.CostEstimate(
            flops=2 * rows * pre_act.size, bytes_accessed=8 * pre_act.size, transcendentals=pre_act.size
        ),
        name="delta_and_x_sums",
    )(table, pre_act, cotangent)


def input_kernel(table_ref, field_ref, delta_ref, out_ref, local_ref, bias_ref, wide, narrow):
    grid_rows, columns, channels = field_ref.shape
    field = field_ref[...].reshape(grid_rows * columns, channels)
    delta = delta_ref[...].reshape(grid_rows * columns, channels)
    wide[...] = field.astype(f32)
    x_transform(table_ref[...], wide, narrow, out_ref)
    local = lax.dot_general(field, delta, (((0,), (0,)), ((), ())), preferred_element_type=f32)
    bias = jnp.sum(delta.astype(f32).reshape(-1, 8, channels), axis=0)

    @pl.when(pl.program_id(0) == 0)
    def _():
        local_ref[...] = local
        bias_ref[...] = bias

    @pl.when(pl.program_id(0) > 0)
    def _():
        local_ref[...] += local
        bias_ref[...] += bias


def input_call(table, field_in, delta):
    grid_rows, columns, channels = field_in.shape
    rows = table.shape[0]
    block = min(16, columns)
    field = pl.BlockSpec((grid_rows, block, channels), lambda i: (0, i, 0))
    return pl.pallas_call(
        input_kernel,
        grid=(columns // block,),
        in_specs=[whole(table.shape), field, field],
        out_specs=[
            pl.BlockSpec((rows, block, channels), lambda i: (0, i, 0)),
            whole((channels, channels)),
            whole((8, channels)),
        ],
        out_shape=[
            jax.ShapeDtypeStruct((rows, columns, channels), bf16),
            jax.ShapeDtypeStruct((channels, channels), f32),
            jax.ShapeDtypeStruct((8, channels), f32),
        ],
        scratch_shapes=[
            pltpu.VMEM((grid_rows * block, channels), f32),
            pltpu.VMEM((rows * block, channels), f32),
        ],
        compiler_params=params(),
        cost_estimate=pl.CostEstimate(
            flops=2 * (rows + channels) * field_in.size, bytes_accessed=4 * field_in.size, transcendentals=0
        ),
        name="input_x_sums_and_local",
    )(table, field_in, delta)


def y_transform_kernel(table_ref, lines_ref, *out_refs):
    sources, rows, columns, channels = lines_ref.shape
    frequencies = rows // 2
    own = len(out_refs) // 2
    size = out_refs[0].shape[1]
    table = table_ref[...]
    for t in range(frequencies):
        lines = jnp.concatenate(
            [
                lines_ref[:, 2 * t + part].reshape(sources * columns, channels)
                for part in range(2)
            ],
            axis=0,
        )
        sums = jnp.dot(table, lines, preferred_element_type=f32).astype(bf16)
        for block, out_ref in enumerate(out_refs):
            held = t if block < own else frequencies - 1 - t
            if 0 <= held < frequencies - 1:
                out_ref[held] = sums[block * size : (block + 1) * size]


def y_transform_call(table, lines, blocks, size):
    sources, rows, columns, channels = lines.shape
    held = rows // 2 - 1
    return pl.pallas_call(
        y_transform_kernel,
        out_shape=[jax.ShapeDtypeStruct((held, size, channels), bf16)] * blocks,
        compiler_params=pltpu.CompilerParams(vmem_limit_bytes=vmem_bytes),
        cost_estimate=pl.CostEstimate(
            flops=rows * table.size * channels, bytes_accessed=4 * lines.size, transcendentals=0
        ),
        name="y_sums",
    )(table, lines)


def turned(values):
    rows = values.shape[0]
    even = lax.broadcasted_iota(jnp.int32, values.shape, 0) % 2 == 0
    up = pltpu.roll(values, rows - 1, 0)
    down = pltpu.roll(values, 1, 0)
    return jnp.concatenate([values, jnp.where(even, up, -down)], axis=1)


def back_kernel(scale_ref, weight_ref, *refs):
    part_refs, (back_ref, delta_ref) = refs[:-2], refs[-2:]
    modes = weight_ref.shape[1]
    total = part_refs[0][0].astype(f32)
    for ref in part_refs[1:]:
        total = total + ref[0].astype(f32)
    delta = total.astype(bf16)
    delta_ref[0] = delta
    both = turned(delta.astype(f32)).astype(bf16)
    rows = []
    for mode in range(modes):
        weight = jnp.concatenate([weight_ref[0, mode, 0], weight_ref[0, mode, 1]], axis=1)
        rows.append(
            lax.dot_general(
                both[2 * mode : 2 * mode + 2],
                weight,
                (((1,), (1,)), ((), ())),
                preferred_element_type=f32,
            )
        )
    back_ref[0] = (jnp.concatenate(rows, axis=0) * scale_ref[...]).astype(bf16)


def back_call(scale_rows, weight, parts):
    held, modes, _, channels, _ = weight.shape
    block = min(16, modes)
    part = pl.BlockSpec((1, 2 * block, channels), lambda j, k: (j, k, 0))
    shape = jax.ShapeDtypeStruct((held, 2 * modes, channels), bf16)
    return pl.pallas_call(
        back_kernel,
        grid=(held, modes // block),
        in_specs=[
            pl.BlockSpec((2 * block, channels), lambda j, k: (k, 0)),
            pl.BlockSpec((1, block, 2, channels, channels), lambda j, k: (j, k, 0, 0, 0)),
        ]
        + [part] * len(parts),
        out_specs=[part, part],
        out_shape=[shape, shape],
        compiler_params=params(2),
        cost_estimate=pl.CostEstimate(
            flops=4 * weight.size, bytes_accessed=2 * weight.size, transcendentals=0
        ),
        name="mode_back",
    )(scale_rows, weight, *parts)


def outer_kernel(scale_ref, delta_ref, *refs):
    part_refs, out_ref = refs[:-1], refs[-1]
    modes = out_ref.shape[1]
    channels = out_ref.shape[-1]
    total = part_refs[0][0].astype(f32)
    for ref in part_refs[1:]:
        total = total + ref[0].astype(f32)
    field = total.astype(bf16).astype(f32) * scale_ref[...]
    across = field.T
    delta = turned(delta_ref[0].astype(f32))
    for mode in range(modes):
        real = across[:, 2 * mode : 2 * mode + 1]
        imag = across[:, 2 * mode + 1 : 2 * mode + 2]
        first = delta[2 * mode : 2 * mode + 1]
        second = delta[2 * mode + 1 : 2 * mode + 2]
        product = (real * first + imag * second).astype(bf16)
        out_ref[0, mode, 0] = product[:, :channels]
        out_ref[0, mode, 1] = product[:, channels:]


def outer_call(scale_rows, delta, parts):
    held, rows, channels = delta.shape
    modes = rows // 2
    block = min(16, modes)
    part = pl.BlockSpec((1, 2 * block, channels), lambda j, k: (j, k, 0))
    return pl.pallas_call(
        outer_kernel,
        grid=(held, modes // block),
        in_specs=[pl.BlockSpec((2 * block, channels), lambda j, k: (k, 0))]
        + [part] * (1 + len(parts)),
        out_specs=pl.BlockSpec(
            (1, block, 2, channels, channels), lambda j, k: (j, k, 0, 0, 0)
        ),
        out_shape=jax.ShapeDtypeStruct((held, modes, 2, channels, channels), bf16),
        compiler_params=params(2),
        cost_estimate=pl.CostEstimate(
            flops=6 * held * modes * channels * channels,
            bytes_accessed=4 * held * modes * channels * channels,
            transcendentals=0,
        ),
        name="grad_spectral",
    )(scale_rows, delta, *parts)


def y_inverse_kernel(table_ref, *refs):
    part_refs, out_ref = refs[:-1], refs[-1]
    targets, rows, columns, channels = out_ref.shape
    frequencies = rows // 2
    own = len(part_refs) // 2
    size = part_refs[0].shape[1]
    table = table_ref[...]
    for t in range(frequencies):
        first = 0 if t < frequencies - 1 else own
        last = 2 * own if t > 0 else own
        modes = jnp.concatenate(
            [
                part_refs[block][t if block < own else frequencies - 1 - t]
                for block in range(first, last)
            ],
            axis=0,
        )
        sums = lax.dot_general(
            table[first * size : last * size],
            modes,
            (((0,), (0,)), ((), ())),
            preferred_element_type=f32,
        ).astype(bf16)
        for part in range(2):
            out_ref[:, 2 * t + part] = sums[
                part * targets * columns : (part + 1) * targets * columns
            ].reshape(targets, columns, channels)


def y_inverse_call(table, parts, targets, columns):
    held, size, channels = parts[0].shape
    rows = 2 * (held + 1)
    return pl.pallas_call(
        y_inverse_kernel,
        out_shape=jax.ShapeDtypeStruct((targets, rows, columns, channels), bf16),
        compiler_params=pltpu.CompilerParams(vmem_limit_bytes=vmem_bytes),
        cost_estimate=pl.CostEstimate(
            flops=rows * table.size * channels,
            bytes_accessed=4 * targets * rows * columns * channels,
            transcendentals=0,
        ),
        name="y_inverse",
    )(table, *parts)


def final_kernel(table_ref, lines_ref, delta_ref, local_ref, out_ref, narrow, wide):
    rows, columns, channels = lines_ref.shape
    grid_rows = out_ref.shape[0]
    narrow[...] = lines_ref[...].reshape(rows * columns, channels).astype(f32)
    table = table_ref[...]
    for y in range(0, columns, 2):
        pair = [narrow[pl.ds(y + i, rows, stride=columns), :].astype(bf16) for i in range(2)]
        sums = lax.dot_general(
            table,
            jnp.concatenate(pair, axis=1),
            (((0,), (0,)), ((), ())),
            preferred_element_type=f32,
        )
        for i in range(2):
            wide[pl.ds(y + i, grid_rows, stride=columns), :] = sums[
                :, i * channels : (i + 1) * channels
            ]
    weight = local_ref[...]
    step = 16

    def slab(i, carry):
        rows_here = pl.ds(pl.multiple_of(i * step, step), step)
        flat = pl.ds(pl.multiple_of(i * step * columns, step * columns), step * columns)
        local = lax.dot_general(
            delta_ref[rows_here].reshape(step * columns, channels),
            weight,
            (((1,), (1,)), ((), ())),
            preferred_element_type=f32,
        )
        spectral = wide[flat, :].astype(bf16).astype(f32)
        out_ref[rows_here] = (spectral + local).astype(bf16).reshape(step, columns, channels)
        return carry

    lax.fori_loop(0, grid_rows // step, slab, 0, unroll=2)


def final_call(table, lines, delta, local_weight):
    rows, columns, channels = lines.shape
    grid_rows = delta.shape[0]
    block = min(16, columns)
    field = pl.BlockSpec((grid_rows, block, channels), lambda i: (0, i, 0))
    return pl.pallas_call(
        final_kernel,
        grid=(columns // block,),
        in_specs=[
            whole(table.shape),
            pl.BlockSpec((rows, block, channels), lambda i: (0, i, 0)),
            field,
            whole(local_weight.shape),
        ],
        out_specs=field,
        out_shape=jax.ShapeDtypeStruct(delta.shape, bf16),
        scratch_shapes=[
            pltpu.VMEM((rows * block, channels), f32),
            pltpu.VMEM((grid_rows * block, channels), f32),
        ],
        compiler_params=params(),
        cost_estimate=pl.CostEstimate(
            flops=2 * (rows + channels) * delta.size, bytes_accessed=5 * delta.size, transcendentals=0
        ),
        name="x_inverse_and_local",
    )(table, lines, delta, local_weight)


def on_device(field_in, pre_act, cotangent, spec_weight, local_weight):
    batch_size, slab_rows, col_block, channels = field_in.shape
    space_count = lax.axis_size("space")
    data_count = lax.axis_size("dp")
    grid_rows = slab_rows * space_count
    grid_cols = col_block * data_count
    kx_local, ky_local = spec_weight.shape[:2]
    half = data_count // 2
    half_cols = half * col_block
    row_count = 2 * (kx_local + 1)
    data_index = lax.axis_index("dp")
    space_index = lax.axis_index("space")
    upper = data_index // half

    row = jnp.arange(half * row_count, dtype=jnp.int32)
    member, inner = row // row_count, row % row_count
    t = inner // 2
    frequency = jnp.where(
        upper == 0, kx_local * member + t, kx_local * (half - 1 - member) + kx_local - t
    )
    positions = space_index * slab_rows + jnp.arange(slab_rows, dtype=jnp.int32)
    phases = frequency[:, None] * positions[None, :] % grid_rows
    angles = phases.astype(f32) * (2.0 * math.pi / grid_rows)
    x_table = jnp.where((inner % 2 == 0)[:, None], jnp.cos(angles), jnp.sin(angles)).astype(bf16)

    blocks = 2 * space_count
    size = 2 * ky_local
    row = jnp.arange(blocks * size, dtype=jnp.int32)
    block, inner = row // size, row % size
    shift = block % space_count
    sign = jnp.where((block // space_count) == upper, 1.0, -1.0).astype(f32)
    ky_index = (space_index + shift) % space_count * ky_local + inner // 2
    imaginary = inner % 2 == 1
    positions = upper * half_cols + jnp.arange(half_cols, dtype=jnp.int32)
    phases = ky_index[:, None] * positions[None, :] % grid_cols
    angles = phases.astype(f32) * (2.0 * math.pi / grid_cols)
    cosine = jnp.cos(angles)
    minus_sine = -jnp.sin(angles)
    left = jnp.where(imaginary[:, None], minus_sine, cosine)
    right = sign[:, None] * jnp.where(imaginary[:, None], -cosine, minus_sine)
    y_table = jnp.concatenate([left, right], axis=1).astype(bf16)

    ky_row = space_index * ky_local + jnp.arange(size, dtype=jnp.int32) // 2
    scale = jnp.where(ky_row == 0, 1.0, 2.0).astype(f32) / (grid_rows * grid_cols)
    scale_rows = jnp.broadcast_to(scale[:, None], (size, channels))

    halves = [list(range(half)), list(range(half, data_count))]

    def exchange(values):
        return lax.all_to_all(
            values, "dp", split_axis=0, concat_axis=0, tiled=True, axis_index_groups=halves
        )

    def pairs(mirror, shift):
        moves = []
        for d in range(data_count):
            for s in range(space_count):
                target = data_count - 1 - d if mirror else d
                moves.append(
                    (d * space_count + s, target * space_count + (s + shift) % space_count)
                )
        return moves

    order = [(mirror, shift) for mirror in (1, 0) for shift in reversed(range(space_count))][:-1]

    def gathered(parts):
        held = [parts[0]]
        for mirror, shift in order:
            held.append(
                lax.ppermute(
                    parts[mirror * space_count + shift], ("dp", "space"), pairs(mirror, shift)
                )
            )
        return held

    def spectrum_parts(x_sums):
        lines = exchange(x_sums.reshape(half, row_count, col_block, channels))
        return gathered(y_transform_call(y_table, lines, blocks, size))

    delta, delta_sums = delta_call(x_table, pre_act[0], cotangent[0])
    delta_parts = spectrum_parts(delta_sums)
    back, delta_owned = back_call(scale_rows, spec_weight, delta_parts)
    received = {(0, 0): back}
    for mirror, shift in order:
        received[(mirror, -shift % space_count)] = lax.ppermute(
            back, ("dp", "space"), pairs(mirror, shift)
        )
    modes = [received[(mirror, shift)] for mirror in (0, 1) for shift in range(space_count)]
    columns = exchange(y_inverse_call(y_table, modes, half, col_block))
    grad_input = final_call(
        x_table, columns.reshape(half * row_count, col_block, channels), delta, local_weight
    )

    input_sums, local_term, bias_term = input_call(x_table, field_in[0], delta)
    input_parts = spectrum_parts(input_sums)
    grad_spectral = outer_call(scale_rows, delta_owned, input_parts)

    device_count = data_count * space_count
    bias_row = jnp.sum(bias_term, axis=0, keepdims=True)
    share = -(-(channels + 1) // device_count)
    filler = jnp.zeros((share * device_count - channels - 1, channels), f32)
    stacked = jnp.concatenate([local_term, bias_row, filler], axis=0)
    shares = lax.all_to_all(
        stacked.reshape(device_count, share, channels), ("dp", "space"), 0, 0, tiled=True
    )
    total = jnp.sum(shares, axis=0)
    spread = jnp.broadcast_to(total[None], (device_count, share, channels))
    totals = lax.all_to_all(spread, ("dp", "space"), 0, 0, tiled=True)
    totals = totals.reshape(device_count * share, channels)
    return (grad_input[None], grad_spectral, totals[:channels], totals[channels])


def solution(mesh):
    placed = (
        P(None, "space", "dp", None),
        P(None, "space", "dp", None),
        P(None, "space", "dp", None),
        P("dp", "space", None, None, None),
        P(),
    )
    return jax.shard_map(
        on_device,
        mesh=mesh,
        in_specs=placed,
        out_specs=(P(None, "space", "dp", None), P("dp", "space", None, None, None), P(), P()),
        check_vma=False,
    )
```

```python
import functools
import math

import jax
import jax.numpy as jnp
from jax import lax
from jax.experimental import pallas as pl
from jax.experimental.pallas import tpu as pltpu
from jax.sharding import PartitionSpec as P

root_two_pi = 0.7978845608028654
cubic_coef = 0.044715
f32 = jnp.float32
bf16 = jnp.bfloat16
mebi = 1024 * 1024


def gelu_slope(values):
    square = values * values
    cubic = root_two_pi * cubic_coef
    tangent = jnp.tanh(values * (root_two_pi + cubic * square))
    inner = values * (1.0 - tangent * tangent)
    return 0.5 * ((1.0 + tangent) + inner * (root_two_pi + (3.0 * cubic) * square))


def cosine_table(phases, period):
    quarter = period // 4
    if period & (period - 1) == 0:
        turns = (phases + quarter // 2) >> (quarter.bit_length() - 1)
    else:
        turns = (phases + quarter // 2) // quarter
    angle = (phases - turns * quarter).astype(f32) * (2.0 * math.pi / period)
    square = angle * angle
    cosine = 1.0 + square * (
        -0.5 + square * (1.0 / 24.0 + square * (-1.0 / 720.0 + square * (1.0 / 40320.0)))
    )
    sine = angle * (
        1.0
        + square
        * (-1.0 / 6.0 + square * (1.0 / 120.0 + square * (-1.0 / 5040.0 + square * (1.0 / 362880.0))))
    )
    turns = turns & 3
    magnitude = jnp.where((turns & 1) == 0, cosine, sine)
    return jnp.where((turns == 1) | (turns == 2), -magnitude, magnitude).astype(bf16)


def params(mebibytes=16):
    return pltpu.CompilerParams(vmem_limit_bytes=mebibytes * mebi)


def whole(shape):
    return pl.BlockSpec(shape, lambda *_: (0,) * len(shape))


def matrix_per_column(table, columns_of):
    channels = columns_of[0].shape[1]
    results = []
    for y in range(0, len(columns_of), 2):
        pair = jnp.concatenate(columns_of[y : y + 2], axis=1)
        sums = jnp.dot(table, pair, preferred_element_type=f32).astype(bf16)
        results += [sums[:, :channels], sums[:, channels:]]
    return jnp.swapaxes(jnp.stack(results, axis=0), 0, 1)


def two_terms(values):
    high = values.astype(bf16)
    return high, (values - high.astype(f32)).astype(bf16)


def extra_rows(channels, half):
    return -(-(2 * (channels // half) + 2) // 8) * 8


def pack_share(share, bias):
    rows, channels = share.shape
    filler = extra_rows(channels, channels // rows) - 2 * rows - 2
    parts = list(two_terms(share) + two_terms(bias))
    if filler:
        parts.append(jnp.zeros((filler, channels), bf16))
    return jnp.concatenate([part.astype(f32) for part in parts], axis=0).astype(bf16)


def unpack_share(rows, message):
    message = message.astype(f32)
    share = message[:rows] + message[rows : 2 * rows]
    bias = message[2 * rows : 2 * rows + 1] + message[2 * rows + 1 : 2 * rows + 2]
    return share, bias


def delta_kernel(
    table_ref, upper_ref, pre_ref, cot_ref, field_ref, delta_ref, out_ref, lines, local, bias
):
    grid_rows, columns, channels = pre_ref.shape
    half = out_ref.shape[0]
    block = pl.program_id(0)
    all_columns = columns * pl.num_programs(0)
    step = 16

    @pl.when(block == 0)
    def _():
        local[...] = jnp.zeros_like(local)
        bias[...] = jnp.zeros_like(bias)

    def slab(i, carry):
        rows = pl.ds(pl.multiple_of(i * step, step), step)
        slope = gelu_slope(pre_ref[rows].astype(f32))
        delta = (cot_ref[rows].astype(f32) * slope).astype(bf16)
        delta_ref[rows] = delta
        lines[:, rows, :] = jnp.swapaxes(delta, 0, 1)
        bias[...] += jnp.sum(delta.astype(f32).reshape(-1, 8, channels), axis=0)
        return carry

    lax.fori_loop(0, grid_rows // step, slab, 0, unroll=2)
    local[...] += lax.dot_general(
        field_ref[...].reshape(grid_rows * columns, channels),
        delta_ref[...].reshape(grid_rows * columns, channels),
        (((0,), (0,)), ((), ())),
        preferred_element_type=f32,
    )
    sums = matrix_per_column(table_ref[...], [lines[y] for y in range(columns)])
    per_target = sums.shape[0] // half
    first = pl.multiple_of(block * columns, columns)
    for target in range(half):
        for row in range(per_target):
            out_ref[target, pl.ds(row * all_columns + first, columns), :] = sums[
                target * per_target + row
            ]

    @pl.when(block == pl.num_programs(0) - 1)
    def _():
        upper = upper_ref[:1] > 0.0
        share = channels // half
        total = jnp.sum(bias[...], axis=0, keepdims=True)
        for target in range(half):
            mine = local[target * share : (target + 1) * share]
            mirrored = local[(half - 1 - target) * share : (half - target) * share]
            rows = pack_share(jnp.where(upper, mirrored, mine), total)
            out_ref[target, per_target * all_columns :] = rows


def delta_call(table, upper, pre_act, cotangent, field_in, half):
    grid_rows, columns, channels = pre_act.shape
    rows = table.shape[0]
    block = min(16, columns)
    field = pl.BlockSpec((grid_rows, block, channels), lambda i: (0, i, 0))
    message = (half, rows // half * columns + extra_rows(channels, half), channels)
    return pl.pallas_call(
        delta_kernel,
        grid=(columns // block,),
        in_specs=[whole(table.shape), whole(upper.shape), field, field, field],
        out_specs=[field, whole(message)],
        out_shape=[
            jax.ShapeDtypeStruct(pre_act.shape, bf16),
            jax.ShapeDtypeStruct(message, bf16),
        ],
        scratch_shapes=[
            pltpu.VMEM((block, grid_rows, channels), bf16),
            pltpu.VMEM((channels, channels), f32),
            pltpu.VMEM((8, channels), f32),
        ],
        compiler_params=params(60),
        cost_estimate=pl.CostEstimate(
            flops=4 * rows * pre_act.size, bytes_accessed=8 * pre_act.size, transcendentals=pre_act.size
        ),
        name="delta_and_x_sums",
    )(table, upper, pre_act, cotangent, field_in)


def input_kernel(table_ref, field_ref, out_ref):
    lines = jnp.swapaxes(field_ref[...], 0, 1)
    out_ref[...] = matrix_per_column(
        table_ref[...], [lines[y] for y in range(field_ref.shape[1])]
    )


def input_call(table, field_in):
    grid_rows, columns, channels = field_in.shape
    rows = table.shape[0]
    block = min(16, columns)
    return pl.pallas_call(
        input_kernel,
        grid=(columns // block,),
        in_specs=[
            whole(table.shape),
            pl.BlockSpec((grid_rows, block, channels), lambda i: (0, i, 0)),
        ],
        out_specs=pl.BlockSpec((rows, block, channels), lambda i: (0, i, 0)),
        out_shape=jax.ShapeDtypeStruct((rows, columns, channels), bf16),
        compiler_params=params(60),
        cost_estimate=pl.CostEstimate(
            flops=2 * rows * field_in.size, bytes_accessed=4 * field_in.size, transcendentals=0
        ),
        name="input_x_sums",
    )(table, field_in)


def y_transform_kernel(columns, extra, blocks, table_ref, lines_ref, *out_refs):
    sources, total_rows, channels = lines_ref.shape
    frequencies = (total_rows - extra) // columns // 2
    own = blocks // 2
    size = table_ref.shape[0] // blocks
    table = table_ref[...]
    for t in range(frequencies):
        lines = jnp.concatenate(
            [
                lines_ref[:, row * columns : (row + 1) * columns].reshape(
                    sources * columns, channels
                )
                for row in (2 * t, 2 * t + 1)
            ],
            axis=0,
        )
        sums = jnp.dot(table, lines, preferred_element_type=f32).astype(bf16)
        for block in range(blocks):
            held = t if block < own else frequencies - 1 - t
            if 0 <= held < frequencies - 1:
                first = (block // len(out_refs)) * (frequencies - 1) + held
                out_refs[block % len(out_refs)][first * size : (first + 1) * size] = sums[
                    block * size : (block + 1) * size
                ]
    if extra:
        rows = channels // sources
        pieces = [unpack_share(rows, lines_ref[i, total_rows - extra :]) for i in range(sources)]
        packed = pack_share(sum(p[0] for p in pieces), sum(p[1] for p in pieces))
        for out_ref in out_refs:
            out_ref[(frequencies - 1) * size :] = packed


def y_transform_call(table, lines, blocks, outputs, columns, extra):
    sources, total_rows, channels = lines.shape
    held = (total_rows - extra) // columns // 2 - 1
    size = table.shape[0] // blocks
    return pl.pallas_call(
        functools.partial(y_transform_kernel, columns, extra, blocks),
        out_shape=[
            jax.ShapeDtypeStruct((blocks // outputs * held * size + extra, channels), bf16)
        ]
        * outputs,
        compiler_params=params(),
        cost_estimate=pl.CostEstimate(
            flops=2 * (held + 1) * table.size * channels, bytes_accessed=4 * lines.size, transcendentals=0
        ),
        name="y_sums",
    )(table, lines)


def turned(values):
    rows = values.shape[0]
    even = lax.broadcasted_iota(jnp.int32, values.shape, 0) % 2 == 0
    up = pltpu.roll(values, rows - 1, 0)
    down = pltpu.roll(values, 1, 0)
    return jnp.concatenate([values, jnp.where(even, up, -down)], axis=1)


def load_kernel(source_ref, target_ref, semaphores):
    copies = [
        pltpu.make_async_copy(source_ref.at[j, k], target_ref.at[j, k], semaphores.at[j, k])
        for j in range(source_ref.shape[0])
        for k in range(source_ref.shape[1])
    ]
    for copy in copies:
        copy.start()
    for copy in copies:
        copy.wait()


def load_call(weight):
    held, modes, _, channels, _ = weight.shape
    parts = weight.reshape(held, 2, modes // 2, 2, channels, channels)
    loaded = pl.pallas_call(
        load_kernel,
        in_specs=[pl.BlockSpec(memory_space=pl.ANY)],
        out_specs=pl.BlockSpec(memory_space=pl.ANY),
        out_shape=pltpu.VMEM(parts.shape, bf16),
        scratch_shapes=[pltpu.SemaphoreType.DMA((held, 2))],
        compiler_params=params(50),
        cost_estimate=pl.CostEstimate(flops=0, bytes_accessed=4 * weight.size, transcendentals=0),
        name="weights_to_vmem",
    )(parts)
    return loaded.reshape(weight.shape)


def back_kernel(share, scale_ref, weight_ref, *refs):
    part_refs, (back_ref, delta_ref, share_ref) = refs[:-3], refs[-3:]
    held, rows, channels = delta_ref.shape
    block = weight_ref.shape[1]
    j, k = pl.program_id(0), pl.program_id(1)
    first = pl.multiple_of((j * (rows // (2 * block)) + k) * 2 * block, 2 * block)
    here = pl.ds(first, 2 * block)
    inner = pl.ds(pl.multiple_of(k * 2 * block, 2 * block), 2 * block)
    total = part_refs[0][here].astype(f32)
    for ref in part_refs[1:]:
        total = total + ref[here].astype(f32)
    delta = total.astype(bf16)
    delta_ref[j, inner] = delta
    both = turned(delta.astype(f32)).astype(bf16)
    sums = []
    for mode in range(block):
        weight = jnp.concatenate([weight_ref[0, mode, 0], weight_ref[0, mode, 1]], axis=1)
        sums.append(
            lax.dot_general(
                both[2 * mode : 2 * mode + 2],
                weight,
                (((1,), (1,)), ((), ())),
                preferred_element_type=f32,
            )
        )
    back_ref[j, inner] = (jnp.concatenate(sums, axis=0) * scale_ref[inner]).astype(bf16)

    @pl.when((j == 0) & (k == 0))
    def _():
        pieces = [unpack_share(share, ref[held * rows :]) for ref in part_refs]
        share_ref[...] = pack_share(sum(p[0] for p in pieces), sum(p[1] for p in pieces))


def back_call(scale_rows, weight, parts, share):
    held, modes, _, channels, _ = weight.shape
    block = min(16, modes)
    shape = (held, 2 * modes, channels)
    extra = (parts[0].shape[0] - held * 2 * modes, channels)
    return pl.pallas_call(
        functools.partial(back_kernel, share),
        grid=(held, modes // block),
        in_specs=[
            whole(scale_rows.shape),
            pl.BlockSpec((1, block, 2, channels, channels), lambda j, k: (j, k, 0, 0, 0)),
        ]
        + [whole(part.shape) for part in parts],
        out_specs=[whole(shape), whole(shape), whole(extra)],
        out_shape=[
            jax.ShapeDtypeStruct(shape, bf16),
            jax.ShapeDtypeStruct(shape, bf16),
            jax.ShapeDtypeStruct(extra, bf16),
        ],
        compiler_params=params(),
        cost_estimate=pl.CostEstimate(
            flops=4 * weight.size, bytes_accessed=2 * weight.size, transcendentals=0
        ),
        name="mode_back",
    )(scale_rows, weight, *parts)


def outer_kernel(scale_ref, delta_ref, *refs):
    part_refs, out_ref = refs[:-1], refs[-1]
    modes = out_ref.shape[1]
    channels = out_ref.shape[-1]
    total = part_refs[0][...].astype(f32)
    for ref in part_refs[1:]:
        total = total + ref[...].astype(f32)
    field = (total.astype(bf16).astype(f32) * scale_ref[...]).astype(bf16).astype(f32)
    delta = turned(delta_ref[0].astype(f32))
    group = 4
    mode_of_row = lax.broadcasted_iota(jnp.int32, (2 * group, 2 * channels), 0) // 2
    for first in range(0, modes, group):
        rows = slice(2 * first, 2 * (first + group))
        alone = [jnp.where(mode_of_row == i, delta[rows], 0.0) for i in range(group)]
        product = lax.dot_general(
            field[rows].astype(bf16),
            jnp.concatenate(alone, axis=1).astype(bf16),
            (((0,), (0,)), ((), ())),
            preferred_element_type=f32,
        ).astype(bf16)
        for i in range(2 * group):
            out_ref[0, first + i // 2, i % 2] = product[:, i * channels : (i + 1) * channels]


def outer_call(scale_rows, delta, parts):
    held, rows, channels = delta.shape
    modes = rows // 2
    part = pl.BlockSpec((1, rows, channels), lambda j: (j, 0, 0))
    return pl.pallas_call(
        outer_kernel,
        grid=(held,),
        in_specs=[whole((rows, channels)), part]
        + [pl.BlockSpec((rows, channels), lambda j: (j, 0))] * len(parts),
        out_specs=pl.BlockSpec((1, modes, 2, channels, channels), lambda j: (j, 0, 0, 0, 0)),
        out_shape=jax.ShapeDtypeStruct((held, modes, 2, channels, channels), bf16),
        compiler_params=params(),
        cost_estimate=pl.CostEstimate(
            flops=6 * held * modes * channels * channels,
            bytes_accessed=4 * held * modes * channels * channels,
            transcendentals=0,
        ),
        name="grad_spectral",
    )(scale_rows, delta, *parts)


def y_inverse_kernel(columns, table_ref, share_ref, *refs):
    part_refs, out_ref = refs[:-1], refs[-1]
    targets, total_rows, channels = out_ref.shape
    extra = share_ref.shape[0]
    frequencies = (total_rows - extra) // columns // 2
    own = len(part_refs) // 2
    size = part_refs[0].shape[1]
    table = table_ref[...]
    for t in range(frequencies):
        first = 0 if t < frequencies - 1 else own
        last = 2 * own if t > 0 else own
        modes = jnp.concatenate(
            [
                part_refs[block][t if block < own else frequencies - 1 - t]
                for block in range(first, last)
            ],
            axis=0,
        )
        sums = lax.dot_general(
            table[first * size : last * size],
            modes,
            (((0,), (0,)), ((), ())),
            preferred_element_type=f32,
        ).astype(bf16)
        for part in range(2):
            row = 2 * t + part
            out_ref[:, row * columns : (row + 1) * columns] = sums[
                part * targets * columns : (part + 1) * targets * columns
            ].reshape(targets, columns, channels)
    for target in range(targets):
        out_ref[target, total_rows - extra :] = share_ref[...]


def y_inverse_call(table, share, parts, targets, columns):
    held, size, channels = parts[0].shape
    rows = 2 * (held + 1)
    return pl.pallas_call(
        functools.partial(y_inverse_kernel, columns),
        out_shape=jax.ShapeDtypeStruct(
            (targets, rows * columns + share.shape[0], channels), bf16
        ),
        compiler_params=params(),
        cost_estimate=pl.CostEstimate(
            flops=rows * table.size * channels,
            bytes_accessed=4 * targets * rows * columns * channels,
            transcendentals=0,
        ),
        name="y_inverse",
    )(table, share, *parts)


def final_kernel(
    table_ref, upper_ref, lines_ref, delta_ref, weight_ref, out_ref, local_ref, bias_ref
):
    grid_rows, columns, channels = out_ref.shape
    half = lines_ref.shape[0]
    block = pl.program_id(0)
    all_columns = columns * pl.num_programs(0)
    per_source = table_ref.shape[0] // half
    first = pl.multiple_of(block * columns, columns)
    lines = jnp.stack(
        [
            lines_ref[source, pl.ds(row * all_columns + first, columns), :]
            for source in range(half)
            for row in range(per_source)
        ],
        axis=0,
    )
    lines = jnp.swapaxes(lines, 0, 1)
    spectral = matrix_per_column(table_ref[...].T, [lines[y] for y in range(columns)])
    local = lax.dot_general(
        delta_ref[...].reshape(grid_rows * columns, channels),
        weight_ref[...],
        (((1,), (1,)), ((), ())),
        preferred_element_type=f32,
    ).reshape(grid_rows, columns, channels)
    out_ref[...] = (spectral.astype(f32) + local).astype(bf16)

    @pl.when(block == 0)
    def _():
        upper = upper_ref[:1] > 0.0
        share = channels // half
        pieces = [
            unpack_share(share, lines_ref[source, per_source * all_columns :])
            for source in range(half)
        ]
        for source in range(half):
            local_ref[source * share : (source + 1) * share] = jnp.where(
                upper, pieces[half - 1 - source][0], pieces[source][0]
            )
        bias_ref[...] = pieces[0][1]


def final_call(table, upper, lines, delta, local_weight):
    grid_rows, columns, channels = delta.shape
    block = min(16, columns)
    field = pl.BlockSpec((grid_rows, block, channels), lambda i: (0, i, 0))
    return pl.pallas_call(
        final_kernel,
        grid=(columns // block,),
        in_specs=[
            whole(table.shape),
            whole(upper.shape),
            whole(lines.shape),
            field,
            whole(local_weight.shape),
        ],
        out_specs=[field, whole((channels, channels)), whole((1, channels))],
        out_shape=[
            jax.ShapeDtypeStruct(delta.shape, bf16),
            jax.ShapeDtypeStruct((channels, channels), f32),
            jax.ShapeDtypeStruct((1, channels), f32),
        ],
        compiler_params=params(),
        cost_estimate=pl.CostEstimate(
            flops=2 * (table.shape[0] + channels) * delta.size,
            bytes_accessed=5 * delta.size,
            transcendentals=0,
        ),
        name="x_inverse_and_local",
    )(table, upper, lines, delta, local_weight)


def on_device(field_in, pre_act, cotangent, spec_weight, local_weight):
    batch_size, slab_rows, col_block, channels = field_in.shape
    space_count = lax.axis_size("space")
    data_count = lax.axis_size("dp")
    grid_rows = slab_rows * space_count
    grid_cols = col_block * data_count
    kx_local, ky_local = spec_weight.shape[:2]
    half = data_count // 2
    half_cols = half * col_block
    row_count = 2 * (kx_local + 1)
    data_index = lax.axis_index("dp")
    space_index = lax.axis_index("space")
    upper = data_index // half

    row = jnp.arange(half * row_count, dtype=jnp.int32)
    member, inner = row // row_count, row % row_count
    t = inner // 2
    frequency = jnp.where(
        upper == 0, kx_local * member + t, kx_local * (half - 1 - member) + kx_local - t
    )
    positions = space_index * slab_rows + jnp.arange(slab_rows, dtype=jnp.int32)
    quarter = grid_rows // 4
    x_table = cosine_table(
        frequency[:, None] * positions[None, :] - (inner % 2 * quarter)[:, None], grid_rows
    )

    blocks = 2 * space_count
    size = 2 * ky_local
    row = jnp.arange(blocks * size, dtype=jnp.int32)
    block, inner = row // size, row % size
    shift = block % space_count
    ky_index = (space_index + shift) % space_count * ky_local + inner // 2
    positions = upper * half_cols + jnp.arange(half_cols, dtype=jnp.int32)
    quarter = grid_cols // 4
    cosine_turn = inner % 2
    sine_turn = jnp.where((block // space_count) == upper, 1 + inner % 2, 3 * (1 - inner % 2))
    turn = jnp.concatenate(
        [
            jnp.broadcast_to(cosine_turn[:, None], (blocks * size, half_cols)),
            jnp.broadcast_to(sine_turn[:, None], (blocks * size, half_cols)),
        ],
        axis=1,
    )
    positions = jnp.concatenate([positions, positions])
    y_table = cosine_table(ky_index[:, None] * positions[None, :] + quarter * turn, grid_cols)

    ky_row = space_index * ky_local + jnp.arange(size, dtype=jnp.int32) // 2
    scale = jnp.where(ky_row == 0, 1.0, 2.0).astype(f32) / (grid_rows * grid_cols)
    scale_rows = jnp.broadcast_to(scale[:, None], (size, channels))

    halves = [list(range(half)), list(range(half, data_count))]

    def exchange(values):
        return lax.all_to_all(
            values, "dp", split_axis=0, concat_axis=0, tiled=True, axis_index_groups=halves
        )

    def pairs(mirror, shift):
        moves = []
        for d in range(data_count):
            for s in range(space_count):
                target = data_count - 1 - d if mirror else d
                moves.append(
                    (d * space_count + s, target * space_count + (s + shift) % space_count)
                )
        return moves

    order = [(mirror, shift) for mirror in (1, 0) for shift in reversed(range(space_count))][:-1]

    def gathered(parts):
        held = [parts[0]]
        for mirror, shift in order:
            held.append(
                lax.ppermute(
                    parts[mirror * space_count + shift], ("dp", "space"), pairs(mirror, shift)
                )
            )
        return held

    tied = lax.optimization_barrier

    share = channels // half
    extra = extra_rows(channels, half)
    flag = jnp.broadcast_to(upper.astype(f32), (8, channels))

    input_sums = input_call(x_table, field_in[0])
    input_lines = exchange(input_sums.reshape(half, row_count * col_block, channels))
    delta, delta_sums = delta_call(x_table, flag, pre_act[0], cotangent[0], field_in[0], half)
    delta_lines = exchange(delta_sums)
    input_parts = list(
        y_transform_call(y_table, input_lines, blocks, space_count, col_block, 0)
    )
    for shift in range(1, space_count):
        input_parts[shift] = lax.ppermute(input_parts[shift], ("dp", "space"), pairs(0, shift))
    held_rows = kx_local * size
    mirrored = sum(part[held_rows:].astype(f32) for part in input_parts).astype(bf16)
    delta_lines, mirrored = tied((delta_lines, mirrored))
    input_held = [part[:held_rows] for part in input_parts]
    input_held.append(lax.ppermute(mirrored, ("dp", "space"), pairs(1, 0)))

    delta_parts = y_transform_call(y_table, delta_lines, blocks, blocks, col_block, extra)
    weight, delta_parts = tied((spec_weight, delta_parts))
    weight = load_call(weight)
    delta_held, input_held[-1] = tied((gathered(delta_parts), input_held[-1]))
    back, delta_owned, share_rows = back_call(scale_rows, weight, delta_held, share)
    received = {(0, 0): back}
    for mirror, shift in order:
        received[(mirror, -shift % space_count)] = lax.ppermute(
            back, ("dp", "space"), pairs(mirror, shift)
        )
    modes = [received[(mirror, shift)] for mirror in (0, 1) for shift in range(space_count)]
    column_sums = y_inverse_call(y_table, share_rows, modes, half, col_block)
    column_sums, delta_owned = tied((column_sums, delta_owned))
    columns = exchange(column_sums)
    grad_spectral = outer_call(scale_rows, delta_owned, input_held)
    columns, grad_spectral = tied((columns, grad_spectral))
    grad_input, grad_local, bias_rows = final_call(x_table, flag, columns, delta, local_weight)
    return (grad_input[None], grad_spectral, grad_local, bias_rows.reshape(channels))


def solution(mesh):
    placed = (
        P(None, "space", "dp", None),
        P(None, "space", "dp", None),
        P(None, "space", "dp", None),
        P("dp", "space", None, None, None),
        P(),
    )
    return jax.shard_map(
        on_device,
        mesh=mesh,
        in_specs=placed,
        out_specs=(P(None, "space", "dp", None), P("dp", "space", None, None, None), P(), P()),
        check_vma=False,
    )
```

```python
import functools
import math

import jax
import jax.numpy as jnp
from jax import lax
from jax.experimental import pallas as pl
from jax.experimental.pallas import tpu as pltpu
from jax.sharding import PartitionSpec as P

root_two_pi = 0.7978845608028654
cubic_coef = 0.044715
f32 = jnp.float32
bf16 = jnp.bfloat16
mebi = 1024 * 1024


def gelu_slope(values):
    square = values * values
    cubic = root_two_pi * cubic_coef
    tangent = jnp.tanh(values * (root_two_pi + cubic * square))
    inner = values * (1.0 - tangent * tangent)
    return 0.5 * ((1.0 + tangent) + inner * (root_two_pi + (3.0 * cubic) * square))


def cosine_table(phases, period):
    quarter = period // 4
    if period & (period - 1) == 0:
        turns = (phases + quarter // 2) >> (quarter.bit_length() - 1)
    else:
        turns = (phases + quarter // 2) // quarter
    angle = (phases - turns * quarter).astype(f32) * (2.0 * math.pi / period)
    square = angle * angle
    cosine = 1.0 + square * (
        -0.5 + square * (1.0 / 24.0 + square * (-1.0 / 720.0 + square * (1.0 / 40320.0)))
    )
    sine = angle * (
        1.0
        + square
        * (-1.0 / 6.0 + square * (1.0 / 120.0 + square * (-1.0 / 5040.0 + square * (1.0 / 362880.0))))
    )
    turns = turns & 3
    magnitude = jnp.where((turns & 1) == 0, cosine, sine)
    return jnp.where((turns == 1) | (turns == 2), -magnitude, magnitude).astype(bf16)


def x_table(sizes, transposed=False):
    half, kx_local, slab_rows, grid_rows = sizes
    row_count = 2 * (kx_local + 1)
    upper = (lax.axis_index("dp") >= half).astype(jnp.int32)
    shape = (half * row_count, slab_rows)
    if transposed:
        shape = shape[::-1]
    row = lax.broadcasted_iota(jnp.int32, shape, 1 if transposed else 0)
    position = lax.axis_index("space") * slab_rows + lax.broadcasted_iota(
        jnp.int32, shape, 0 if transposed else 1
    )
    member = sum((row >= i * row_count).astype(jnp.int32) for i in range(1, half))
    inner = row - member * row_count
    ascending = member * kx_local + (inner >> 1)
    frequency = ascending + upper * (half * kx_local - 2 * ascending)
    quarter = grid_rows // 4
    return cosine_table(frequency * position - (inner & 1) * quarter, grid_rows)


def params(mebibytes=16):
    return pltpu.CompilerParams(vmem_limit_bytes=mebibytes * mebi)


def whole(shape):
    return pl.BlockSpec(shape, lambda *_: (0,) * len(shape))


def matrix_per_column(table, columns_of):
    channels = columns_of[0].shape[1]
    results = []
    for y in range(0, len(columns_of), 2):
        pair = jnp.concatenate(columns_of[y : y + 2], axis=1)
        sums = jnp.dot(table, pair, preferred_element_type=f32).astype(bf16)
        results += [sums[:, :channels], sums[:, channels:]]
    return jnp.swapaxes(jnp.stack(results, axis=0), 0, 1)


def two_terms(values):
    high = values.astype(bf16)
    return high, (values - high.astype(f32)).astype(bf16)


def extra_rows(channels, half):
    return -(-(2 * (channels // half) + 2) // 8) * 8


def pack_share(share, bias):
    rows, channels = share.shape
    filler = extra_rows(channels, channels // rows) - 2 * rows - 2
    parts = list(two_terms(share) + two_terms(bias))
    if filler:
        parts.append(jnp.zeros((filler, channels), bf16))
    return jnp.concatenate([part.astype(f32) for part in parts], axis=0).astype(bf16)


def unpack_share(rows, message):
    message = message.astype(f32)
    share = message[:rows] + message[rows : 2 * rows]
    bias = message[2 * rows : 2 * rows + 1] + message[2 * rows + 1 : 2 * rows + 2]
    return share, bias


def delta_kernel(
    sizes, pre_ref, cot_ref, field_ref, delta_ref, out_ref, lines, local, bias, table
):
    grid_rows, columns, channels = pre_ref.shape
    half = out_ref.shape[0]
    block = pl.program_id(0)
    all_columns = columns * pl.num_programs(0)
    step = 16

    @pl.when(block == 0)
    def _():
        local[...] = jnp.zeros_like(local)
        bias[...] = jnp.zeros_like(bias)
        table[...] = x_table(sizes)

    def slab(i, carry):
        rows = pl.ds(pl.multiple_of(i * step, step), step)
        slope = gelu_slope(pre_ref[rows].astype(f32))
        delta = (cot_ref[rows].astype(f32) * slope).astype(bf16)
        delta_ref[rows] = delta
        lines[:, rows, :] = jnp.swapaxes(delta, 0, 1)
        bias[...] += jnp.sum(delta.astype(f32).reshape(-1, 8, channels), axis=0)
        return carry

    lax.fori_loop(0, grid_rows // step, slab, 0, unroll=2)
    local[...] += lax.dot_general(
        field_ref[...].reshape(grid_rows * columns, channels),
        delta_ref[...].reshape(grid_rows * columns, channels),
        (((0,), (0,)), ((), ())),
        preferred_element_type=f32,
    )
    sums = matrix_per_column(table[...], [lines[y] for y in range(columns)])
    per_target = sums.shape[0] // half
    first = pl.multiple_of(block * columns, columns)
    for target in range(half):
        for row in range(per_target):
            out_ref[target, pl.ds(row * all_columns + first, columns), :] = sums[
                target * per_target + row
            ]

    @pl.when(block == pl.num_programs(0) - 1)
    def _():
        upper = lax.axis_index("dp") >= half
        share = channels // half
        total = jnp.sum(bias[...], axis=0, keepdims=True)
        for target in range(half):
            mine = local[target * share : (target + 1) * share]
            mirrored = local[(half - 1 - target) * share : (half - target) * share]
            rows = pack_share(jnp.where(upper, mirrored, mine), total)
            out_ref[target, per_target * all_columns :] = rows


def delta_call(sizes, pre_act, cotangent, field_in):
    grid_rows, columns, channels = pre_act.shape
    half = sizes[0]
    rows = 2 * half * (sizes[1] + 1)
    block = min(16, columns)
    field = pl.BlockSpec((grid_rows, block, channels), lambda i: (0, i, 0))
    message = (half, rows // half * columns + extra_rows(channels, half), channels)
    return pl.pallas_call(
        functools.partial(delta_kernel, sizes),
        grid=(columns // block,),
        in_specs=[field, field, field],
        out_specs=[field, whole(message)],
        out_shape=[
            jax.ShapeDtypeStruct(pre_act.shape, bf16),
            jax.ShapeDtypeStruct(message, bf16),
        ],
        scratch_shapes=[
            pltpu.VMEM((block, grid_rows, channels), bf16),
            pltpu.VMEM((channels, channels), f32),
            pltpu.VMEM((8, channels), f32),
            pltpu.VMEM((rows, grid_rows), bf16),
        ],
        compiler_params=params(60),
        cost_estimate=pl.CostEstimate(
            flops=4 * rows * pre_act.size, bytes_accessed=8 * pre_act.size, transcendentals=pre_act.size
        ),
        name="delta_and_x_sums",
    )(pre_act, cotangent, field_in)


def input_kernel(sizes, *refs):
    field_refs, (out_ref, table) = refs[:-2], refs[-2:]

    @pl.when(pl.program_id(0) == 0)
    def _():
        table[...] = x_table(sizes)

    lines = [jnp.swapaxes(ref[...], 0, 1) for ref in field_refs]
    out_ref[...] = matrix_per_column(
        table[...],
        [jnp.concatenate([part[y] for part in lines], axis=0) for y in range(out_ref.shape[1])],
    )


def input_call(sizes, field_in):
    grid_rows, columns, channels = field_in.shape
    rows = 2 * sizes[0] * (sizes[1] + 1)
    block = min(16, columns)
    pieces = 4
    return pl.pallas_call(
        functools.partial(input_kernel, sizes),
        grid=(columns // block,),
        in_specs=[
            pl.BlockSpec(
                (grid_rows // pieces, block, channels), lambda i, piece=piece: (piece, i, 0)
            )
            for piece in range(pieces)
        ],
        out_specs=pl.BlockSpec((rows, block, channels), lambda i: (0, i, 0)),
        out_shape=jax.ShapeDtypeStruct((rows, columns, channels), bf16),
        scratch_shapes=[pltpu.VMEM((rows, grid_rows), bf16)],
        compiler_params=params(60),
        cost_estimate=pl.CostEstimate(
            flops=2 * rows * field_in.size, bytes_accessed=4 * field_in.size, transcendentals=0
        ),
        name="input_x_sums",
    )(*[field_in] * pieces)


def y_transform_kernel(columns, extra, blocks, tails, table_ref, lines_ref, *refs):
    tail_refs, out_refs = refs[:tails], refs[tails:]
    sources, total_rows, channels = lines_ref.shape
    frequencies = (total_rows - extra) // columns // 2
    own = blocks // 2
    size = table_ref.shape[0] // blocks
    table = table_ref[...]
    for t in range(frequencies):
        lines = jnp.concatenate(
            [
                lines_ref[:, row * columns : (row + 1) * columns].reshape(
                    sources * columns, channels
                )
                for row in (2 * t, 2 * t + 1)
            ],
            axis=0,
        )
        sums = jnp.dot(table, lines, preferred_element_type=f32).astype(bf16)
        for block in range(blocks):
            held = t if block < own else frequencies - 1 - t
            if 0 <= held < frequencies - 1:
                first = (block // len(out_refs)) * (frequencies - 1) + held
                out_refs[block % len(out_refs)][first * size : (first + 1) * size] = sums[
                    block * size : (block + 1) * size
                ]
    if extra:
        rows = channels // sources
        pieces = [unpack_share(rows, lines_ref[i, total_rows - extra :]) for i in range(sources)]
        packed = pack_share(sum(p[0] for p in pieces), sum(p[1] for p in pieces))
        for out_ref in out_refs:
            out_ref[out_ref.shape[0] - extra :] = packed
    for tail_ref in tail_refs:
        rows = tail_ref.shape[0]
        out_refs[own][rows : 2 * rows] = tail_ref[...]


def y_transform_call(table, lines, blocks, outputs, columns, extra, tails=()):
    sources, total_rows, channels = lines.shape
    held = (total_rows - extra) // columns // 2 - 1
    size = table.shape[0] // blocks
    out_rows = [blocks // outputs * held * size + extra] * outputs
    for tail in tails:
        out_rows[blocks // 2] += tail.shape[0]
    return pl.pallas_call(
        functools.partial(y_transform_kernel, columns, extra, blocks, len(tails)),
        out_shape=[jax.ShapeDtypeStruct((rows, channels), bf16) for rows in out_rows],
        compiler_params=params(),
        cost_estimate=pl.CostEstimate(
            flops=2 * (held + 1) * table.size * channels, bytes_accessed=4 * lines.size, transcendentals=0
        ),
        name="y_sums",
    )(table, lines, *tails)


def turned(values):
    rows = values.shape[0]
    even = lax.broadcasted_iota(jnp.int32, values.shape, 0) % 2 == 0
    up = pltpu.roll(values, rows - 1, 0)
    down = pltpu.roll(values, 1, 0)
    return jnp.concatenate([values, jnp.where(even, up, -down)], axis=1)


def load_kernel(source_ref, target_ref, semaphores):
    copies = [
        pltpu.make_async_copy(source_ref.at[j, k], target_ref.at[j, k], semaphores.at[j, k])
        for j in range(source_ref.shape[0])
        for k in range(source_ref.shape[1])
    ]
    for copy in copies:
        copy.start()
    for copy in copies:
        copy.wait()


def load_call(weight):
    held, modes, _, channels, _ = weight.shape
    parts = weight.reshape(held, 2, modes // 2, 2, channels, channels)
    loaded = pl.pallas_call(
        load_kernel,
        in_specs=[pl.BlockSpec(memory_space=pl.ANY)],
        out_specs=pl.BlockSpec(memory_space=pl.ANY),
        out_shape=pltpu.VMEM(parts.shape, bf16),
        scratch_shapes=[pltpu.SemaphoreType.DMA((held, 2))],
        compiler_params=params(50),
        cost_estimate=pl.CostEstimate(flops=0, bytes_accessed=4 * weight.size, transcendentals=0),
        name="weights_to_vmem",
    )(parts)
    return loaded.reshape(weight.shape)


def back_kernel(share, scale_ref, weight_ref, *refs):
    part_refs, (back_ref, delta_ref, share_ref) = refs[:-3], refs[-3:]
    held, rows, channels = delta_ref.shape
    block = weight_ref.shape[1]
    j, k = pl.program_id(0), pl.program_id(1)
    first = pl.multiple_of((j * (rows // (2 * block)) + k) * 2 * block, 2 * block)
    here = pl.ds(first, 2 * block)
    inner = pl.ds(pl.multiple_of(k * 2 * block, 2 * block), 2 * block)
    total = part_refs[0][here].astype(f32)
    for ref in part_refs[1:]:
        total = total + ref[here].astype(f32)
    delta = total.astype(bf16)
    delta_ref[j, inner] = delta
    both = turned(delta.astype(f32)).astype(bf16)
    sums = []
    for mode in range(block):
        weight = jnp.concatenate([weight_ref[0, mode, 0], weight_ref[0, mode, 1]], axis=1)
        sums.append(
            lax.dot_general(
                both[2 * mode : 2 * mode + 2],
                weight,
                (((1,), (1,)), ((), ())),
                preferred_element_type=f32,
            )
        )
    back_ref[j, inner] = (jnp.concatenate(sums, axis=0) * scale_ref[inner]).astype(bf16)

    @pl.when((j == 0) & (k == 0))
    def _():
        extra = share_ref.shape[0]
        pieces = [unpack_share(share, ref[ref.shape[0] - extra :]) for ref in part_refs]
        share_ref[...] = pack_share(sum(p[0] for p in pieces), sum(p[1] for p in pieces))


def back_call(scale_rows, weight, parts, share):
    held, modes, _, channels, _ = weight.shape
    block = min(16, modes)
    shape = (held, 2 * modes, channels)
    extra = (parts[0].shape[0] - held * 2 * modes, channels)
    return pl.pallas_call(
        functools.partial(back_kernel, share),
        grid=(held, modes // block),
        in_specs=[
            whole(scale_rows.shape),
            pl.BlockSpec((1, block, 2, channels, channels), lambda j, k: (j, k, 0, 0, 0)),
        ]
        + [whole(part.shape) for part in parts],
        out_specs=[whole(shape), whole(shape), whole(extra)],
        out_shape=[
            jax.ShapeDtypeStruct(shape, bf16),
            jax.ShapeDtypeStruct(shape, bf16),
            jax.ShapeDtypeStruct(extra, bf16),
        ],
        compiler_params=params(),
        cost_estimate=pl.CostEstimate(
            flops=4 * weight.size, bytes_accessed=2 * weight.size, transcendentals=0
        ),
        name="mode_back",
    )(scale_rows, weight, *parts)


def outer_kernel(scale_ref, delta_ref, *refs):
    part_refs, out_ref = refs[:-1], refs[-1]
    modes = out_ref.shape[1]
    channels = out_ref.shape[-1]
    total = part_refs[0][...].astype(f32)
    for ref in part_refs[1:]:
        total = total + ref[...].astype(f32)
    field = (total.astype(bf16).astype(f32) * scale_ref[...]).astype(bf16).astype(f32)
    delta = turned(delta_ref[0].astype(f32))
    group = 4
    mode_of_row = lax.broadcasted_iota(jnp.int32, (2 * group, 2 * channels), 0) // 2
    for first in range(0, modes, group):
        rows = slice(2 * first, 2 * (first + group))
        alone = [jnp.where(mode_of_row == i, delta[rows], 0.0) for i in range(group)]
        product = lax.dot_general(
            field[rows].astype(bf16),
            jnp.concatenate(alone, axis=1).astype(bf16),
            (((0,), (0,)), ((), ())),
            preferred_element_type=f32,
        ).astype(bf16)
        for i in range(2 * group):
            out_ref[0, first + i // 2, i % 2] = product[:, i * channels : (i + 1) * channels]


def outer_call(scale_rows, delta, parts):
    held, rows, channels = delta.shape
    modes = rows // 2
    part = pl.BlockSpec((1, rows, channels), lambda j: (j, 0, 0))
    return pl.pallas_call(
        outer_kernel,
        grid=(held,),
        in_specs=[whole((rows, channels)), part]
        + [
            pl.BlockSpec((rows, channels), lambda j, first=first: (j + first, 0))
            for _, first in parts
        ],
        out_specs=pl.BlockSpec((1, modes, 2, channels, channels), lambda j: (j, 0, 0, 0, 0)),
        out_shape=jax.ShapeDtypeStruct((held, modes, 2, channels, channels), bf16),
        compiler_params=params(),
        cost_estimate=pl.CostEstimate(
            flops=6 * held * modes * channels * channels,
            bytes_accessed=4 * held * modes * channels * channels,
            transcendentals=0,
        ),
        name="grad_spectral",
    )(scale_rows, delta, *[part for part, _ in parts])


def y_inverse_kernel(columns, table_ref, share_ref, *refs):
    part_refs, out_ref = refs[:-1], refs[-1]
    targets, total_rows, channels = out_ref.shape
    extra = share_ref.shape[0]
    frequencies = (total_rows - extra) // columns // 2
    own = len(part_refs) // 2
    size = part_refs[0].shape[1]
    table = table_ref[...]
    for t in range(frequencies):
        first = 0 if t < frequencies - 1 else own
        last = 2 * own if t > 0 else own
        modes = jnp.concatenate(
            [
                part_refs[block][t if block < own else frequencies - 1 - t]
                for block in range(first, last)
            ],
            axis=0,
        )
        sums = lax.dot_general(
            table[first * size : last * size],
            modes,
            (((0,), (0,)), ((), ())),
            preferred_element_type=f32,
        ).astype(bf16)
        for part in range(2):
            row = 2 * t + part
            out_ref[:, row * columns : (row + 1) * columns] = sums[
                part * targets * columns : (part + 1) * targets * columns
            ].reshape(targets, columns, channels)
    for target in range(targets):
        out_ref[target, total_rows - extra :] = share_ref[...]


def y_inverse_call(table, share, parts, targets, columns):
    held, size, channels = parts[0].shape
    rows = 2 * (held + 1)
    return pl.pallas_call(
        functools.partial(y_inverse_kernel, columns),
        out_shape=jax.ShapeDtypeStruct(
            (targets, rows * columns + share.shape[0], channels), bf16
        ),
        compiler_params=params(),
        cost_estimate=pl.CostEstimate(
            flops=rows * table.size * channels,
            bytes_accessed=4 * targets * rows * columns * channels,
            transcendentals=0,
        ),
        name="y_inverse",
    )(table, share, *parts)


def final_kernel(
    sizes, lines_ref, delta_ref, weight_ref, out_ref, local_ref, bias_ref, table
):
    grid_rows, columns, channels = out_ref.shape
    half = lines_ref.shape[0]
    block = pl.program_id(0)
    all_columns = columns * pl.num_programs(0)
    per_source = table.shape[1] // half
    first = pl.multiple_of(block * columns, columns)

    @pl.when(block == 0)
    def _():
        table[...] = x_table(sizes, transposed=True)

    lines = jnp.stack(
        [
            lines_ref[source, pl.ds(row * all_columns + first, columns), :]
            for source in range(half)
            for row in range(per_source)
        ],
        axis=0,
    )
    lines = jnp.swapaxes(lines, 0, 1)
    spectral = matrix_per_column(table[...], [lines[y] for y in range(columns)])
    local = lax.dot_general(
        delta_ref[...].reshape(grid_rows * columns, channels),
        weight_ref[...],
        (((1,), (1,)), ((), ())),
        preferred_element_type=f32,
    ).reshape(grid_rows, columns, channels)
    out_ref[...] = (spectral.astype(f32) + local).astype(bf16)

    @pl.when(block == 0)
    def _():
        upper = lax.axis_index("dp") >= half
        share = channels // half
        pieces = [
            unpack_share(share, lines_ref[source, per_source * all_columns :])
            for source in range(half)
        ]
        for source in range(half):
            local_ref[source * share : (source + 1) * share] = jnp.where(
                upper, pieces[half - 1 - source][0], pieces[source][0]
            )
        bias_ref[...] = pieces[0][1]


def final_call(sizes, lines, delta, local_weight):
    grid_rows, columns, channels = delta.shape
    rows = 2 * sizes[0] * (sizes[1] + 1)
    block = min(16, columns)
    field = pl.BlockSpec((grid_rows, block, channels), lambda i: (0, i, 0))
    return pl.pallas_call(
        functools.partial(final_kernel, sizes),
        grid=(columns // block,),
        in_specs=[
            whole(lines.shape),
            field,
            whole(local_weight.shape),
        ],
        out_specs=[field, whole((channels, channels)), whole((1, channels))],
        out_shape=[
            jax.ShapeDtypeStruct(delta.shape, bf16),
            jax.ShapeDtypeStruct((channels, channels), f32),
            jax.ShapeDtypeStruct((1, channels), f32),
        ],
        scratch_shapes=[pltpu.VMEM((grid_rows, rows), bf16)],
        compiler_params=params(),
        cost_estimate=pl.CostEstimate(
            flops=2 * (rows + channels) * delta.size,
            bytes_accessed=5 * delta.size,
            transcendentals=0,
        ),
        name="x_inverse_and_local",
    )(lines, delta, local_weight)


def on_device(field_in, pre_act, cotangent, spec_weight, local_weight):
    batch_size, slab_rows, col_block, channels = field_in.shape
    space_count = lax.axis_size("space")
    data_count = lax.axis_size("dp")
    grid_rows = slab_rows * space_count
    grid_cols = col_block * data_count
    kx_local, ky_local = spec_weight.shape[:2]
    half = data_count // 2
    half_cols = half * col_block
    row_count = 2 * (kx_local + 1)
    data_index = lax.axis_index("dp")
    space_index = lax.axis_index("space")
    upper = data_index // half

    sizes = (half, kx_local, slab_rows, grid_rows)

    blocks = 2 * space_count
    size = 2 * ky_local
    row = jnp.arange(blocks * size, dtype=jnp.int32)
    block, inner = row // size, row % size
    shift = block % space_count
    ky_index = (space_index + shift) % space_count * ky_local + inner // 2
    positions = upper * half_cols + jnp.arange(half_cols, dtype=jnp.int32)
    quarter = grid_cols // 4
    cosine_turn = inner % 2
    sine_turn = jnp.where((block // space_count) == upper, 1 + inner % 2, 3 * (1 - inner % 2))
    turn = jnp.concatenate(
        [
            jnp.broadcast_to(cosine_turn[:, None], (blocks * size, half_cols)),
            jnp.broadcast_to(sine_turn[:, None], (blocks * size, half_cols)),
        ],
        axis=1,
    )
    positions = jnp.concatenate([positions, positions])
    y_table = cosine_table(ky_index[:, None] * positions[None, :] + quarter * turn, grid_cols)

    ky_row = space_index * ky_local + jnp.arange(size, dtype=jnp.int32) // 2
    scale = jnp.where(ky_row == 0, 1.0, 2.0).astype(f32) / (grid_rows * grid_cols)
    scale_rows = jnp.broadcast_to(scale[:, None], (size, channels))

    halves = [list(range(half)), list(range(half, data_count))]

    def exchange(values):
        return lax.all_to_all(
            values, "dp", split_axis=0, concat_axis=0, tiled=True, axis_index_groups=halves
        )

    def pairs(mirror, shift):
        moves = []
        for d in range(data_count):
            for s in range(space_count):
                target = data_count - 1 - d if mirror else d
                moves.append(
                    (d * space_count + s, target * space_count + (s + shift) % space_count)
                )
        return moves

    order = [(mirror, shift) for mirror in (1, 0) for shift in reversed(range(space_count))][:-1]

    def gathered(parts):
        held = [parts[0]]
        for mirror, shift in order:
            held.append(
                lax.ppermute(
                    parts[mirror * space_count + shift], ("dp", "space"), pairs(mirror, shift)
                )
            )
        return held

    tied = lax.optimization_barrier

    share = channels // half
    extra = extra_rows(channels, half)

    input_sums = input_call(sizes, field_in[0])
    input_lines = exchange(input_sums.reshape(half, row_count * col_block, channels))
    delta, delta_sums = delta_call(sizes, pre_act[0], cotangent[0], field_in[0])
    delta_lines = exchange(delta_sums)
    input_parts = list(
        y_transform_call(y_table, input_lines, blocks, space_count, col_block, 0)
    )
    for shift in range(1, space_count):
        input_parts[shift] = lax.ppermute(input_parts[shift], ("dp", "space"), pairs(0, shift))
    held_rows = kx_local * size
    mirrored = sum(part[held_rows:].astype(f32) for part in input_parts).astype(bf16)
    delta_lines, mirrored = tied((delta_lines, mirrored))

    delta_parts = y_transform_call(
        y_table, delta_lines, blocks, blocks, col_block, extra, (mirrored,)
    )
    weight, delta_parts = tied((spec_weight, delta_parts))
    weight = load_call(weight)
    delta_held = gathered(delta_parts)
    input_held = [(part, 0) for part in input_parts]
    input_held.append((delta_held[1 + order.index((1, 0))], kx_local))
    back, delta_owned, share_rows = back_call(scale_rows, weight, delta_held, share)
    received = {(0, 0): back}
    for mirror, shift in order:
        received[(mirror, -shift % space_count)] = lax.ppermute(
            back, ("dp", "space"), pairs(mirror, shift)
        )
    modes = [received[(mirror, shift)] for mirror in (0, 1) for shift in range(space_count)]
    column_sums = y_inverse_call(y_table, share_rows, modes, half, col_block)
    column_sums, delta_owned = tied((column_sums, delta_owned))
    columns = exchange(column_sums)
    grad_spectral = outer_call(scale_rows, delta_owned, input_held)
    columns, grad_spectral = tied((columns, grad_spectral))
    grad_input, grad_local, bias_rows = final_call(sizes, columns, delta, local_weight)
    return (grad_input[None], grad_spectral, grad_local, bias_rows.reshape(channels))


def solution(mesh):
    placed = (
        P(None, "space", "dp", None),
        P(None, "space", "dp", None),
        P(None, "space", "dp", None),
        P("dp", "space", None, None, None),
        P(),
    )
    return jax.shard_map(
        on_device,
        mesh=mesh,
        in_specs=placed,
        out_specs=(P(None, "space", "dp", None), P("dp", "space", None, None, None), P(), P()),
        check_vma=False,
    )
```

```python
import functools
import math

import jax
import jax.numpy as jnp
from jax import lax
from jax.experimental import pallas as pl
from jax.experimental.pallas import tpu as pltpu
from jax.sharding import PartitionSpec as P

root_two_pi = 0.7978845608028654
cubic_coef = 0.044715
f32 = jnp.float32
bf16 = jnp.bfloat16
mebi = 1024 * 1024


def gelu_slope(values):
    square = values * values
    cubic = root_two_pi * cubic_coef
    tangent = jnp.tanh(values * (root_two_pi + cubic * square))
    inner = values * (1.0 - tangent * tangent)
    return 0.5 * ((1.0 + tangent) + inner * (root_two_pi + (3.0 * cubic) * square))


def cosine_table(phases, period):
    quarter = period // 4
    if period & (period - 1) == 0:
        turns = (phases + quarter // 2) >> (quarter.bit_length() - 1)
    else:
        turns = (phases + quarter // 2) // quarter
    angle = (phases - turns * quarter).astype(f32) * (2.0 * math.pi / period)
    square = angle * angle
    cosine = 1.0 + square * (
        -0.5 + square * (1.0 / 24.0 + square * (-1.0 / 720.0 + square * (1.0 / 40320.0)))
    )
    sine = angle * (
        1.0
        + square
        * (-1.0 / 6.0 + square * (1.0 / 120.0 + square * (-1.0 / 5040.0 + square * (1.0 / 362880.0))))
    )
    turns = turns & 3
    magnitude = jnp.where((turns & 1) == 0, cosine, sine)
    return jnp.where((turns == 1) | (turns == 2), -magnitude, magnitude).astype(bf16)


def x_table(sizes, transposed=False, relative=False):
    half, kx_local, slab_rows, grid_rows = sizes
    row_count = 2 * (kx_local + 1)
    upper = (lax.axis_index("dp") >= half).astype(jnp.int32)
    shape = (half * row_count, slab_rows)
    if transposed:
        shape = shape[::-1]
    row = lax.broadcasted_iota(jnp.int32, shape, 1 if transposed else 0)
    position = lax.axis_index("space") * slab_rows + lax.broadcasted_iota(
        jnp.int32, shape, 0 if transposed else 1
    )
    member = sum((row >= i * row_count).astype(jnp.int32) for i in range(1, half))
    inner = row - member * row_count
    if relative:
        member = member ^ (lax.axis_index("dp") & (half - 1))
    ascending = member * kx_local + (inner >> 1)
    frequency = ascending + upper * (half * kx_local - 2 * ascending)
    quarter = grid_rows // 4
    return cosine_table(frequency * position - (inner & 1) * quarter, grid_rows)


def params(mebibytes=16):
    return pltpu.CompilerParams(vmem_limit_bytes=mebibytes * mebi)


def whole(shape):
    return pl.BlockSpec(shape, lambda *_: (0,) * len(shape))


def matrix_per_column(table, columns_of, rows=()):
    channels = columns_of[0].shape[1]
    results = []
    totals = [0.0] * len(rows)
    for y in range(0, len(columns_of), 2):
        pair = jnp.concatenate(columns_of[y : y + 2], axis=1)
        sums = jnp.dot(table, pair, preferred_element_type=f32)
        totals = [total + sums[row : row + 1] for total, row in zip(totals, rows)]
        sums = sums.astype(bf16)
        results += [sums[:, :channels], sums[:, channels:]]
    results = jnp.swapaxes(jnp.stack(results, axis=0), 0, 1)
    if rows:
        return results, [total[:, :channels] + total[:, channels:] for total in totals]
    return results


def two_terms(values):
    high = values.astype(bf16)
    return high, (values - high.astype(f32)).astype(bf16)


def extra_rows(channels, half):
    return -(-(2 * (channels // half) + 2) // 8) * 8


def pack_share(share, bias):
    rows, channels = share.shape
    filler = extra_rows(channels, channels // rows) - 2 * rows - 2
    parts = list(two_terms(share) + two_terms(bias))
    if filler:
        parts.append(jnp.zeros((filler, channels), bf16))
    return jnp.concatenate([part.astype(f32) for part in parts], axis=0).astype(bf16)


def unpack_share(rows, message):
    message = message.astype(f32)
    share = message[:rows] + message[rows : 2 * rows]
    bias = message[2 * rows : 2 * rows + 1] + message[2 * rows + 1 : 2 * rows + 2]
    return share, bias


def delta_kernel(
    sizes,
    pre_ref,
    cot_ref,
    field_ref,
    delta_ref,
    out_ref,
    lines,
    local,
    bias,
    table,
    field,
    semaphores,
):
    grid_rows, columns, channels = pre_ref.shape
    half = out_ref.shape[0]
    block = pl.program_id(0)
    all_columns = columns * pl.num_programs(0)
    step = 16
    blocks = field.shape[0]

    def arriving(i):
        return pltpu.make_async_copy(
            field_ref.at[:, pl.ds(i * columns, columns)], field.at[i], semaphores.at[i]
        )

    @pl.when(block == 0)
    def _():
        for i in range(blocks):
            arriving(i).start()
        local[...] = jnp.zeros_like(local)
        bias[...] = jnp.zeros_like(bias)
        table[...] = x_table(sizes)

    def slab(i, carry):
        rows = pl.ds(pl.multiple_of(i * step, step), step)
        slope = gelu_slope(pre_ref[rows].astype(f32))
        delta = (cot_ref[rows].astype(f32) * slope).astype(bf16)
        delta_ref[rows] = delta
        lines[:, rows, :] = jnp.swapaxes(delta, 0, 1)
        return carry

    lax.fori_loop(0, grid_rows // step, slab, 0, unroll=2)
    sums, totals = matrix_per_column(
        table[...], [lines[y] for y in range(columns)], (0, table.shape[0] - 2)
    )
    upper = lax.axis_index("dp") >= half
    bias[...] += jnp.where(upper, totals[1], totals[0])
    for i in range(blocks):

        @pl.when(block == i)
        def _(i=i):
            arriving(i).wait()

    local[...] += lax.dot_general(
        field[block].reshape(grid_rows * columns, channels),
        delta_ref[...].reshape(grid_rows * columns, channels),
        (((0,), (0,)), ((), ())),
        preferred_element_type=f32,
    )
    per_target = sums.shape[0] // half
    first = pl.multiple_of(block * columns, columns)
    for target in range(half):
        for row in range(per_target):
            out_ref[target, pl.ds(row * all_columns + first, columns), :] = sums[
                target * per_target + row
            ]

    @pl.when(block == pl.num_programs(0) - 1)
    def _():
        share = channels // half
        total = bias[...]
        for target in range(half):
            mine = local[target * share : (target + 1) * share]
            mirrored = local[(half - 1 - target) * share : (half - target) * share]
            rows = pack_share(jnp.where(upper, mirrored, mine), total)
            out_ref[target, per_target * all_columns :] = rows


def delta_call(sizes, pre_act, cotangent, field_in):
    grid_rows, columns, channels = pre_act.shape
    half = sizes[0]
    rows = 2 * half * (sizes[1] + 1)
    block = min(16, columns)
    field = pl.BlockSpec((grid_rows, block, channels), lambda i: (0, i, 0))
    message = (half, rows // half * columns + extra_rows(channels, half), channels)
    return pl.pallas_call(
        functools.partial(delta_kernel, sizes),
        grid=(columns // block,),
        in_specs=[field, field, pl.BlockSpec(memory_space=pl.ANY)],
        out_specs=[field, whole(message)],
        out_shape=[
            jax.ShapeDtypeStruct(pre_act.shape, bf16),
            jax.ShapeDtypeStruct(message, bf16),
        ],
        scratch_shapes=[
            pltpu.VMEM((block, grid_rows, channels), bf16),
            pltpu.VMEM((channels, channels), f32),
            pltpu.VMEM((1, channels), f32),
            pltpu.VMEM((rows, grid_rows), bf16),
            pltpu.VMEM((columns // block, grid_rows, block, channels), bf16),
            pltpu.SemaphoreType.DMA((columns // block,)),
        ],
        compiler_params=params(60),
        cost_estimate=pl.CostEstimate(
            flops=4 * rows * pre_act.size, bytes_accessed=8 * pre_act.size, transcendentals=pre_act.size
        ),
        name="delta_and_x_sums",
    )(pre_act, cotangent, field_in)


def input_kernel(sizes, pieces, *refs):
    field_refs, out_refs, table = refs[:pieces], refs[pieces:-1], refs[-1]
    columns, channels = field_refs[0].shape[1:]
    block = pl.program_id(0)
    all_columns = columns * pl.num_programs(0)

    @pl.when(block == 0)
    def _():
        table[...] = x_table(sizes, relative=True)

    lines = [jnp.swapaxes(ref[...], 0, 1) for ref in field_refs]
    sums = matrix_per_column(
        table[...],
        [jnp.concatenate([part[y] for part in lines], axis=0) for y in range(columns)],
    )
    first = pl.multiple_of(block * columns, columns)
    rows = sums.shape[0] // len(out_refs)
    for pair, out_ref in enumerate(out_refs):
        for row in range(rows):
            out_ref[pl.ds(row * all_columns + first, columns), :] = sums[pair * rows + row]


def input_call(sizes, field_in):
    grid_rows, columns, channels = field_in.shape
    half = sizes[0]
    rows = 2 * half * (sizes[1] + 1)
    block = min(16, columns)
    pieces = 4
    message = (2 * rows // half * columns, channels)
    return pl.pallas_call(
        functools.partial(input_kernel, sizes, pieces),
        grid=(columns // block,),
        in_specs=[
            pl.BlockSpec(
                (grid_rows // pieces, block, channels), lambda i, piece=piece: (piece, i, 0)
            )
            for piece in range(pieces)
        ],
        out_specs=[whole(message)] * (half // 2),
        out_shape=[jax.ShapeDtypeStruct(message, bf16)] * (half // 2),
        scratch_shapes=[pltpu.VMEM((rows, grid_rows), bf16)],
        compiler_params=params(60),
        cost_estimate=pl.CostEstimate(
            flops=2 * rows * field_in.size, bytes_accessed=4 * field_in.size, transcendentals=0
        ),
        name="input_x_sums",
    )(*[field_in] * pieces)


def y_transform_kernel(columns, extra, blocks, total_rows, places, arrays, table_ref, *refs):
    line_refs, out_refs = refs[:arrays], refs[arrays:]
    sources, channels = len(places), line_refs[0].shape[-1]

    def rows_of(source, first, last):
        array, at = places[source]
        return line_refs[array][at + first : at + last]

    frequencies = (total_rows - extra) // columns // 2
    own = blocks // 2
    size = table_ref.shape[0] // blocks
    table = table_ref[...]
    for t in range(frequencies):
        lines = jnp.concatenate(
            [
                rows_of(source, row * columns, (row + 1) * columns)
                for row in (2 * t, 2 * t + 1)
                for source in range(sources)
            ],
            axis=0,
        )
        sums = jnp.dot(table, lines, preferred_element_type=f32).astype(bf16)
        for block in range(blocks):
            held = t if block < own else frequencies - 1 - t
            if 0 <= held < frequencies - 1:
                first = (block // len(out_refs)) * (frequencies - 1) + held
                out_refs[block % len(out_refs)][first * size : (first + 1) * size] = sums[
                    block * size : (block + 1) * size
                ]
    if extra:
        rows = channels // sources
        pieces = [
            unpack_share(rows, rows_of(i, total_rows - extra, total_rows)) for i in range(sources)
        ]
        packed = pack_share(sum(p[0] for p in pieces), sum(p[1] for p in pieces))
        for out_ref in out_refs:
            out_ref[out_ref.shape[0] - extra :] = packed


def y_transform_call(table, lines, places, total_rows, blocks, outputs, columns, extra):
    channels = lines[0].shape[-1]
    held = (total_rows - extra) // columns // 2 - 1
    size = table.shape[0] // blocks
    rows = blocks // outputs * held * size + extra
    return pl.pallas_call(
        functools.partial(
            y_transform_kernel, columns, extra, blocks, total_rows, places, len(lines)
        ),
        out_shape=[jax.ShapeDtypeStruct((rows, channels), bf16)] * outputs,
        compiler_params=params(),
        cost_estimate=pl.CostEstimate(
            flops=2 * (held + 1) * table.size * channels,
            bytes_accessed=4 * len(places) * total_rows * channels,
            transcendentals=0,
        ),
        name="y_sums",
    )(table, *lines)


def turned(values):
    rows = values.shape[0]
    even = lax.broadcasted_iota(jnp.int32, values.shape, 0) % 2 == 0
    up = pltpu.roll(values, rows - 1, 0)
    down = pltpu.roll(values, 1, 0)
    return jnp.concatenate([values, jnp.where(even, up, -down)], axis=1)


def load_kernel(source_ref, target_ref, semaphores):
    copies = [
        pltpu.make_async_copy(source_ref.at[j, k], target_ref.at[j, k], semaphores.at[j, k])
        for j in range(source_ref.shape[0])
        for k in range(source_ref.shape[1])
    ]
    for copy in copies:
        copy.start()
    for copy in copies:
        copy.wait()


def load_call(weight):
    held, modes, _, channels, _ = weight.shape
    parts = weight.reshape(held, 2, modes // 2, 2, channels, channels)
    loaded = pl.pallas_call(
        load_kernel,
        in_specs=[pl.BlockSpec(memory_space=pl.ANY)],
        out_specs=pl.BlockSpec(memory_space=pl.ANY),
        out_shape=pltpu.VMEM(parts.shape, bf16),
        scratch_shapes=[pltpu.SemaphoreType.DMA((held, 2))],
        compiler_params=params(50),
        cost_estimate=pl.CostEstimate(flops=0, bytes_accessed=4 * weight.size, transcendentals=0),
        name="weights_to_vmem",
    )(parts)
    return loaded.reshape(weight.shape)


def back_kernel(share, scale_ref, weight_ref, *refs):
    part_refs, (back_ref, delta_ref, share_ref) = refs[:-3], refs[-3:]
    held, rows, channels = delta_ref.shape
    block = weight_ref.shape[1]
    j, k = pl.program_id(0), pl.program_id(1)
    first = pl.multiple_of((j * (rows // (2 * block)) + k) * 2 * block, 2 * block)
    here = pl.ds(first, 2 * block)
    inner = pl.ds(pl.multiple_of(k * 2 * block, 2 * block), 2 * block)
    total = part_refs[0][here].astype(f32)
    for ref in part_refs[1:]:
        total = total + ref[here].astype(f32)
    delta = total.astype(bf16)
    delta_ref[j, inner] = delta
    both = turned(delta.astype(f32)).astype(bf16)
    sums = []
    for mode in range(block):
        weight = jnp.concatenate([weight_ref[0, mode, 0], weight_ref[0, mode, 1]], axis=1)
        sums.append(
            lax.dot_general(
                both[2 * mode : 2 * mode + 2],
                weight,
                (((1,), (1,)), ((), ())),
                preferred_element_type=f32,
            )
        )
    back_ref[j, inner] = (jnp.concatenate(sums, axis=0) * scale_ref[inner]).astype(bf16)

    @pl.when((j == 0) & (k == 0))
    def _():
        extra = share_ref.shape[0]
        pieces = [unpack_share(share, ref[ref.shape[0] - extra :]) for ref in part_refs]
        share_ref[...] = pack_share(sum(p[0] for p in pieces), sum(p[1] for p in pieces))


def back_call(scale_rows, weight, parts, share):
    held, modes, _, channels, _ = weight.shape
    block = min(16, modes)
    shape = (held, 2 * modes, channels)
    extra = (parts[0].shape[0] - held * 2 * modes, channels)
    return pl.pallas_call(
        functools.partial(back_kernel, share),
        grid=(held, modes // block),
        in_specs=[
            whole(scale_rows.shape),
            pl.BlockSpec((1, block, 2, channels, channels), lambda j, k: (j, k, 0, 0, 0)),
        ]
        + [whole(part.shape) for part in parts],
        out_specs=[whole(shape), whole(shape), whole(extra)],
        out_shape=[
            jax.ShapeDtypeStruct(shape, bf16),
            jax.ShapeDtypeStruct(shape, bf16),
            jax.ShapeDtypeStruct(extra, bf16),
        ],
        compiler_params=params(),
        cost_estimate=pl.CostEstimate(
            flops=4 * weight.size, bytes_accessed=2 * weight.size, transcendentals=0
        ),
        name="mode_back",
    )(scale_rows, weight, *parts)


def outer_kernel(scale_ref, delta_ref, *refs):
    part_refs, out_ref = refs[:-1], refs[-1]
    modes = out_ref.shape[1]
    channels = out_ref.shape[-1]
    total = part_refs[0][...].astype(f32)
    for ref in part_refs[1:]:
        total = total + ref[...].astype(f32)
    field = (total.astype(bf16).astype(f32) * scale_ref[...]).astype(bf16).astype(f32)
    delta = turned(delta_ref[0].astype(f32))
    group = 4
    mode_of_row = lax.broadcasted_iota(jnp.int32, (2 * group, 2 * channels), 0) // 2
    for first in range(0, modes, group):
        rows = slice(2 * first, 2 * (first + group))
        alone = [jnp.where(mode_of_row == i, delta[rows], 0.0) for i in range(group)]
        product = lax.dot_general(
            field[rows].astype(bf16),
            jnp.concatenate(alone, axis=1).astype(bf16),
            (((0,), (0,)), ((), ())),
            preferred_element_type=f32,
        ).astype(bf16)
        for i in range(2 * group):
            out_ref[0, first + i // 2, i % 2] = product[:, i * channels : (i + 1) * channels]


def outer_call(scale_rows, delta, parts):
    held, rows, channels = delta.shape
    modes = rows // 2
    part = pl.BlockSpec((1, rows, channels), lambda j: (j, 0, 0))
    return pl.pallas_call(
        outer_kernel,
        grid=(held,),
        in_specs=[whole((rows, channels)), part]
        + [
            pl.BlockSpec((rows, channels), lambda j, first=first: (j + first, 0))
            for _, first in parts
        ],
        out_specs=pl.BlockSpec((1, modes, 2, channels, channels), lambda j: (j, 0, 0, 0, 0)),
        out_shape=jax.ShapeDtypeStruct((held, modes, 2, channels, channels), bf16),
        compiler_params=params(),
        cost_estimate=pl.CostEstimate(
            flops=6 * held * modes * channels * channels,
            bytes_accessed=4 * held * modes * channels * channels,
            transcendentals=0,
        ),
        name="grad_spectral",
    )(scale_rows, delta, *[part for part, _ in parts])


def y_inverse_kernel(columns, table_ref, share_ref, *refs):
    part_refs, out_ref = refs[:-1], refs[-1]
    targets, total_rows, channels = out_ref.shape
    extra = share_ref.shape[0]
    frequencies = (total_rows - extra) // columns // 2
    own = len(part_refs) // 2
    size = part_refs[0].shape[1]
    table = table_ref[...]
    for t in range(frequencies):
        first = 0 if t < frequencies - 1 else own
        last = 2 * own if t > 0 else own
        modes = jnp.concatenate(
            [
                part_refs[block][t if block < own else frequencies - 1 - t]
                for block in range(first, last)
            ],
            axis=0,
        )
        sums = lax.dot_general(
            table[first * size : last * size],
            modes,
            (((0,), (0,)), ((), ())),
            preferred_element_type=f32,
        ).astype(bf16)
        for part in range(2):
            row = 2 * t + part
            out_ref[:, row * columns : (row + 1) * columns] = sums[
                part * targets * columns : (part + 1) * targets * columns
            ].reshape(targets, columns, channels)
    for target in range(targets):
        out_ref[target, total_rows - extra :] = share_ref[...]


def y_inverse_call(table, share, parts, targets, columns):
    held, size, channels = parts[0].shape
    rows = 2 * (held + 1)
    return pl.pallas_call(
        functools.partial(y_inverse_kernel, columns),
        out_shape=jax.ShapeDtypeStruct(
            (targets, rows * columns + share.shape[0], channels), bf16
        ),
        compiler_params=params(),
        cost_estimate=pl.CostEstimate(
            flops=rows * table.size * channels,
            bytes_accessed=4 * targets * rows * columns * channels,
            transcendentals=0,
        ),
        name="y_inverse",
    )(table, share, *parts)


def final_kernel(
    sizes, lines_ref, delta_ref, weight_ref, out_ref, local_ref, bias_ref, table
):
    grid_rows, columns, channels = out_ref.shape
    half = lines_ref.shape[0]
    block = pl.program_id(0)
    all_columns = columns * pl.num_programs(0)
    per_source = table.shape[1] // half
    first = pl.multiple_of(block * columns, columns)

    @pl.when(block == 0)
    def _():
        table[...] = x_table(sizes, transposed=True)

    lines = jnp.stack(
        [
            lines_ref[source, pl.ds(row * all_columns + first, columns), :]
            for source in range(half)
            for row in range(per_source)
        ],
        axis=0,
    )
    lines = jnp.swapaxes(lines, 0, 1)
    spectral = matrix_per_column(table[...], [lines[y] for y in range(columns)])
    local = lax.dot_general(
        delta_ref[...].reshape(grid_rows * columns, channels),
        weight_ref[...],
        (((1,), (1,)), ((), ())),
        preferred_element_type=f32,
    ).reshape(grid_rows, columns, channels)
    out_ref[...] = (spectral.astype(f32) + local).astype(bf16)

    @pl.when(block == 0)
    def _():
        upper = lax.axis_index("dp") >= half
        share = channels // half
        pieces = [
            unpack_share(share, lines_ref[source, per_source * all_columns :])
            for source in range(half)
        ]
        for source in range(half):
            local_ref[source * share : (source + 1) * share] = jnp.where(
                upper, pieces[half - 1 - source][0], pieces[source][0]
            )
        bias_ref[...] = pieces[0][1]


def final_call(sizes, lines, delta, local_weight):
    grid_rows, columns, channels = delta.shape
    rows = 2 * sizes[0] * (sizes[1] + 1)
    block = min(16, columns)
    field = pl.BlockSpec((grid_rows, block, channels), lambda i: (0, i, 0))
    return pl.pallas_call(
        functools.partial(final_kernel, sizes),
        grid=(columns // block,),
        in_specs=[
            whole(lines.shape),
            field,
            whole(local_weight.shape),
        ],
        out_specs=[field, whole((channels, channels)), whole((1, channels))],
        out_shape=[
            jax.ShapeDtypeStruct(delta.shape, bf16),
            jax.ShapeDtypeStruct((channels, channels), f32),
            jax.ShapeDtypeStruct((1, channels), f32),
        ],
        scratch_shapes=[pltpu.VMEM((grid_rows, rows), bf16)],
        compiler_params=params(),
        cost_estimate=pl.CostEstimate(
            flops=2 * (rows + channels) * delta.size,
            bytes_accessed=5 * delta.size,
            transcendentals=0,
        ),
        name="x_inverse_and_local",
    )(lines, delta, local_weight)


def on_device(field_in, pre_act, cotangent, spec_weight, local_weight):
    batch_size, slab_rows, col_block, channels = field_in.shape
    space_count = lax.axis_size("space")
    data_count = lax.axis_size("dp")
    grid_rows = slab_rows * space_count
    grid_cols = col_block * data_count
    kx_local, ky_local = spec_weight.shape[:2]
    half = data_count // 2
    half_cols = half * col_block
    row_count = 2 * (kx_local + 1)
    data_index = lax.axis_index("dp")
    space_index = lax.axis_index("space")
    upper = data_index // half

    sizes = (half, kx_local, slab_rows, grid_rows)

    blocks = 2 * space_count
    size = 2 * ky_local
    row = jnp.arange(blocks * size, dtype=jnp.int32)
    block, inner = row // size, row % size
    shift = block % space_count
    ky_index = (space_index + shift) % space_count * ky_local + inner // 2
    quarter = grid_cols // 4
    cosine_turn = inner % 2
    sine_turn = jnp.where((block // space_count) == upper, 1 + inner % 2, 3 * (1 - inner % 2))
    turn = jnp.concatenate(
        [
            jnp.broadcast_to(cosine_turn[:, None], (blocks * size, half_cols)),
            jnp.broadcast_to(sine_turn[:, None], (blocks * size, half_cols)),
        ],
        axis=1,
    )

    def y_basis(flip):
        column = jnp.arange(half_cols, dtype=jnp.int32)
        member = (column // col_block) ^ flip
        positions = upper * half_cols + member * col_block + column % col_block
        positions = jnp.concatenate([positions, positions])
        return cosine_table(ky_index[:, None] * positions[None, :] + quarter * turn, grid_cols)

    ky_row = space_index * ky_local + jnp.arange(size, dtype=jnp.int32) // 2
    scale = jnp.where(ky_row == 0, 1.0, 2.0).astype(f32) / (grid_rows * grid_cols)
    scale_rows = jnp.broadcast_to(scale[:, None], (size, channels))

    halves = [list(range(half)), list(range(half, data_count))]

    def exchange(values):
        return lax.all_to_all(
            values, "dp", split_axis=0, concat_axis=0, tiled=True, axis_index_groups=halves
        )

    def pairs(mirror, shift):
        moves = []
        for d in range(data_count):
            for s in range(space_count):
                target = data_count - 1 - d if mirror else d
                moves.append(
                    (d * space_count + s, target * space_count + (s + shift) % space_count)
                )
        return moves

    order = [(mirror, shift) for mirror in (1, 0) for shift in reversed(range(space_count))][:-1]

    def gathered(parts):
        held = [parts[0]]
        for mirror, shift in order:
            held.append(
                lax.ppermute(
                    parts[mirror * space_count + shift], ("dp", "space"), pairs(mirror, shift)
                )
            )
        return held

    tied = lax.optimization_barrier

    share = channels // half
    extra = extra_rows(channels, half)

    message = row_count * col_block
    y_table = y_basis(0)
    input_table = y_basis(data_index % half)

    chips = input_call(sizes, field_in[0])
    arrived = [chips[0]]
    for pair in range(1, half // 2):
        moves = [(d, d ^ (2 * pair)) for d in range(data_count)]
        arrived.append(lax.ppermute(chips[pair], "dp", moves))
    delta, delta_sums = delta_call(sizes, pre_act[0], cotangent[0], field_in[0])
    delta_sums, arrived = tied((delta_sums, arrived))
    delta_lines = exchange(delta_sums)
    mates = jnp.concatenate([part[message:] for part in arrived], axis=0)
    arrived.append(lax.ppermute(mates, "dp", [(d, d ^ 1) for d in range(data_count)]))
    places = [
        (source // 2, 0) if source % 2 == 0 else (half // 2, source // 2 * message)
        for source in range(half)
    ]
    input_parts = list(
        y_transform_call(input_table, arrived, places, message, blocks, space_count, col_block, 0)
    )
    for shift in range(1, space_count):
        input_parts[shift] = lax.ppermute(input_parts[shift], ("dp", "space"), pairs(0, shift))
    held_rows = kx_local * size
    mirrored = sum(part[held_rows:].astype(f32) for part in input_parts).astype(bf16)
    delta_lines, mirrored = tied((delta_lines, mirrored))

    message += extra
    delta_parts = y_transform_call(
        y_table,
        [delta_lines.reshape(half * message, channels)],
        [(0, source * message) for source in range(half)],
        message,
        blocks,
        blocks,
        col_block,
        extra,
    )
    weight, delta_parts = tied((spec_weight, delta_parts))
    weight = load_call(weight)
    delta_held = gathered(delta_parts)
    input_held = [(part, 0) for part in input_parts]
    back, delta_owned, share_rows = back_call(scale_rows, weight, delta_held, share)
    mirrored, back = tied((mirrored, back))
    received = {(0, 0): back}
    for mirror, shift in order:
        received[(mirror, -shift % space_count)] = lax.ppermute(
            back, ("dp", "space"), pairs(mirror, shift)
        )
    modes = [received[(mirror, shift)] for mirror in (0, 1) for shift in range(space_count)]
    column_sums = y_inverse_call(y_table, share_rows, modes, half, col_block)
    mirrored = lax.ppermute(mirrored, ("dp", "space"), pairs(1, 0))
    column_sums, delta_owned, mirrored = tied((column_sums, delta_owned, mirrored))
    input_held.append((mirrored, 0))
    columns = exchange(column_sums)
    grad_spectral = outer_call(scale_rows, delta_owned, input_held)
    columns, grad_spectral = tied((columns, grad_spectral))
    grad_input, grad_local, bias_rows = final_call(sizes, columns, delta, local_weight)
    return (grad_input[None], grad_spectral, grad_local, bias_rows.reshape(channels))


def solution(mesh):
    placed = (
        P(None, "space", "dp", None),
        P(None, "space", "dp", None),
        P(None, "space", "dp", None),
        P("dp", "space", None, None, None),
        P(),
    )
    return jax.shard_map(
        on_device,
        mesh=mesh,
        in_specs=placed,
        out_specs=(P(None, "space", "dp", None), P("dp", "space", None, None, None), P(), P()),
        check_vma=False,
    )
```

```python
import functools
import math

import jax
import jax.numpy as jnp
from jax import lax
from jax.experimental import pallas as pl
from jax.experimental.pallas import tpu as pltpu
from jax.sharding import PartitionSpec as P

root_two_pi = 0.7978845608028654
cubic_coef = 0.044715
f32 = jnp.float32
bf16 = jnp.bfloat16
mebi = 1024 * 1024


def gelu_slope(values):
    square = values * values
    cubic = root_two_pi * cubic_coef
    tangent = jnp.tanh(values * (root_two_pi + cubic * square))
    inner = values * (1.0 - tangent * tangent)
    return 0.5 * ((1.0 + tangent) + inner * (root_two_pi + (3.0 * cubic) * square))


def cosine_table(phases, period):
    quarter = period // 4
    if period & (period - 1) == 0:
        turns = (phases + quarter // 2) >> (quarter.bit_length() - 1)
    else:
        turns = (phases + quarter // 2) // quarter
    angle = (phases - turns * quarter).astype(f32) * (2.0 * math.pi / period)
    square = angle * angle
    cosine = 1.0 + square * (
        -0.5 + square * (1.0 / 24.0 + square * (-1.0 / 720.0 + square * (1.0 / 40320.0)))
    )
    sine = angle * (
        1.0
        + square
        * (-1.0 / 6.0 + square * (1.0 / 120.0 + square * (-1.0 / 5040.0 + square * (1.0 / 362880.0))))
    )
    turns = turns & 3
    magnitude = jnp.where((turns & 1) == 0, cosine, sine)
    return jnp.where((turns == 1) | (turns == 2), -magnitude, magnitude).astype(bf16)


def x_table(sizes, transposed=False, relative=False):
    half, kx_local, slab_rows, grid_rows = sizes
    row_count = 2 * (kx_local + 1)
    upper = (lax.axis_index("dp") >= half).astype(jnp.int32)
    shape = (half * row_count, slab_rows)
    if transposed:
        shape = shape[::-1]
    row = lax.broadcasted_iota(jnp.int32, shape, 1 if transposed else 0)
    position = lax.axis_index("space") * slab_rows + lax.broadcasted_iota(
        jnp.int32, shape, 0 if transposed else 1
    )
    member = sum((row >= i * row_count).astype(jnp.int32) for i in range(1, half))
    inner = row - member * row_count
    if relative:
        member = member ^ (lax.axis_index("dp") & (half - 1))
    ascending = member * kx_local + (inner >> 1)
    frequency = ascending + upper * (half * kx_local - 2 * ascending)
    quarter = grid_rows // 4
    return cosine_table(frequency * position - (inner & 1) * quarter, grid_rows)


def params(mebibytes=16):
    return pltpu.CompilerParams(vmem_limit_bytes=mebibytes * mebi)


def whole(shape):
    return pl.BlockSpec(shape, lambda *_: (0,) * len(shape))


def matrix_per_column(table, columns_of, rows=()):
    channels = columns_of[0].shape[1]
    results = []
    totals = [0.0] * len(rows)
    for y in range(0, len(columns_of), 2):
        pair = jnp.concatenate(columns_of[y : y + 2], axis=1)
        sums = jnp.dot(table, pair, preferred_element_type=f32)
        totals = [total + sums[row : row + 1] for total, row in zip(totals, rows)]
        sums = sums.astype(bf16)
        results += [sums[:, :channels], sums[:, channels:]]
    results = jnp.swapaxes(jnp.stack(results, axis=0), 0, 1)
    if rows:
        return results, [total[:, :channels] + total[:, channels:] for total in totals]
    return results


def two_terms(values):
    high = values.astype(bf16)
    return high, (values - high.astype(f32)).astype(bf16)


def extra_rows(channels, half):
    return -(-(2 * (channels // half) + 2) // 8) * 8


def pack_share(share, bias):
    rows, channels = share.shape
    filler = extra_rows(channels, channels // rows) - 2 * rows - 2
    parts = list(two_terms(share) + two_terms(bias))
    if filler:
        parts.append(jnp.zeros((filler, channels), bf16))
    return jnp.concatenate([part.astype(f32) for part in parts], axis=0).astype(bf16)


def unpack_share(rows, message):
    message = message.astype(f32)
    share = message[:rows] + message[rows : 2 * rows]
    bias = message[2 * rows : 2 * rows + 1] + message[2 * rows + 1 : 2 * rows + 2]
    return share, bias


def in_relative_order(pieces, half):
    place = lax.axis_index("dp")
    key = jnp.where(place >= half, 2 * half - 1 - place, place)
    step = 1
    while step < half:
        flag = (key & step) != 0
        pieces = [jnp.where(flag, pieces[i ^ step], pieces[i]) for i in range(half)]
        step *= 2
    return pieces


def delta_kernel(
    sizes,
    pre_ref,
    cot_ref,
    field_ref,
    delta_ref,
    out_ref,
    lines,
    local,
    bias,
    table,
    field,
    semaphores,
):
    grid_rows, columns, channels = pre_ref.shape
    half = out_ref.shape[0]
    block = pl.program_id(0)
    all_columns = columns * pl.num_programs(0)
    step = 16
    blocks = field.shape[0]

    def arriving(i):
        return pltpu.make_async_copy(
            field_ref.at[:, pl.ds(i * columns, columns)], field.at[i], semaphores.at[i]
        )

    @pl.when(block == 0)
    def _():
        for i in range(blocks):
            arriving(i).start()
        local[...] = jnp.zeros_like(local)
        bias[...] = jnp.zeros_like(bias)
        table[...] = x_table(sizes)

    def slab(i, carry):
        rows = pl.ds(pl.multiple_of(i * step, step), step)
        slope = gelu_slope(pre_ref[rows].astype(f32))
        delta = (cot_ref[rows].astype(f32) * slope).astype(bf16)
        delta_ref[rows] = delta
        lines[:, rows, :] = jnp.swapaxes(delta, 0, 1)
        return carry

    lax.fori_loop(0, grid_rows // step, slab, 0, unroll=2)
    sums, totals = matrix_per_column(
        table[...], [lines[y] for y in range(columns)], (0, table.shape[0] - 2)
    )
    upper = lax.axis_index("dp") >= half
    bias[...] += jnp.where(upper, totals[1], totals[0])
    for i in range(blocks):

        @pl.when(block == i)
        def _(i=i):
            arriving(i).wait()

    local[...] += lax.dot_general(
        field[block].reshape(grid_rows * columns, channels),
        delta_ref[...].reshape(grid_rows * columns, channels),
        (((0,), (0,)), ((), ())),
        preferred_element_type=f32,
    )
    per_target = sums.shape[0] // half
    first = pl.multiple_of(block * columns, columns)
    for target in range(half):
        for row in range(per_target):
            out_ref[target, pl.ds(row * all_columns + first, columns), :] = sums[
                target * per_target + row
            ]

    @pl.when(block == pl.num_programs(0) - 1)
    def _():
        share = channels // half
        total = bias[...]
        for target in range(half):
            mine = local[target * share : (target + 1) * share]
            mirrored = local[(half - 1 - target) * share : (half - target) * share]
            rows = pack_share(jnp.where(upper, mirrored, mine), total)
            out_ref[target, per_target * all_columns :] = rows


def delta_call(sizes, pre_act, cotangent, field_in):
    grid_rows, columns, channels = pre_act.shape
    half = sizes[0]
    rows = 2 * half * (sizes[1] + 1)
    block = min(16, columns)
    field = pl.BlockSpec((grid_rows, block, channels), lambda i: (0, i, 0))
    message = (half, rows // half * columns + extra_rows(channels, half), channels)
    return pl.pallas_call(
        functools.partial(delta_kernel, sizes),
        grid=(columns // block,),
        in_specs=[field, field, pl.BlockSpec(memory_space=pl.ANY)],
        out_specs=[field, whole(message)],
        out_shape=[
            jax.ShapeDtypeStruct(pre_act.shape, bf16),
            jax.ShapeDtypeStruct(message, bf16),
        ],
        scratch_shapes=[
            pltpu.VMEM((block, grid_rows, channels), bf16),
            pltpu.VMEM((channels, channels), f32),
            pltpu.VMEM((1, channels), f32),
            pltpu.VMEM((rows, grid_rows), bf16),
            pltpu.VMEM((columns // block, grid_rows, block, channels), bf16),
            pltpu.SemaphoreType.DMA((columns // block,)),
        ],
        compiler_params=params(60),
        cost_estimate=pl.CostEstimate(
            flops=4 * rows * pre_act.size, bytes_accessed=8 * pre_act.size, transcendentals=pre_act.size
        ),
        name="delta_and_x_sums",
    )(pre_act, cotangent, field_in)


def input_kernel(sizes, pieces, *refs):
    field_refs, out_refs, table = refs[:pieces], refs[pieces:-1], refs[-1]
    columns, channels = field_refs[0].shape[1:]
    block = pl.program_id(0)
    all_columns = columns * pl.num_programs(0)

    @pl.when(block == 0)
    def _():
        table[...] = x_table(sizes, relative=True)

    lines = [jnp.swapaxes(ref[...], 0, 1) for ref in field_refs]
    sums = matrix_per_column(
        table[...],
        [jnp.concatenate([part[y] for part in lines], axis=0) for y in range(columns)],
    )
    first = pl.multiple_of(block * columns, columns)
    rows = sums.shape[0] // len(out_refs)
    for pair, out_ref in enumerate(out_refs):
        for row in range(rows):
            out_ref[pl.ds(row * all_columns + first, columns), :] = sums[pair * rows + row]


def input_call(sizes, field_in):
    grid_rows, columns, channels = field_in.shape
    half = sizes[0]
    rows = 2 * half * (sizes[1] + 1)
    block = min(16, columns)
    pieces = 4
    message = (2 * rows // half * columns, channels)
    return pl.pallas_call(
        functools.partial(input_kernel, sizes, pieces),
        grid=(columns // block,),
        in_specs=[
            pl.BlockSpec(
                (grid_rows // pieces, block, channels), lambda i, piece=piece: (piece, i, 0)
            )
            for piece in range(pieces)
        ],
        out_specs=[whole(message)] * (half // 2),
        out_shape=[jax.ShapeDtypeStruct(message, bf16)] * (half // 2),
        scratch_shapes=[pltpu.VMEM((rows, grid_rows), bf16)],
        compiler_params=params(60),
        cost_estimate=pl.CostEstimate(
            flops=2 * rows * field_in.size, bytes_accessed=4 * field_in.size, transcendentals=0
        ),
        name="input_x_sums",
    )(*[field_in] * pieces)


def y_transform_kernel(columns, extra, blocks, total_rows, places, arrays, table_ref, *refs):
    line_refs, out_refs = refs[:arrays], refs[arrays:]
    sources, channels = len(places), line_refs[0].shape[-1]

    def rows_of(source, first, last):
        array, at = places[source]
        return line_refs[array][at + first : at + last]

    frequencies = (total_rows - extra) // columns // 2
    own = blocks // 2
    size = table_ref.shape[0] // blocks
    table = table_ref[...]
    for t in range(frequencies):
        lines = jnp.concatenate(
            [
                rows_of(source, row * columns, (row + 1) * columns)
                for row in (2 * t, 2 * t + 1)
                for source in range(sources)
            ],
            axis=0,
        )
        sums = jnp.dot(table, lines, preferred_element_type=f32).astype(bf16)
        for block in range(blocks):
            held = t if block < own else frequencies - 1 - t
            if 0 <= held < frequencies - 1:
                first = (block // len(out_refs)) * (frequencies - 1) + held
                out_refs[block % len(out_refs)][first * size : (first + 1) * size] = sums[
                    block * size : (block + 1) * size
                ]
    if extra:
        rows = channels // sources
        pieces = [
            unpack_share(rows, rows_of(i, total_rows - extra, total_rows)) for i in range(sources)
        ]
        packed = pack_share(sum(p[0] for p in pieces), sum(p[1] for p in pieces))
        for out_ref in out_refs:
            out_ref[out_ref.shape[0] - extra :] = packed


def y_transform_call(table, lines, places, total_rows, blocks, outputs, columns, extra):
    channels = lines[0].shape[-1]
    held = (total_rows - extra) // columns // 2 - 1
    size = table.shape[0] // blocks
    rows = blocks // outputs * held * size + extra
    return pl.pallas_call(
        functools.partial(
            y_transform_kernel, columns, extra, blocks, total_rows, places, len(lines)
        ),
        out_shape=[jax.ShapeDtypeStruct((rows, channels), bf16)] * outputs,
        compiler_params=params(),
        cost_estimate=pl.CostEstimate(
            flops=2 * (held + 1) * table.size * channels,
            bytes_accessed=4 * len(places) * total_rows * channels,
            transcendentals=0,
        ),
        name="y_sums",
    )(table, *lines)


def turned(values):
    rows = values.shape[0]
    even = lax.broadcasted_iota(jnp.int32, values.shape, 0) % 2 == 0
    up = pltpu.roll(values, rows - 1, 0)
    down = pltpu.roll(values, 1, 0)
    return jnp.concatenate([values, jnp.where(even, up, -down)], axis=1)


def load_kernel(source_ref, target_ref, semaphores):
    copies = [
        pltpu.make_async_copy(source_ref.at[j, k], target_ref.at[j, k], semaphores.at[j, k])
        for j in range(source_ref.shape[0])
        for k in range(source_ref.shape[1])
    ]
    for copy in copies:
        copy.start()
    for copy in copies:
        copy.wait()


def load_call(weight):
    held, modes, _, channels, _ = weight.shape
    parts = weight.reshape(held, 2, modes // 2, 2, channels, channels)
    loaded = pl.pallas_call(
        load_kernel,
        in_specs=[pl.BlockSpec(memory_space=pl.ANY)],
        out_specs=pl.BlockSpec(memory_space=pl.ANY),
        out_shape=pltpu.VMEM(parts.shape, bf16),
        scratch_shapes=[pltpu.SemaphoreType.DMA((held, 2))],
        compiler_params=params(50),
        cost_estimate=pl.CostEstimate(flops=0, bytes_accessed=4 * weight.size, transcendentals=0),
        name="weights_to_vmem",
    )(parts)
    return loaded.reshape(weight.shape)


def back_kernel(share, scale_ref, weight_ref, *refs):
    part_refs, (back_ref, delta_ref, share_ref) = refs[:-3], refs[-3:]
    held, rows, channels = delta_ref.shape
    block = weight_ref.shape[1]
    j, k = pl.program_id(0), pl.program_id(1)
    first = pl.multiple_of((j * (rows // (2 * block)) + k) * 2 * block, 2 * block)
    here = pl.ds(first, 2 * block)
    inner = pl.ds(pl.multiple_of(k * 2 * block, 2 * block), 2 * block)
    total = part_refs[0][here].astype(f32)
    for ref in part_refs[1:]:
        total = total + ref[here].astype(f32)
    delta = total.astype(bf16)
    delta_ref[j, inner] = delta
    both = turned(delta.astype(f32)).astype(bf16)
    sums = []
    for mode in range(block):
        weight = jnp.concatenate([weight_ref[0, mode, 0], weight_ref[0, mode, 1]], axis=1)
        sums.append(
            lax.dot_general(
                both[2 * mode : 2 * mode + 2],
                weight,
                (((1,), (1,)), ((), ())),
                preferred_element_type=f32,
            )
        )
    back_ref[j, inner] = (jnp.concatenate(sums, axis=0) * scale_ref[inner]).astype(bf16)

    @pl.when((j == 0) & (k == 0))
    def _():
        extra = share_ref.shape[0]
        pieces = [unpack_share(share, ref[ref.shape[0] - extra :]) for ref in part_refs]
        share_ref[...] = pack_share(sum(p[0] for p in pieces), sum(p[1] for p in pieces))


def back_call(scale_rows, weight, parts, share):
    held, modes, _, channels, _ = weight.shape
    block = min(16, modes)
    shape = (held, 2 * modes, channels)
    extra = (parts[0].shape[0] - held * 2 * modes, channels)
    return pl.pallas_call(
        functools.partial(back_kernel, share),
        grid=(held, modes // block),
        in_specs=[
            whole(scale_rows.shape),
            pl.BlockSpec((1, block, 2, channels, channels), lambda j, k: (j, k, 0, 0, 0)),
        ]
        + [whole(part.shape) for part in parts],
        out_specs=[whole(shape), whole(shape), whole(extra)],
        out_shape=[
            jax.ShapeDtypeStruct(shape, bf16),
            jax.ShapeDtypeStruct(shape, bf16),
            jax.ShapeDtypeStruct(extra, bf16),
        ],
        compiler_params=params(),
        cost_estimate=pl.CostEstimate(
            flops=4 * weight.size, bytes_accessed=2 * weight.size, transcendentals=0
        ),
        name="mode_back",
    )(scale_rows, weight, *parts)


def outer_kernel(scale_ref, delta_ref, *refs):
    part_refs, out_ref = refs[:-1], refs[-1]
    modes = out_ref.shape[1]
    channels = out_ref.shape[-1]
    total = part_refs[0][...].astype(f32)
    for ref in part_refs[1:]:
        total = total + ref[...].astype(f32)
    field = (total.astype(bf16).astype(f32) * scale_ref[...]).astype(bf16).astype(f32)
    delta = turned(delta_ref[0].astype(f32))
    group = 4
    mode_of_row = lax.broadcasted_iota(jnp.int32, (2 * group, 2 * channels), 0) // 2
    for first in range(0, modes, group):
        rows = slice(2 * first, 2 * (first + group))
        alone = [jnp.where(mode_of_row == i, delta[rows], 0.0) for i in range(group)]
        product = lax.dot_general(
            field[rows].astype(bf16),
            jnp.concatenate(alone, axis=1).astype(bf16),
            (((0,), (0,)), ((), ())),
            preferred_element_type=f32,
        ).astype(bf16)
        for i in range(2 * group):
            out_ref[0, first + i // 2, i % 2] = product[:, i * channels : (i + 1) * channels]


def outer_call(scale_rows, delta, parts):
    held, rows, channels = delta.shape
    modes = rows // 2
    part = pl.BlockSpec((1, rows, channels), lambda j: (j, 0, 0))
    return pl.pallas_call(
        outer_kernel,
        grid=(held,),
        in_specs=[whole((rows, channels)), part]
        + [
            pl.BlockSpec((rows, channels), lambda j, first=first: (j + first, 0))
            for _, first in parts
        ],
        out_specs=pl.BlockSpec((1, modes, 2, channels, channels), lambda j: (j, 0, 0, 0, 0)),
        out_shape=jax.ShapeDtypeStruct((held, modes, 2, channels, channels), bf16),
        compiler_params=params(),
        cost_estimate=pl.CostEstimate(
            flops=6 * held * modes * channels * channels,
            bytes_accessed=4 * held * modes * channels * channels,
            transcendentals=0,
        ),
        name="grad_spectral",
    )(scale_rows, delta, *[part for part, _ in parts])


def y_inverse_kernel(columns, parts, table_ref, share_ref, *refs):
    part_refs, out_refs = refs[:parts], refs[parts:]
    channels = share_ref.shape[1]
    extra = share_ref.shape[0]
    message = out_refs[0].shape[0] // 2
    targets = 2 * len(out_refs)
    frequencies = (message - extra) // columns // 2
    own = parts // 2
    size = part_refs[0].shape[1]
    table = table_ref[...]
    for t in range(frequencies):
        first = 0 if t < frequencies - 1 else own
        last = 2 * own if t > 0 else own
        modes = jnp.concatenate(
            [
                part_refs[block][t if block < own else frequencies - 1 - t]
                for block in range(first, last)
            ],
            axis=0,
        )
        sums = lax.dot_general(
            table[first * size : last * size],
            modes,
            (((0,), (0,)), ((), ())),
            preferred_element_type=f32,
        ).astype(bf16)
        for part in range(2):
            for target in range(targets):
                at = target % 2 * message + (2 * t + part) * columns
                piece = part * targets + target
                out_refs[target // 2][at : at + columns] = sums[
                    piece * columns : (piece + 1) * columns
                ]
    for target in range(targets):
        last = (target % 2 + 1) * message
        out_refs[target // 2][last - extra : last] = share_ref[...]


def y_inverse_call(table, share, parts, targets, columns):
    held, size, channels = parts[0].shape
    rows = 2 * (held + 1)
    message = (2 * (rows * columns + share.shape[0]), channels)
    return pl.pallas_call(
        functools.partial(y_inverse_kernel, columns, len(parts)),
        out_shape=[jax.ShapeDtypeStruct(message, bf16)] * (targets // 2),
        compiler_params=params(),
        cost_estimate=pl.CostEstimate(
            flops=rows * table.size * channels,
            bytes_accessed=4 * targets * rows * columns * channels,
            transcendentals=0,
        ),
        name="y_inverse",
    )(table, share, *parts)


def final_kernel(sizes, places, arrays, *refs):
    line_refs, refs = refs[:arrays], refs[arrays:]
    delta_ref, weight_ref, out_ref, local_ref, bias_ref, table = refs
    grid_rows, columns, channels = out_ref.shape
    half = len(places)
    block = pl.program_id(0)
    all_columns = columns * pl.num_programs(0)
    per_source = table.shape[1] // half
    first = pl.multiple_of(block * columns, columns)

    @pl.when(block == 0)
    def _():
        table[...] = x_table(sizes, transposed=True, relative=True)

    lines = jnp.stack(
        [
            line_refs[array][pl.ds(at + row * all_columns + first, columns), :]
            for array, at in places
            for row in range(per_source)
        ],
        axis=0,
    )
    lines = jnp.swapaxes(lines, 0, 1)
    spectral = matrix_per_column(table[...], [lines[y] for y in range(columns)])
    local = lax.dot_general(
        delta_ref[...].reshape(grid_rows * columns, channels),
        weight_ref[...],
        (((1,), (1,)), ((), ())),
        preferred_element_type=f32,
    ).reshape(grid_rows, columns, channels)
    out_ref[...] = (spectral.astype(f32) + local).astype(bf16)

    @pl.when(block == 0)
    def _():
        share = channels // half
        extra = extra_rows(channels, half)
        pieces = []
        for array, at in places:
            begin = at + per_source * all_columns
            pieces.append(unpack_share(share, line_refs[array][begin : begin + extra]))
        for source, rows in enumerate(in_relative_order([piece[0] for piece in pieces], half)):
            local_ref[source * share : (source + 1) * share] = rows
        bias_ref[...] = pieces[0][1]


def final_call(sizes, lines, places, delta, local_weight):
    grid_rows, columns, channels = delta.shape
    rows = 2 * sizes[0] * (sizes[1] + 1)
    block = min(16, columns)
    field = pl.BlockSpec((grid_rows, block, channels), lambda i: (0, i, 0))
    return pl.pallas_call(
        functools.partial(final_kernel, sizes, places, len(lines)),
        grid=(columns // block,),
        in_specs=[whole(line.shape) for line in lines] + [field, whole(local_weight.shape)],
        out_specs=[field, whole((channels, channels)), whole((1, channels))],
        out_shape=[
            jax.ShapeDtypeStruct(delta.shape, bf16),
            jax.ShapeDtypeStruct((channels, channels), f32),
            jax.ShapeDtypeStruct((1, channels), f32),
        ],
        scratch_shapes=[pltpu.VMEM((grid_rows, rows), bf16)],
        compiler_params=params(),
        cost_estimate=pl.CostEstimate(
            flops=2 * (rows + channels) * delta.size, bytes_accessed=5 * delta.size, transcendentals=0
        ),
        name="x_inverse_and_local",
    )(*lines, delta, local_weight)


def on_device(field_in, pre_act, cotangent, spec_weight, local_weight):
    batch_size, slab_rows, col_block, channels = field_in.shape
    space_count = lax.axis_size("space")
    data_count = lax.axis_size("dp")
    grid_rows = slab_rows * space_count
    grid_cols = col_block * data_count
    kx_local, ky_local = spec_weight.shape[:2]
    half = data_count // 2
    half_cols = half * col_block
    row_count = 2 * (kx_local + 1)
    data_index = lax.axis_index("dp")
    space_index = lax.axis_index("space")
    upper = data_index // half

    sizes = (half, kx_local, slab_rows, grid_rows)

    blocks = 2 * space_count
    size = 2 * ky_local
    row = jnp.arange(blocks * size, dtype=jnp.int32)
    block, inner = row // size, row % size
    shift = block % space_count
    ky_index = (space_index + shift) % space_count * ky_local + inner // 2
    quarter = grid_cols // 4
    cosine_turn = inner % 2
    sine_turn = jnp.where((block // space_count) == upper, 1 + inner % 2, 3 * (1 - inner % 2))
    turn = jnp.concatenate(
        [
            jnp.broadcast_to(cosine_turn[:, None], (blocks * size, half_cols)),
            jnp.broadcast_to(sine_turn[:, None], (blocks * size, half_cols)),
        ],
        axis=1,
    )

    def y_basis(flip):
        column = jnp.arange(half_cols, dtype=jnp.int32)
        member = (column // col_block) ^ flip
        positions = upper * half_cols + member * col_block + column % col_block
        positions = jnp.concatenate([positions, positions])
        return cosine_table(ky_index[:, None] * positions[None, :] + quarter * turn, grid_cols)

    ky_row = space_index * ky_local + jnp.arange(size, dtype=jnp.int32) // 2
    scale = jnp.where(ky_row == 0, 1.0, 2.0).astype(f32) / (grid_rows * grid_cols)
    scale_rows = jnp.broadcast_to(scale[:, None], (size, channels))

    halves = [list(range(half)), list(range(half, data_count))]

    def exchange(values):
        return lax.all_to_all(
            values, "dp", split_axis=0, concat_axis=0, tiled=True, axis_index_groups=halves
        )

    def to_chips(chips):
        arrived = [chips[0]]
        for pair in range(1, half // 2):
            moves = [(d, d ^ (2 * pair)) for d in range(data_count)]
            arrived.append(lax.ppermute(chips[pair], "dp", moves))
        return arrived

    def between_cores(arrived):
        rows = arrived[0].shape[0] // 2
        mates = jnp.concatenate([part[rows:] for part in arrived], axis=0)
        mates = lax.ppermute(mates, "dp", [(d, d ^ 1) for d in range(data_count)])
        places = [
            (source // 2, 0) if source % 2 == 0 else (half // 2, source // 2 * rows)
            for source in range(half)
        ]
        return arrived + [mates], places

    def pairs(mirror, shift):
        moves = []
        for d in range(data_count):
            for s in range(space_count):
                target = data_count - 1 - d if mirror else d
                moves.append(
                    (d * space_count + s, target * space_count + (s + shift) % space_count)
                )
        return moves

    order = [(mirror, shift) for mirror in (1, 0) for shift in reversed(range(space_count))][:-1]

    def gathered(parts):
        held = [parts[0]]
        for mirror, shift in order:
            held.append(
                lax.ppermute(
                    parts[mirror * space_count + shift], ("dp", "space"), pairs(mirror, shift)
                )
            )
        return held

    tied = lax.optimization_barrier

    share = channels // half
    extra = extra_rows(channels, half)

    message = row_count * col_block
    y_table = y_basis(0)
    relative_table = y_basis(data_index % half)

    arrived = to_chips(input_call(sizes, field_in[0]))
    delta, delta_sums = delta_call(sizes, pre_act[0], cotangent[0], field_in[0])
    delta_sums, arrived = tied((delta_sums, arrived))
    delta_lines = exchange(delta_sums)
    lines, places = between_cores(arrived)
    input_parts = list(
        y_transform_call(
            relative_table, lines, places, message, blocks, space_count, col_block, 0
        )
    )
    for shift in range(1, space_count):
        input_parts[shift] = lax.ppermute(input_parts[shift], ("dp", "space"), pairs(0, shift))
    held_rows = kx_local * size
    mirrored = sum(part[held_rows:].astype(f32) for part in input_parts).astype(bf16)
    delta_lines, mirrored = tied((delta_lines, mirrored))

    message += extra
    delta_parts = y_transform_call(
        y_table,
        [delta_lines.reshape(half * message, channels)],
        [(0, source * message) for source in range(half)],
        message,
        blocks,
        blocks,
        col_block,
        extra,
    )
    delta_parts = list(delta_parts)
    rows = delta_parts[space_count].shape[0]
    delta_parts[space_count] = jnp.concatenate([delta_parts[space_count], mirrored], axis=0)
    weight, delta_parts = tied((spec_weight, delta_parts))
    weight = load_call(weight)
    delta_held = gathered(delta_parts)
    place = 1 + order.index((1, 0))
    input_held = [(part, 0) for part in input_parts] + [(delta_held[place][rows:], 0)]
    delta_held[place] = delta_held[place][:rows]
    back, delta_owned, share_rows = back_call(scale_rows, weight, delta_held, share)
    received = {(0, 0): back}
    for mirror, shift in order:
        received[(mirror, -shift % space_count)] = lax.ppermute(
            back, ("dp", "space"), pairs(mirror, shift)
        )
    modes = [received[(mirror, shift)] for mirror in (0, 1) for shift in range(space_count)]
    column_sums = y_inverse_call(relative_table, share_rows, modes, half, col_block)
    column_sums, delta_owned = tied((column_sums, delta_owned))
    columns = to_chips(column_sums)
    grad_spectral = outer_call(scale_rows, delta_owned, input_held)
    columns, grad_spectral = tied((columns, grad_spectral))
    lines, places = between_cores(columns)
    grad_input, grad_local, bias_rows = final_call(sizes, lines, places, delta, local_weight)
    return (grad_input[None], grad_spectral, grad_local, bias_rows.reshape(channels))


def solution(mesh):
    placed = (
        P(None, "space", "dp", None),
        P(None, "space", "dp", None),
        P(None, "space", "dp", None),
        P("dp", "space", None, None, None),
        P(),
    )
    return jax.shard_map(
        on_device,
        mesh=mesh,
        in_specs=placed,
        out_specs=(P(None, "space", "dp", None), P("dp", "space", None, None, None), P(), P()),
        check_vma=False,
    )
```

```python
import functools
import math

import jax
import jax.numpy as jnp
from jax import lax
from jax.experimental import pallas as pl
from jax.experimental.pallas import tpu as pltpu
from jax.sharding import PartitionSpec as P

root_two_pi = 0.7978845608028654
cubic_coef = 0.044715
f32 = jnp.float32
bf16 = jnp.bfloat16
mebi = 1024 * 1024


def gelu_slope(values):
    square = values * values
    cubic = root_two_pi * cubic_coef
    tangent = jnp.tanh(values * (root_two_pi + cubic * square))
    inner = values * (1.0 - tangent * tangent)
    return 0.5 * ((1.0 + tangent) + inner * (root_two_pi + (3.0 * cubic) * square))


def cosine_table(phases, period):
    quarter = period // 4
    if period & (period - 1) == 0:
        turns = (phases + quarter // 2) >> (quarter.bit_length() - 1)
    else:
        turns = (phases + quarter // 2) // quarter
    angle = (phases - turns * quarter).astype(f32) * (2.0 * math.pi / period)
    square = angle * angle
    cosine = 1.0 + square * (
        -0.5 + square * (1.0 / 24.0 + square * (-1.0 / 720.0 + square * (1.0 / 40320.0)))
    )
    sine = angle * (
        1.0
        + square
        * (-1.0 / 6.0 + square * (1.0 / 120.0 + square * (-1.0 / 5040.0 + square * (1.0 / 362880.0))))
    )
    turns = turns & 3
    magnitude = jnp.where((turns & 1) == 0, cosine, sine)
    return jnp.where((turns == 1) | (turns == 2), -magnitude, magnitude).astype(bf16)


def x_table(sizes, transposed=False, relative=False):
    half, kx_local, slab_rows, grid_rows = sizes
    row_count = 2 * (kx_local + 1)
    upper = (lax.axis_index("dp") >= half).astype(jnp.int32)
    shape = (half * row_count, slab_rows)
    if transposed:
        shape = shape[::-1]
    row = lax.broadcasted_iota(jnp.int32, shape, 1 if transposed else 0)
    position = lax.axis_index("space") * slab_rows + lax.broadcasted_iota(
        jnp.int32, shape, 0 if transposed else 1
    )
    member = sum((row >= i * row_count).astype(jnp.int32) for i in range(1, half))
    inner = row - member * row_count
    if relative:
        member = member ^ (lax.axis_index("dp") & (half - 1))
    ascending = member * kx_local + (inner >> 1)
    frequency = ascending + upper * (half * kx_local - 2 * ascending)
    quarter = grid_rows // 4
    return cosine_table(frequency * position - (inner & 1) * quarter, grid_rows)


def params(mebibytes=16):
    return pltpu.CompilerParams(vmem_limit_bytes=mebibytes * mebi)


def whole(shape):
    return pl.BlockSpec(shape, lambda *_: (0,) * len(shape))


def matrix_per_column(table, columns_of, rows=()):
    channels = columns_of[0].shape[1]
    results = []
    totals = [0.0] * len(rows)
    for y in range(0, len(columns_of), 2):
        pair = jnp.concatenate(columns_of[y : y + 2], axis=1)
        sums = jnp.dot(table, pair, preferred_element_type=f32)
        totals = [total + sums[row : row + 1] for total, row in zip(totals, rows)]
        sums = sums.astype(bf16)
        results += [sums[:, :channels], sums[:, channels:]]
    results = jnp.swapaxes(jnp.stack(results, axis=0), 0, 1)
    if rows:
        return results, [total[:, :channels] + total[:, channels:] for total in totals]
    return results


def two_terms(values):
    high = values.astype(bf16)
    return high, (values - high.astype(f32)).astype(bf16)


def extra_rows(channels, half):
    return -(-2 * (channels // half) // 16) * 16


def packed_rows(channels, half):
    return -(-(2 * (channels // half) + 2) // 16) * 16


def stacked(parts, rows):
    parts = list(parts)
    filled = sum(part.shape[0] for part in parts)
    if rows > filled:
        parts.append(jnp.zeros((rows - filled, parts[0].shape[1]), bf16))
    return jnp.concatenate([part.astype(f32) for part in parts], axis=0).astype(bf16)


def pack_share(share, bias):
    rows, channels = share.shape
    return stacked(two_terms(share) + two_terms(bias), packed_rows(channels, channels // rows))


def unpack_terms(rows, message):
    message = message.astype(f32)
    return message[:rows] + message[rows : 2 * rows]


def unpack_share(rows, message):
    return unpack_terms(rows, message), unpack_terms(1, message[2 * rows : 2 * rows + 2])


def bias_places(half, rows):
    return (0, 1), (half - 1, rows - 1)


def in_relative_order(pieces, half):
    place = lax.axis_index("dp")
    key = jnp.where(place >= half, 2 * half - 1 - place, place)
    step = 1
    while step < half:
        flag = (key & step) != 0
        pieces = [jnp.where(flag, pieces[i ^ step], pieces[i]) for i in range(half)]
        step *= 2
    return pieces


def delta_kernel(
    sizes,
    pre_ref,
    cot_ref,
    field_ref,
    delta_ref,
    out_ref,
    lines,
    local,
    bias,
    table,
    field,
    semaphores,
):
    grid_rows, columns, channels = pre_ref.shape
    half = out_ref.shape[0]
    block = pl.program_id(0)
    all_columns = columns * pl.num_programs(0)
    step = 16
    blocks = field.shape[0]

    def arriving(i):
        return pltpu.make_async_copy(
            field_ref.at[:, pl.ds(i * columns, columns)], field.at[i], semaphores.at[i]
        )

    @pl.when(block == 0)
    def _():
        for i in range(blocks):
            arriving(i).start()
        local[...] = jnp.zeros_like(local)
        bias[...] = jnp.zeros_like(bias)
        table[...] = x_table(sizes)

    def slab(i, carry):
        rows = pl.ds(pl.multiple_of(i * step, step), step)
        slope = gelu_slope(pre_ref[rows].astype(f32))
        delta = (cot_ref[rows].astype(f32) * slope).astype(bf16)
        delta_ref[rows] = delta
        lines[:, rows, :] = jnp.swapaxes(delta, 0, 1)
        return carry

    lax.fori_loop(0, grid_rows // step, slab, 0, unroll=2)
    sums, totals = matrix_per_column(
        table[...], [lines[y] for y in range(columns)], (0, table.shape[0] - 2)
    )
    upper = lax.axis_index("dp") >= half
    bias[...] += jnp.where(upper, totals[1], totals[0])
    for i in range(blocks):

        @pl.when(block == i)
        def _(i=i):
            arriving(i).wait()

    local[...] += lax.dot_general(
        field[block].reshape(grid_rows * columns, channels),
        delta_ref[...].reshape(grid_rows * columns, channels),
        (((0,), (0,)), ((), ())),
        preferred_element_type=f32,
    )
    per_target = sums.shape[0] // half
    first = pl.multiple_of(block * columns, columns)
    for target in range(half):
        for row in range(per_target):
            out_ref[target, pl.ds(row * all_columns + first, columns), :] = sums[
                target * per_target + row
            ]

    @pl.when(block == pl.num_programs(0) - 1)
    def _():
        share = channels // half
        for target in range(half):
            mine = local[target * share : (target + 1) * share]
            mirrored = local[(half - 1 - target) * share : (half - target) * share]
            rows = two_terms(jnp.where(upper, mirrored, mine))
            out_ref[target, per_target * all_columns :] = stacked(
                rows, out_ref.shape[1] - per_target * all_columns
            )
        terms = stacked(two_terms(bias[...]), columns).astype(f32)
        for in_upper, (member, row) in enumerate(bias_places(half, per_target)):
            here = slice(row * all_columns, row * all_columns + columns)
            old = out_ref[member, here].astype(f32)
            ours = upper if in_upper else jnp.logical_not(upper)
            out_ref[member, here] = jnp.where(ours, terms, old).astype(bf16)


def delta_call(sizes, pre_act, cotangent, field_in):
    grid_rows, columns, channels = pre_act.shape
    half = sizes[0]
    rows = 2 * half * (sizes[1] + 1)
    block = min(16, columns)
    field = pl.BlockSpec((grid_rows, block, channels), lambda i: (0, i, 0))
    message = (half, rows // half * columns + extra_rows(channels, half), channels)
    return pl.pallas_call(
        functools.partial(delta_kernel, sizes),
        grid=(columns // block,),
        in_specs=[field, field, pl.BlockSpec(memory_space=pl.ANY)],
        out_specs=[field, whole(message)],
        out_shape=[
            jax.ShapeDtypeStruct(pre_act.shape, bf16),
            jax.ShapeDtypeStruct(message, bf16),
        ],
        scratch_shapes=[
            pltpu.VMEM((block, grid_rows, channels), bf16),
            pltpu.VMEM((channels, channels), f32),
            pltpu.VMEM((1, channels), f32),
            pltpu.VMEM((rows, grid_rows), bf16),
            pltpu.VMEM((columns // block, grid_rows, block, channels), bf16),
            pltpu.SemaphoreType.DMA((columns // block,)),
        ],
        compiler_params=params(60),
        cost_estimate=pl.CostEstimate(
            flops=4 * rows * pre_act.size, bytes_accessed=8 * pre_act.size, transcendentals=pre_act.size
        ),
        name="delta_and_x_sums",
    )(pre_act, cotangent, field_in)


def input_kernel(sizes, pieces, *refs):
    field_refs, out_refs, table = refs[:pieces], refs[pieces:-1], refs[-1]
    columns, channels = field_refs[0].shape[1:]
    block = pl.program_id(0)
    all_columns = columns * pl.num_programs(0)

    @pl.when(block == 0)
    def _():
        table[...] = x_table(sizes, relative=True)

    lines = [jnp.swapaxes(ref[...], 0, 1) for ref in field_refs]
    sums = matrix_per_column(
        table[...],
        [jnp.concatenate([part[y] for part in lines], axis=0) for y in range(columns)],
    )
    first = pl.multiple_of(block * columns, columns)
    rows = sums.shape[0] // len(out_refs)
    for pair, out_ref in enumerate(out_refs):
        for row in range(rows):
            out_ref[pl.ds(row * all_columns + first, columns), :] = sums[pair * rows + row]


def input_call(sizes, field_in):
    grid_rows, columns, channels = field_in.shape
    half = sizes[0]
    rows = 2 * half * (sizes[1] + 1)
    block = min(16, columns)
    pieces = 4
    message = (2 * rows // half * columns, channels)
    return pl.pallas_call(
        functools.partial(input_kernel, sizes, pieces),
        grid=(columns // block,),
        in_specs=[
            pl.BlockSpec(
                (grid_rows // pieces, block, channels), lambda i, piece=piece: (piece, i, 0)
            )
            for piece in range(pieces)
        ],
        out_specs=[whole(message)] * (half // 2),
        out_shape=[jax.ShapeDtypeStruct(message, bf16)] * (half // 2),
        scratch_shapes=[pltpu.VMEM((rows, grid_rows), bf16)],
        compiler_params=params(60),
        cost_estimate=pl.CostEstimate(
            flops=2 * rows * field_in.size, bytes_accessed=4 * field_in.size, transcendentals=0
        ),
        name="input_x_sums",
    )(*[field_in] * pieces)


def y_transform_kernel(columns, extra, blocks, total_rows, places, arrays, table_ref, *refs):
    line_refs, out_refs = refs[:arrays], refs[arrays:]
    sources, channels = len(places), line_refs[0].shape[-1]

    def rows_of(source, first, last):
        array, at = places[source]
        return line_refs[array][at + first : at + last]

    frequencies = (total_rows - extra) // columns // 2
    own = blocks // 2
    size = table_ref.shape[0] // blocks
    table = table_ref[...]
    place = lax.axis_index("dp")
    for t in range(frequencies):
        pieces = [
            rows_of(source, row * columns, (row + 1) * columns)
            for row in (2 * t, 2 * t + 1)
            for source in range(sources)
        ]
        for in_upper, (member, row) in enumerate(bias_places(sources, 2 * frequencies)):
            if extra and row == 2 * t + 1:
                keep = jnp.where(place == in_upper * (2 * sources - 1), 0.0, 1.0).astype(f32)
                pieces[sources:] = [
                    (piece.astype(f32) * keep).astype(bf16) for piece in pieces[sources:]
                ]
        lines = jnp.concatenate(pieces, axis=0)
        sums = jnp.dot(table, lines, preferred_element_type=f32).astype(bf16)
        for block in range(blocks):
            held = t if block < own else frequencies - 1 - t
            if 0 <= held < frequencies - 1:
                first = (block // len(out_refs)) * (frequencies - 1) + held
                out_refs[block % len(out_refs)][first * size : (first + 1) * size] = sums[
                    block * size : (block + 1) * size
                ]
    if extra:
        share = channels // sources
        shares = [
            unpack_terms(share, rows_of(i, total_rows - extra, total_rows)) for i in range(sources)
        ]
        bias = 0.0
        for in_upper, (member, row) in enumerate(bias_places(sources, 2 * frequencies)):
            first = row * columns
            total = sum(
                unpack_terms(1, rows_of(i, first, first + min(16, columns))) for i in range(sources)
            )
            bias = bias + jnp.where(place == in_upper * (2 * sources - 1), total, 0.0)
        packed = pack_share(sum(shares), bias)
        for out_ref in out_refs:
            out_ref[out_ref.shape[0] - packed.shape[0] :] = packed


def y_transform_call(table, lines, places, total_rows, blocks, outputs, columns, extra):
    channels = lines[0].shape[-1]
    held = (total_rows - extra) // columns // 2 - 1
    size = table.shape[0] // blocks
    rows = blocks // outputs * held * size
    if extra:
        rows += packed_rows(channels, len(places))
    return pl.pallas_call(
        functools.partial(
            y_transform_kernel, columns, extra, blocks, total_rows, places, len(lines)
        ),
        out_shape=[jax.ShapeDtypeStruct((rows, channels), bf16)] * outputs,
        compiler_params=params(),
        cost_estimate=pl.CostEstimate(
            flops=2 * (held + 1) * table.size * channels,
            bytes_accessed=4 * len(places) * total_rows * channels,
            transcendentals=0,
        ),
        name="y_sums",
    )(table, *lines)


def turned(values):
    rows = values.shape[0]
    even = lax.broadcasted_iota(jnp.int32, values.shape, 0) % 2 == 0
    up = pltpu.roll(values, rows - 1, 0)
    down = pltpu.roll(values, 1, 0)
    return jnp.concatenate([values, jnp.where(even, up, -down)], axis=1)


def load_kernel(source_ref, target_ref, semaphores):
    copies = [
        pltpu.make_async_copy(source_ref.at[j, k], target_ref.at[j, k], semaphores.at[j, k])
        for j in range(source_ref.shape[0])
        for k in range(source_ref.shape[1])
    ]
    for copy in copies:
        copy.start()
    for copy in copies:
        copy.wait()


def load_call(weight):
    held, modes, _, channels, _ = weight.shape
    parts = weight.reshape(held, 2, modes // 2, 2, channels, channels)
    loaded = pl.pallas_call(
        load_kernel,
        in_specs=[pl.BlockSpec(memory_space=pl.ANY)],
        out_specs=pl.BlockSpec(memory_space=pl.ANY),
        out_shape=pltpu.VMEM(parts.shape, bf16),
        scratch_shapes=[pltpu.SemaphoreType.DMA((held, 2))],
        compiler_params=params(50),
        cost_estimate=pl.CostEstimate(flops=0, bytes_accessed=4 * weight.size, transcendentals=0),
        name="weights_to_vmem",
    )(parts)
    return loaded.reshape(weight.shape)


def back_kernel(share, scale_ref, weight_ref, *refs):
    part_refs, (back_ref, delta_ref, share_ref) = refs[:-3], refs[-3:]
    held, rows, channels = delta_ref.shape
    block = weight_ref.shape[1]
    j, k = pl.program_id(0), pl.program_id(1)
    first = pl.multiple_of((j * (rows // (2 * block)) + k) * 2 * block, 2 * block)
    here = pl.ds(first, 2 * block)
    inner = pl.ds(pl.multiple_of(k * 2 * block, 2 * block), 2 * block)
    total = part_refs[0][here].astype(f32)
    for ref in part_refs[1:]:
        total = total + ref[here].astype(f32)
    delta = total.astype(bf16)
    delta_ref[j, inner] = delta
    both = turned(delta.astype(f32)).astype(bf16)
    sums = []
    for mode in range(block):
        weight = jnp.concatenate([weight_ref[0, mode, 0], weight_ref[0, mode, 1]], axis=1)
        sums.append(
            lax.dot_general(
                both[2 * mode : 2 * mode + 2],
                weight,
                (((1,), (1,)), ((), ())),
                preferred_element_type=f32,
            )
        )
    back_ref[j, inner] = (jnp.concatenate(sums, axis=0) * scale_ref[inner]).astype(bf16)

    @pl.when((j == 0) & (k == 0))
    def _():
        extra = share_ref.shape[0]
        pieces = [unpack_share(share, ref[ref.shape[0] - extra :]) for ref in part_refs]
        share_ref[...] = pack_share(sum(p[0] for p in pieces), sum(p[1] for p in pieces))


def back_call(scale_rows, weight, parts, share):
    held, modes, _, channels, _ = weight.shape
    block = min(16, modes)
    shape = (held, 2 * modes, channels)
    extra = (parts[0].shape[0] - held * 2 * modes, channels)
    return pl.pallas_call(
        functools.partial(back_kernel, share),
        grid=(held, modes // block),
        in_specs=[
            whole(scale_rows.shape),
            pl.BlockSpec((1, block, 2, channels, channels), lambda j, k: (j, k, 0, 0, 0)),
        ]
        + [whole(part.shape) for part in parts],
        out_specs=[whole(shape), whole(shape), whole(extra)],
        out_shape=[
            jax.ShapeDtypeStruct(shape, bf16),
            jax.ShapeDtypeStruct(shape, bf16),
            jax.ShapeDtypeStruct(extra, bf16),
        ],
        compiler_params=params(),
        cost_estimate=pl.CostEstimate(
            flops=4 * weight.size, bytes_accessed=2 * weight.size, transcendentals=0
        ),
        name="mode_back",
    )(scale_rows, weight, *parts)


def outer_kernel(scale_ref, delta_ref, *refs):
    part_refs, out_ref = refs[:-1], refs[-1]
    modes = out_ref.shape[1]
    channels = out_ref.shape[-1]
    total = part_refs[0][...].astype(f32)
    for ref in part_refs[1:]:
        total = total + ref[...].astype(f32)
    field = (total.astype(bf16).astype(f32) * scale_ref[...]).astype(bf16).astype(f32)
    delta = turned(delta_ref[0].astype(f32))
    group = 4
    mode_of_row = lax.broadcasted_iota(jnp.int32, (2 * group, 2 * channels), 0) // 2
    for first in range(0, modes, group):
        rows = slice(2 * first, 2 * (first + group))
        alone = [jnp.where(mode_of_row == i, delta[rows], 0.0) for i in range(group)]
        product = lax.dot_general(
            field[rows].astype(bf16),
            jnp.concatenate(alone, axis=1).astype(bf16),
            (((0,), (0,)), ((), ())),
            preferred_element_type=f32,
        ).astype(bf16)
        for i in range(2 * group):
            out_ref[0, first + i // 2, i % 2] = product[:, i * channels : (i + 1) * channels]


def outer_call(scale_rows, delta, parts):
    held, rows, channels = delta.shape
    modes = rows // 2
    part = pl.BlockSpec((1, rows, channels), lambda j: (j, 0, 0))
    return pl.pallas_call(
        outer_kernel,
        grid=(held,),
        in_specs=[whole((rows, channels)), part]
        + [
            pl.BlockSpec((rows, channels), lambda j, first=first: (j + first, 0))
            for _, first in parts
        ],
        out_specs=pl.BlockSpec((1, modes, 2, channels, channels), lambda j: (j, 0, 0, 0, 0)),
        out_shape=jax.ShapeDtypeStruct((held, modes, 2, channels, channels), bf16),
        compiler_params=params(),
        cost_estimate=pl.CostEstimate(
            flops=6 * held * modes * channels * channels,
            bytes_accessed=4 * held * modes * channels * channels,
            transcendentals=0,
        ),
        name="grad_spectral",
    )(scale_rows, delta, *[part for part, _ in parts])


def y_inverse_kernel(columns, parts, table_ref, share_ref, *refs):
    part_refs, out_refs = refs[:parts], refs[parts:]
    channels = share_ref.shape[1]
    message = out_refs[0].shape[0] // 2
    targets = 2 * len(out_refs)
    extra = extra_rows(channels, targets)
    frequencies = (message - extra) // columns // 2
    own = parts // 2
    size = part_refs[0].shape[1]
    table = table_ref[...]
    for t in range(frequencies):
        first = 0 if t < frequencies - 1 else own
        last = 2 * own if t > 0 else own
        modes = jnp.concatenate(
            [
                part_refs[block][t if block < own else frequencies - 1 - t]
                for block in range(first, last)
            ],
            axis=0,
        )
        sums = lax.dot_general(
            table[first * size : last * size],
            modes,
            (((0,), (0,)), ((), ())),
            preferred_element_type=f32,
        ).astype(bf16)
        for part in range(2):
            for target in range(targets):
                at = target % 2 * message + (2 * t + part) * columns
                piece = part * targets + target
                out_refs[target // 2][at : at + columns] = sums[
                    piece * columns : (piece + 1) * columns
                ]
    for target in range(targets):
        last = (target % 2 + 1) * message
        out_refs[target // 2][last - extra : last] = share_ref[:extra]
    place = lax.axis_index("dp")
    height = min(16, columns)
    share = channels // targets
    terms = share_ref[2 * share : 2 * share + height].astype(f32)
    for in_upper, (member, row) in enumerate(bias_places(targets, 2 * frequencies)):
        ours = place == in_upper * (2 * targets - 1)
        for target in range(targets):
            first = target % 2 * message + row * columns
            old = out_refs[target // 2][first : first + height].astype(f32)
            out_refs[target // 2][first : first + height] = jnp.where(ours, terms, old).astype(bf16)


def y_inverse_call(table, share, parts, targets, columns):
    held, size, channels = parts[0].shape
    rows = 2 * (held + 1)
    message = (2 * (rows * columns + extra_rows(channels, targets)), channels)
    return pl.pallas_call(
        functools.partial(y_inverse_kernel, columns, len(parts)),
        out_shape=[jax.ShapeDtypeStruct(message, bf16)] * (targets // 2),
        compiler_params=params(),
        cost_estimate=pl.CostEstimate(
            flops=rows * table.size * channels,
            bytes_accessed=4 * targets * rows * columns * channels,
            transcendentals=0,
        ),
        name="y_inverse",
    )(table, share, *parts)


def final_kernel(sizes, places, arrays, *refs):
    line_refs, refs = refs[:arrays], refs[arrays:]
    delta_ref, weight_ref, out_ref, local_ref, bias_ref, table = refs
    grid_rows, columns, channels = out_ref.shape
    half = len(places)
    block = pl.program_id(0)
    all_columns = columns * pl.num_programs(0)
    per_source = table.shape[1] // half
    first = pl.multiple_of(block * columns, columns)

    @pl.when(block == 0)
    def _():
        table[...] = x_table(sizes, transposed=True, relative=True)

    lines = jnp.stack(
        [
            line_refs[array][pl.ds(at + row * all_columns + first, columns), :]
            for array, at in places
            for row in range(per_source)
        ],
        axis=0,
    )
    lines = jnp.swapaxes(lines, 0, 1)
    spectral = matrix_per_column(table[...], [lines[y] for y in range(columns)])
    local = lax.dot_general(
        delta_ref[...].reshape(grid_rows * columns, channels),
        weight_ref[...],
        (((1,), (1,)), ((), ())),
        preferred_element_type=f32,
    ).reshape(grid_rows, columns, channels)
    out_ref[...] = (spectral.astype(f32) + local).astype(bf16)

    @pl.when(block == 0)
    def _():
        share = channels // half
        extra = extra_rows(channels, half)
        upper = lax.axis_index("dp") >= half
        rows_low, rows_high = (row for _, row in bias_places(half, per_source))
        shares, biases = [], []
        for array, at in places:
            begin = at + per_source * all_columns
            shares.append(unpack_terms(share, line_refs[array][begin : begin + extra]))
            low, high = (
                unpack_terms(1, line_refs[array][at + row * all_columns : at + row * all_columns + columns])
                for row in (rows_low, rows_high)
            )
            biases.append(jnp.where(upper, high, low))
        for source, rows in enumerate(in_relative_order(shares, half)):
            local_ref[source * share : (source + 1) * share] = rows
        bias_ref[...] = in_relative_order(biases, half)[0]


def final_call(sizes, lines, places, delta, local_weight):
    grid_rows, columns, channels = delta.shape
    rows = 2 * sizes[0] * (sizes[1] + 1)
    block = min(16, columns)
    field = pl.BlockSpec((grid_rows, block, channels), lambda i: (0, i, 0))
    return pl.pallas_call(
        functools.partial(final_kernel, sizes, places, len(lines)),
        grid=(columns // block,),
        in_specs=[whole(line.shape) for line in lines] + [field, whole(local_weight.shape)],
        out_specs=[field, whole((channels, channels)), whole((1, channels))],
        out_shape=[
            jax.ShapeDtypeStruct(delta.shape, bf16),
            jax.ShapeDtypeStruct((channels, channels), f32),
            jax.ShapeDtypeStruct((1, channels), f32),
        ],
        scratch_shapes=[pltpu.VMEM((grid_rows, rows), bf16)],
        compiler_params=params(),
        cost_estimate=pl.CostEstimate(
            flops=2 * (rows + channels) * delta.size, bytes_accessed=5 * delta.size, transcendentals=0
        ),
        name="x_inverse_and_local",
    )(*lines, delta, local_weight)


def on_device(field_in, pre_act, cotangent, spec_weight, local_weight):
    batch_size, slab_rows, col_block, channels = field_in.shape
    space_count = lax.axis_size("space")
    data_count = lax.axis_size("dp")
    grid_rows = slab_rows * space_count
    grid_cols = col_block * data_count
    kx_local, ky_local = spec_weight.shape[:2]
    half = data_count // 2
    half_cols = half * col_block
    row_count = 2 * (kx_local + 1)
    data_index = lax.axis_index("dp")
    space_index = lax.axis_index("space")
    upper = data_index // half

    sizes = (half, kx_local, slab_rows, grid_rows)

    blocks = 2 * space_count
    size = 2 * ky_local
    row = jnp.arange(blocks * size, dtype=jnp.int32)
    block, inner = row // size, row % size
    shift = block % space_count
    ky_index = (space_index + shift) % space_count * ky_local + inner // 2
    quarter = grid_cols // 4
    cosine_turn = inner % 2
    sine_turn = jnp.where((block // space_count) == upper, 1 + inner % 2, 3 * (1 - inner % 2))
    turn = jnp.concatenate(
        [
            jnp.broadcast_to(cosine_turn[:, None], (blocks * size, half_cols)),
            jnp.broadcast_to(sine_turn[:, None], (blocks * size, half_cols)),
        ],
        axis=1,
    )

    def y_basis(flip):
        column = jnp.arange(half_cols, dtype=jnp.int32)
        member = (column // col_block) ^ flip
        positions = upper * half_cols + member * col_block + column % col_block
        positions = jnp.concatenate([positions, positions])
        return cosine_table(ky_index[:, None] * positions[None, :] + quarter * turn, grid_cols)

    ky_row = space_index * ky_local + jnp.arange(size, dtype=jnp.int32) // 2
    scale = jnp.where(ky_row == 0, 1.0, 2.0).astype(f32) / (grid_rows * grid_cols)
    scale_rows = jnp.broadcast_to(scale[:, None], (size, channels))

    halves = [list(range(half)), list(range(half, data_count))]

    def exchange(values):
        return lax.all_to_all(
            values, "dp", split_axis=0, concat_axis=0, tiled=True, axis_index_groups=halves
        )

    def to_chips(chips):
        arrived = [chips[0]]
        for pair in range(1, half // 2):
            moves = [(d, d ^ (2 * pair)) for d in range(data_count)]
            arrived.append(lax.ppermute(chips[pair], "dp", moves))
        return arrived

    def between_cores(arrived):
        rows = arrived[0].shape[0] // 2
        mates = jnp.concatenate([part[rows:] for part in arrived], axis=0)
        mates = lax.ppermute(mates, "dp", [(d, d ^ 1) for d in range(data_count)])
        places = [
            (source // 2, 0) if source % 2 == 0 else (half // 2, source // 2 * rows)
            for source in range(half)
        ]
        return arrived + [mates], places

    def pairs(mirror, shift):
        moves = []
        for d in range(data_count):
            for s in range(space_count):
                target = data_count - 1 - d if mirror else d
                moves.append(
                    (d * space_count + s, target * space_count + (s + shift) % space_count)
                )
        return moves

    order = [(mirror, shift) for mirror in (1, 0) for shift in reversed(range(space_count))][:-1]

    def gathered(parts):
        held = [parts[0]]
        for mirror, shift in order:
            held.append(
                lax.ppermute(
                    parts[mirror * space_count + shift], ("dp", "space"), pairs(mirror, shift)
                )
            )
        return held

    tied = lax.optimization_barrier

    share = channels // half
    extra = extra_rows(channels, half)

    message = row_count * col_block
    y_table = y_basis(0)
    relative_table = y_basis(data_index % half)

    arrived = to_chips(input_call(sizes, field_in[0]))
    delta, delta_sums = delta_call(sizes, pre_act[0], cotangent[0], field_in[0])
    delta_sums, arrived = tied((delta_sums, arrived))
    delta_lines = exchange(delta_sums)
    lines, places = between_cores(arrived)
    input_parts = list(
        y_transform_call(
            relative_table, lines, places, message, blocks, space_count, col_block, 0
        )
    )
    for shift in range(1, space_count):
        input_parts[shift] = lax.ppermute(input_parts[shift], ("dp", "space"), pairs(0, shift))
    held_rows = kx_local * size
    mirrored = sum(part[held_rows:].astype(f32) for part in input_parts).astype(bf16)
    delta_lines, mirrored = tied((delta_lines, mirrored))

    message += extra
    delta_parts = y_transform_call(
        y_table,
        [delta_lines.reshape(half * message, channels)],
        [(0, source * message) for source in range(half)],
        message,
        blocks,
        blocks,
        col_block,
        extra,
    )
    delta_parts = list(delta_parts)
    rows = delta_parts[space_count].shape[0]
    delta_parts[space_count] = jnp.concatenate([delta_parts[space_count], mirrored], axis=0)
    weight, delta_parts = tied((spec_weight, delta_parts))
    weight = load_call(weight)
    delta_held = gathered(delta_parts)
    place = 1 + order.index((1, 0))
    input_held = [(part, 0) for part in input_parts] + [(delta_held[place][rows:], 0)]
    delta_held[place] = delta_held[place][:rows]
    back, delta_owned, share_rows = back_call(scale_rows, weight, delta_held, share)
    received = {(0, 0): back}
    for mirror, shift in order:
        received[(mirror, -shift % space_count)] = lax.ppermute(
            back, ("dp", "space"), pairs(mirror, shift)
        )
    modes = [received[(mirror, shift)] for mirror in (0, 1) for shift in range(space_count)]
    column_sums = y_inverse_call(relative_table, share_rows, modes, half, col_block)
    column_sums, delta_owned = tied((column_sums, delta_owned))
    columns = to_chips(column_sums)
    grad_spectral = outer_call(scale_rows, delta_owned, input_held)
    columns, grad_spectral = tied((columns, grad_spectral))
    lines, places = between_cores(columns)
    grad_input, grad_local, bias_rows = final_call(sizes, lines, places, delta, local_weight)
    return (grad_input[None], grad_spectral, grad_local, bias_rows.reshape(channels))


def solution(mesh):
    placed = (
        P(None, "space", "dp", None),
        P(None, "space", "dp", None),
        P(None, "space", "dp", None),
        P("dp", "space", None, None, None),
        P(),
    )
    return jax.shard_map(
        on_device,
        mesh=mesh,
        in_specs=placed,
        out_specs=(P(None, "space", "dp", None), P("dp", "space", None, None, None), P(), P()),
        check_vma=False,
    )
```

```python
import functools
import math

import jax
import jax.numpy as jnp
from jax import lax
from jax.experimental import pallas as pl
from jax.experimental.pallas import tpu as pltpu
from jax.sharding import PartitionSpec as P

root_two_pi = 0.7978845608028654
cubic_coef = 0.044715
f32 = jnp.float32
bf16 = jnp.bfloat16
mebi = 1024 * 1024


def gelu_slope(values):
    square = values * values
    cubic = root_two_pi * cubic_coef
    tangent = jnp.tanh(values * (root_two_pi + cubic * square))
    inner = values * (1.0 - tangent * tangent)
    return 0.5 * ((1.0 + tangent) + inner * (root_two_pi + (3.0 * cubic) * square))


def cosine_table(phases, period):
    quarter = period // 4
    if period & (period - 1) == 0:
        turns = (phases + quarter // 2) >> (quarter.bit_length() - 1)
    else:
        turns = (phases + quarter // 2) // quarter
    angle = (phases - turns * quarter).astype(f32) * (2.0 * math.pi / period)
    square = angle * angle
    cosine = 1.0 + square * (
        -0.5 + square * (1.0 / 24.0 + square * (-1.0 / 720.0 + square * (1.0 / 40320.0)))
    )
    sine = angle * (
        1.0
        + square
        * (-1.0 / 6.0 + square * (1.0 / 120.0 + square * (-1.0 / 5040.0 + square * (1.0 / 362880.0))))
    )
    turns = turns & 3
    magnitude = jnp.where((turns & 1) == 0, cosine, sine)
    return jnp.where((turns == 1) | (turns == 2), -magnitude, magnitude).astype(bf16)


def x_table(sizes, transposed=False, relative=False):
    half, kx_local, slab_rows, grid_rows = sizes
    row_count = 2 * (kx_local + 1)
    upper = (lax.axis_index("dp") >= half).astype(jnp.int32)
    shape = (half * row_count, slab_rows)
    if transposed:
        shape = shape[::-1]
    row = lax.broadcasted_iota(jnp.int32, shape, 1 if transposed else 0)
    position = lax.axis_index("space") * slab_rows + lax.broadcasted_iota(
        jnp.int32, shape, 0 if transposed else 1
    )
    member = sum((row >= i * row_count).astype(jnp.int32) for i in range(1, half))
    inner = row - member * row_count
    if relative:
        member = member ^ (lax.axis_index("dp") & (half - 1))
    ascending = member * kx_local + (inner >> 1)
    frequency = ascending + upper * (half * kx_local - 2 * ascending)
    quarter = grid_rows // 4
    return cosine_table(frequency * position - (inner & 1) * quarter, grid_rows)


def params(mebibytes=16):
    return pltpu.CompilerParams(vmem_limit_bytes=mebibytes * mebi)


def whole(shape):
    return pl.BlockSpec(shape, lambda *_: (0,) * len(shape))


def matrix_per_column(table, columns_of, rows=()):
    channels = columns_of[0].shape[1]
    results = []
    totals = [0.0] * len(rows)
    for y in range(0, len(columns_of), 2):
        pair = jnp.concatenate(columns_of[y : y + 2], axis=1)
        sums = jnp.dot(table, pair, preferred_element_type=f32)
        totals = [total + sums[row : row + 1] for total, row in zip(totals, rows)]
        sums = sums.astype(bf16)
        results += [sums[:, :channels], sums[:, channels:]]
    results = jnp.swapaxes(jnp.stack(results, axis=0), 0, 1)
    if rows:
        return results, [total[:, :channels] + total[:, channels:] for total in totals]
    return results


def two_terms(values):
    high = values.astype(bf16)
    return high, (values - high.astype(f32)).astype(bf16)


def extra_rows(channels, half):
    return -(-2 * (channels // half) // 16) * 16


def packed_rows(channels, half):
    return -(-(2 * (channels // half) + 2) // 16) * 16


def stacked(parts, rows):
    parts = list(parts)
    filled = sum(part.shape[0] for part in parts)
    if rows > filled:
        parts.append(jnp.zeros((rows - filled, parts[0].shape[1]), bf16))
    return jnp.concatenate([part.astype(f32) for part in parts], axis=0).astype(bf16)


def pack_share(share, bias):
    rows, channels = share.shape
    return stacked(two_terms(share) + two_terms(bias), packed_rows(channels, channels // rows))


def unpack_terms(rows, message):
    message = message.astype(f32)
    return message[:rows] + message[rows : 2 * rows]


def unpack_share(rows, message):
    return unpack_terms(rows, message), unpack_terms(1, message[2 * rows : 2 * rows + 2])


def bias_places(half, rows):
    return (0, 1), (half - 1, rows - 1)


def in_relative_order(pieces, half):
    place = lax.axis_index("dp")
    key = jnp.where(place >= half, 2 * half - 1 - place, place)
    step = 1
    while step < half:
        flag = (key & step) != 0
        pieces = [jnp.where(flag, pieces[i ^ step], pieces[i]) for i in range(half)]
        step *= 2
    return pieces


def delta_kernel(
    sizes,
    pre_ref,
    cot_ref,
    field_ref,
    delta_ref,
    out_ref,
    lines,
    local,
    bias,
    table,
    field,
    semaphores,
):
    grid_rows, columns, channels = pre_ref.shape
    half = out_ref.shape[0]
    block = pl.program_id(0)
    all_columns = columns * pl.num_programs(0)
    step = 16
    blocks = field.shape[0]

    def arriving(i):
        return pltpu.make_async_copy(
            field_ref.at[:, pl.ds(i * columns, columns)], field.at[i], semaphores.at[i]
        )

    @pl.when(block == 0)
    def _():
        for i in range(blocks):
            arriving(i).start()
        local[...] = jnp.zeros_like(local)
        bias[...] = jnp.zeros_like(bias)
        table[...] = x_table(sizes)

    def slab(i, carry):
        rows = pl.ds(pl.multiple_of(i * step, step), step)
        slope = gelu_slope(pre_ref[rows].astype(f32))
        delta = (cot_ref[rows].astype(f32) * slope).astype(bf16)
        delta_ref[rows] = delta
        lines[:, rows, :] = jnp.swapaxes(delta, 0, 1)
        return carry

    lax.fori_loop(0, grid_rows // step, slab, 0)
    sums, totals = matrix_per_column(
        table[...], [lines[y] for y in range(columns)], (0, table.shape[0] - 2)
    )
    upper = lax.axis_index("dp") >= half
    bias[...] += jnp.where(upper, totals[1], totals[0])
    for i in range(blocks):

        @pl.when(block == i)
        def _(i=i):
            arriving(i).wait()

    local[...] += lax.dot_general(
        field[block].reshape(grid_rows * columns, channels),
        delta_ref[...].reshape(grid_rows * columns, channels),
        (((0,), (0,)), ((), ())),
        preferred_element_type=f32,
    )
    per_target = sums.shape[0] // half
    first = pl.multiple_of(block * columns, columns)
    for target in range(half):
        for row in range(per_target):
            out_ref[target, pl.ds(row * all_columns + first, columns), :] = sums[
                target * per_target + row
            ]

    @pl.when(block == pl.num_programs(0) - 1)
    def _():
        share = channels // half
        for target in range(half):
            mine = local[target * share : (target + 1) * share]
            mirrored = local[(half - 1 - target) * share : (half - target) * share]
            rows = two_terms(jnp.where(upper, mirrored, mine))
            out_ref[target, per_target * all_columns :] = stacked(
                rows, out_ref.shape[1] - per_target * all_columns
            )
        terms = stacked(two_terms(bias[...]), columns).astype(f32)
        for in_upper, (member, row) in enumerate(bias_places(half, per_target)):
            here = slice(row * all_columns, row * all_columns + columns)
            old = out_ref[member, here].astype(f32)
            ours = upper if in_upper else jnp.logical_not(upper)
            out_ref[member, here] = jnp.where(ours, terms, old).astype(bf16)


def delta_call(sizes, pre_act, cotangent, field_in):
    grid_rows, columns, channels = pre_act.shape
    half = sizes[0]
    rows = 2 * half * (sizes[1] + 1)
    block = min(16, columns)
    field = pl.BlockSpec((grid_rows, block, channels), lambda i: (0, i, 0))
    message = (half, rows // half * columns + extra_rows(channels, half), channels)
    return pl.pallas_call(
        functools.partial(delta_kernel, sizes),
        grid=(columns // block,),
        in_specs=[field, field, pl.BlockSpec(memory_space=pl.ANY)],
        out_specs=[field, whole(message)],
        out_shape=[
            jax.ShapeDtypeStruct(pre_act.shape, bf16),
            jax.ShapeDtypeStruct(message, bf16),
        ],
        scratch_shapes=[
            pltpu.VMEM((block, grid_rows, channels), bf16),
            pltpu.VMEM((channels, channels), f32),
            pltpu.VMEM((1, channels), f32),
            pltpu.VMEM((rows, grid_rows), bf16),
            pltpu.VMEM((columns // block, grid_rows, block, channels), bf16),
            pltpu.SemaphoreType.DMA((columns // block,)),
        ],
        compiler_params=params(60),
        cost_estimate=pl.CostEstimate(
            flops=4 * rows * pre_act.size, bytes_accessed=8 * pre_act.size, transcendentals=pre_act.size
        ),
        name="delta_and_x_sums",
    )(pre_act, cotangent, field_in)


def input_kernel(sizes, pieces, *refs):
    field_refs, out_refs, table = refs[:pieces], refs[pieces:-1], refs[-1]
    columns, channels = field_refs[0].shape[1:]
    block = pl.program_id(0)
    all_columns = columns * pl.num_programs(0)

    @pl.when(block == 0)
    def _():
        table[...] = x_table(sizes, relative=True)

    lines = [jnp.swapaxes(ref[...], 0, 1) for ref in field_refs]
    sums = matrix_per_column(
        table[...],
        [jnp.concatenate([part[y] for part in lines], axis=0) for y in range(columns)],
    )
    first = pl.multiple_of(block * columns, columns)
    rows = sums.shape[0] // len(out_refs)
    for pair, out_ref in enumerate(out_refs):
        for row in range(rows):
            out_ref[pl.ds(row * all_columns + first, columns), :] = sums[pair * rows + row]


def input_call(sizes, field_in):
    grid_rows, columns, channels = field_in.shape
    half = sizes[0]
    rows = 2 * half * (sizes[1] + 1)
    block = min(16, columns)
    pieces = 4
    message = (2 * rows // half * columns, channels)
    return pl.pallas_call(
        functools.partial(input_kernel, sizes, pieces),
        grid=(columns // block,),
        in_specs=[
            pl.BlockSpec(
                (grid_rows // pieces, block, channels), lambda i, piece=piece: (piece, i, 0)
            )
            for piece in range(pieces)
        ],
        out_specs=[whole(message)] * (half // 2),
        out_shape=[jax.ShapeDtypeStruct(message, bf16)] * (half // 2),
        scratch_shapes=[pltpu.VMEM((rows, grid_rows), bf16)],
        compiler_params=params(60),
        cost_estimate=pl.CostEstimate(
            flops=2 * rows * field_in.size, bytes_accessed=4 * field_in.size, transcendentals=0
        ),
        name="input_x_sums",
    )(*[field_in] * pieces)


def y_transform_kernel(columns, extra, blocks, total_rows, places, arrays, table_ref, *refs):
    line_refs, out_refs = refs[:arrays], refs[arrays:]
    sources, channels = len(places), line_refs[0].shape[-1]

    def rows_of(source, first, last):
        array, at = places[source]
        return line_refs[array][at + first : at + last]

    frequencies = (total_rows - extra) // columns // 2
    own = blocks // 2
    size = table_ref.shape[0] // blocks
    table = table_ref[...]
    place = lax.axis_index("dp")
    for t in range(frequencies):
        pieces = [
            rows_of(source, row * columns, (row + 1) * columns)
            for row in (2 * t, 2 * t + 1)
            for source in range(sources)
        ]
        for in_upper, (member, row) in enumerate(bias_places(sources, 2 * frequencies)):
            if extra and row == 2 * t + 1:
                keep = jnp.where(place == in_upper * (2 * sources - 1), 0.0, 1.0).astype(f32)
                pieces[sources:] = [
                    (piece.astype(f32) * keep).astype(bf16) for piece in pieces[sources:]
                ]
        lines = jnp.concatenate(pieces, axis=0)
        sums = jnp.dot(table, lines, preferred_element_type=f32).astype(bf16)
        for block in range(blocks):
            held = t if block < own else frequencies - 1 - t
            if 0 <= held < frequencies - 1:
                first = (block // len(out_refs)) * (frequencies - 1) + held
                out_refs[block % len(out_refs)][first * size : (first + 1) * size] = sums[
                    block * size : (block + 1) * size
                ]
    if extra:
        share = channels // sources
        shares = [
            unpack_terms(share, rows_of(i, total_rows - extra, total_rows)) for i in range(sources)
        ]
        bias = 0.0
        for in_upper, (member, row) in enumerate(bias_places(sources, 2 * frequencies)):
            first = row * columns
            total = sum(
                unpack_terms(1, rows_of(i, first, first + min(16, columns))) for i in range(sources)
            )
            bias = bias + jnp.where(place == in_upper * (2 * sources - 1), total, 0.0)
        packed = pack_share(sum(shares), bias)
        for out_ref in out_refs:
            out_ref[out_ref.shape[0] - packed.shape[0] :] = packed


def y_transform_call(table, lines, places, total_rows, blocks, outputs, columns, extra):
    channels = lines[0].shape[-1]
    held = (total_rows - extra) // columns // 2 - 1
    size = table.shape[0] // blocks
    rows = blocks // outputs * held * size
    if extra:
        rows += packed_rows(channels, len(places))
    return pl.pallas_call(
        functools.partial(
            y_transform_kernel, columns, extra, blocks, total_rows, places, len(lines)
        ),
        out_shape=[jax.ShapeDtypeStruct((rows, channels), bf16)] * outputs,
        compiler_params=params(),
        cost_estimate=pl.CostEstimate(
            flops=2 * (held + 1) * table.size * channels,
            bytes_accessed=4 * len(places) * total_rows * channels,
            transcendentals=0,
        ),
        name="y_sums",
    )(table, *lines)


def turned(values):
    rows = values.shape[0]
    even = lax.broadcasted_iota(jnp.int32, values.shape, 0) % 2 == 0
    up = pltpu.roll(values, rows - 1, 0)
    down = pltpu.roll(values, 1, 0)
    return jnp.concatenate([values, jnp.where(even, up, -down)], axis=1)


def load_kernel(source_ref, target_ref, semaphores):
    held, modes = source_ref.shape[:2]
    pieces = semaphores.shape[1]
    rows = modes // pieces
    copies = [
        [
            pltpu.make_async_copy(
                source_ref.at[j, pl.ds(k * rows, rows)],
                target_ref.at[j, pl.ds(k * rows, rows)],
                semaphores.at[j, k],
            )
            for k in range(pieces)
        ]
        for j in range(held)
    ]
    for copy in sum(copies, []):
        copy.start()
    for j in range(held):
        for copy in copies[j]:
            copy.wait()
        if j >= turned_count(held):
            continue

        def turn(mode, carry, j=j):
            for part in range(2):
                target_ref[j, mode, part] = target_ref[j, mode, part].T
            return carry

        lax.fori_loop(0, modes, turn, 0, unroll=4)


def turned_count(held):
    return held // 2


def load_call(weight):
    held = weight.shape[0]
    return pl.pallas_call(
        load_kernel,
        in_specs=[pl.BlockSpec(memory_space=pl.ANY)],
        out_specs=pl.BlockSpec(memory_space=pltpu.VMEM),
        out_shape=pltpu.VMEM(weight.shape, bf16),
        scratch_shapes=[pltpu.SemaphoreType.DMA((held, 2))],
        compiler_params=params(50),
        cost_estimate=pl.CostEstimate(flops=0, bytes_accessed=4 * weight.size, transcendentals=0),
        name="weights_to_vmem",
    )(weight)


def back_kernel(share, scale_ref, weight_ref, *refs):
    part_refs, (back_ref, delta_ref, share_ref) = refs[:-3], refs[-3:]
    held, rows, channels = delta_ref.shape
    block = weight_ref.shape[1]
    j, k = pl.program_id(0), pl.program_id(1)
    first = pl.multiple_of((j * (rows // (2 * block)) + k) * 2 * block, 2 * block)
    here = pl.ds(first, 2 * block)
    inner = pl.ds(pl.multiple_of(k * 2 * block, 2 * block), 2 * block)
    total = part_refs[0][here].astype(f32)
    for ref in part_refs[1:]:
        total = total + ref[here].astype(f32)
    delta = total.astype(bf16)
    delta_ref[j, inner] = delta
    both = turned(delta.astype(f32)).astype(bf16)

    def products(is_turned):
        sums = []
        for mode in range(block):
            weight = jnp.concatenate(
                [weight_ref[0, mode, 0], weight_ref[0, mode, 1]], axis=0 if is_turned else 1
            )
            sums.append(
                lax.dot_general(
                    both[2 * mode : 2 * mode + 2],
                    weight,
                    (((1,), (0 if is_turned else 1,)), ((), ())),
                    preferred_element_type=f32,
                )
            )
        back_ref[j, inner] = (jnp.concatenate(sums, axis=0) * scale_ref[inner]).astype(bf16)

    pl.when(j < turned_count(held))(lambda: products(True))
    pl.when(j >= turned_count(held))(lambda: products(False))

    @pl.when((j == 0) & (k == 0))
    def _():
        extra = share_ref.shape[0]
        pieces = [unpack_share(share, ref[ref.shape[0] - extra :]) for ref in part_refs]
        share_ref[...] = pack_share(sum(p[0] for p in pieces), sum(p[1] for p in pieces))


def back_call(scale_rows, weight, parts, share):
    held, modes, _, channels, _ = weight.shape
    block = min(16, modes)
    shape = (held, 2 * modes, channels)
    extra = (parts[0].shape[0] - held * 2 * modes, channels)
    return pl.pallas_call(
        functools.partial(back_kernel, share),
        grid=(held, modes // block),
        in_specs=[
            whole(scale_rows.shape),
            pl.BlockSpec((1, block, 2, channels, channels), lambda j, k: (j, k, 0, 0, 0)),
        ]
        + [whole(part.shape) for part in parts],
        out_specs=[whole(shape), whole(shape), whole(extra)],
        out_shape=[
            jax.ShapeDtypeStruct(shape, bf16),
            jax.ShapeDtypeStruct(shape, bf16),
            jax.ShapeDtypeStruct(extra, bf16),
        ],
        compiler_params=params(),
        cost_estimate=pl.CostEstimate(
            flops=4 * weight.size, bytes_accessed=2 * weight.size, transcendentals=0
        ),
        name="mode_back",
    )(scale_rows, weight, *parts)


def outer_kernel(scale_ref, delta_ref, *refs):
    part_refs, out_ref = refs[:-1], refs[-1]
    modes = out_ref.shape[1]
    channels = out_ref.shape[-1]
    total = part_refs[0][...].astype(f32)
    for ref in part_refs[1:]:
        total = total + ref[...].astype(f32)
    field = (total.astype(bf16).astype(f32) * scale_ref[...]).astype(bf16).astype(f32)
    delta = turned(delta_ref[0].astype(f32))
    group = 4
    mode_of_row = lax.broadcasted_iota(jnp.int32, (2 * group, 2 * channels), 0) // 2
    for first in range(0, modes, group):
        rows = slice(2 * first, 2 * (first + group))
        alone = [jnp.where(mode_of_row == i, delta[rows], 0.0) for i in range(group)]
        product = lax.dot_general(
            field[rows].astype(bf16),
            jnp.concatenate(alone, axis=1).astype(bf16),
            (((0,), (0,)), ((), ())),
            preferred_element_type=f32,
        ).astype(bf16)
        for i in range(2 * group):
            out_ref[0, first + i // 2, i % 2] = product[:, i * channels : (i + 1) * channels]


def outer_call(scale_rows, delta, parts):
    held, rows, channels = delta.shape
    modes = rows // 2
    part = pl.BlockSpec((1, rows, channels), lambda j: (j, 0, 0))
    return pl.pallas_call(
        outer_kernel,
        grid=(held,),
        in_specs=[whole((rows, channels)), part]
        + [
            pl.BlockSpec((rows, channels), lambda j, first=first: (j + first, 0))
            for _, first in parts
        ],
        out_specs=pl.BlockSpec((1, modes, 2, channels, channels), lambda j: (j, 0, 0, 0, 0)),
        out_shape=jax.ShapeDtypeStruct((held, modes, 2, channels, channels), bf16),
        compiler_params=params(),
        cost_estimate=pl.CostEstimate(
            flops=6 * held * modes * channels * channels,
            bytes_accessed=4 * held * modes * channels * channels,
            transcendentals=0,
        ),
        name="grad_spectral",
    )(scale_rows, delta, *[part for part, _ in parts])


def y_inverse_kernel(columns, parts, table_ref, share_ref, *refs):
    part_refs, out_refs = refs[:parts], refs[parts:]
    channels = share_ref.shape[1]
    message = out_refs[0].shape[0] // 2
    targets = 2 * len(out_refs)
    extra = extra_rows(channels, targets)
    frequencies = (message - extra) // columns // 2
    own = parts // 2
    size = part_refs[0].shape[1]
    table = table_ref[...]
    for t in range(frequencies):
        first = 0 if t < frequencies - 1 else own
        last = 2 * own if t > 0 else own
        modes = jnp.concatenate(
            [
                part_refs[block][t if block < own else frequencies - 1 - t]
                for block in range(first, last)
            ],
            axis=0,
        )
        sums = lax.dot_general(
            table[first * size : last * size],
            modes,
            (((0,), (0,)), ((), ())),
            preferred_element_type=f32,
        ).astype(bf16)
        for part in range(2):
            for target in range(targets):
                at = target % 2 * message + (2 * t + part) * columns
                piece = part * targets + target
                out_refs[target // 2][at : at + columns] = sums[
                    piece * columns : (piece + 1) * columns
                ]
    for target in range(targets):
        last = (target % 2 + 1) * message
        out_refs[target // 2][last - extra : last] = share_ref[:extra]
    place = lax.axis_index("dp")
    height = min(16, columns)
    share = channels // targets
    terms = share_ref[2 * share : 2 * share + height].astype(f32)
    for in_upper, (member, row) in enumerate(bias_places(targets, 2 * frequencies)):
        ours = place == in_upper * (2 * targets - 1)
        for target in range(targets):
            first = target % 2 * message + row * columns
            old = out_refs[target // 2][first : first + height].astype(f32)
            out_refs[target // 2][first : first + height] = jnp.where(ours, terms, old).astype(bf16)


def y_inverse_call(table, share, parts, targets, columns):
    held, size, channels = parts[0].shape
    rows = 2 * (held + 1)
    message = (2 * (rows * columns + extra_rows(channels, targets)), channels)
    return pl.pallas_call(
        functools.partial(y_inverse_kernel, columns, len(parts)),
        out_shape=[jax.ShapeDtypeStruct(message, bf16)] * (targets // 2),
        compiler_params=params(),
        cost_estimate=pl.CostEstimate(
            flops=rows * table.size * channels,
            bytes_accessed=4 * targets * rows * columns * channels,
            transcendentals=0,
        ),
        name="y_inverse",
    )(table, share, *parts)


def final_kernel(sizes, places, arrays, *refs):
    line_refs, refs = refs[:arrays], refs[arrays:]
    delta_ref, weight_ref, out_ref, local_ref, bias_ref, table = refs
    grid_rows, columns, channels = out_ref.shape
    half = len(places)
    block = pl.program_id(0)
    all_columns = columns * pl.num_programs(0)
    per_source = table.shape[1] // half
    first = pl.multiple_of(block * columns, columns)

    @pl.when(block == 0)
    def _():
        table[...] = x_table(sizes, transposed=True, relative=True)

    lines = jnp.stack(
        [
            line_refs[array][pl.ds(at + row * all_columns + first, columns), :]
            for array, at in places
            for row in range(per_source)
        ],
        axis=0,
    )
    lines = jnp.swapaxes(lines, 0, 1)
    spectral = matrix_per_column(table[...], [lines[y] for y in range(columns)])
    local = lax.dot_general(
        delta_ref[...].reshape(grid_rows * columns, channels),
        weight_ref[...],
        (((1,), (1,)), ((), ())),
        preferred_element_type=f32,
    ).reshape(grid_rows, columns, channels)
    out_ref[...] = (spectral.astype(f32) + local).astype(bf16)

    @pl.when(block == 0)
    def _():
        share = channels // half
        extra = extra_rows(channels, half)
        upper = lax.axis_index("dp") >= half
        rows_low, rows_high = (row for _, row in bias_places(half, per_source))
        shares, biases = [], []
        for array, at in places:
            begin = at + per_source * all_columns
            shares.append(unpack_terms(share, line_refs[array][begin : begin + extra]))
            low, high = (
                unpack_terms(1, line_refs[array][at + row * all_columns : at + row * all_columns + columns])
                for row in (rows_low, rows_high)
            )
            biases.append(jnp.where(upper, high, low))
        for source, rows in enumerate(in_relative_order(shares, half)):
            local_ref[source * share : (source + 1) * share] = rows
        bias_ref[...] = in_relative_order(biases, half)[0]


def final_call(sizes, lines, places, delta, local_weight):
    grid_rows, columns, channels = delta.shape
    rows = 2 * sizes[0] * (sizes[1] + 1)
    block = min(16, columns)
    field = pl.BlockSpec((grid_rows, block, channels), lambda i: (0, i, 0))
    return pl.pallas_call(
        functools.partial(final_kernel, sizes, places, len(lines)),
        grid=(columns // block,),
        in_specs=[whole(line.shape) for line in lines] + [field, whole(local_weight.shape)],
        out_specs=[field, whole((channels, channels)), whole((1, channels))],
        out_shape=[
            jax.ShapeDtypeStruct(delta.shape, bf16),
            jax.ShapeDtypeStruct((channels, channels), f32),
            jax.ShapeDtypeStruct((1, channels), f32),
        ],
        scratch_shapes=[pltpu.VMEM((grid_rows, rows), bf16)],
        compiler_params=params(),
        cost_estimate=pl.CostEstimate(
            flops=2 * (rows + channels) * delta.size, bytes_accessed=5 * delta.size, transcendentals=0
        ),
        name="x_inverse_and_local",
    )(*lines, delta, local_weight)


def on_device(field_in, pre_act, cotangent, spec_weight, local_weight):
    batch_size, slab_rows, col_block, channels = field_in.shape
    space_count = lax.axis_size("space")
    data_count = lax.axis_size("dp")
    grid_rows = slab_rows * space_count
    grid_cols = col_block * data_count
    kx_local, ky_local = spec_weight.shape[:2]
    half = data_count // 2
    half_cols = half * col_block
    row_count = 2 * (kx_local + 1)
    data_index = lax.axis_index("dp")
    space_index = lax.axis_index("space")
    upper = data_index // half

    sizes = (half, kx_local, slab_rows, grid_rows)

    blocks = 2 * space_count
    size = 2 * ky_local
    row = jnp.arange(blocks * size, dtype=jnp.int32)
    block, inner = row // size, row % size
    shift = block % space_count
    ky_index = (space_index + shift) % space_count * ky_local + inner // 2
    quarter = grid_cols // 4
    cosine_turn = inner % 2
    sine_turn = jnp.where((block // space_count) == upper, 1 + inner % 2, 3 * (1 - inner % 2))
    turn = jnp.concatenate(
        [
            jnp.broadcast_to(cosine_turn[:, None], (blocks * size, half_cols)),
            jnp.broadcast_to(sine_turn[:, None], (blocks * size, half_cols)),
        ],
        axis=1,
    )

    def y_basis(flip):
        column = jnp.arange(half_cols, dtype=jnp.int32)
        member = (column // col_block) ^ flip
        positions = upper * half_cols + member * col_block + column % col_block
        positions = jnp.concatenate([positions, positions])
        return cosine_table(ky_index[:, None] * positions[None, :] + quarter * turn, grid_cols)

    ky_row = space_index * ky_local + jnp.arange(size, dtype=jnp.int32) // 2
    scale = jnp.where(ky_row == 0, 1.0, 2.0).astype(f32) / (grid_rows * grid_cols)
    scale_rows = jnp.broadcast_to(scale[:, None], (size, channels))

    halves = [list(range(half)), list(range(half, data_count))]

    def exchange(values):
        return lax.all_to_all(
            values, "dp", split_axis=0, concat_axis=0, tiled=True, axis_index_groups=halves
        )

    def to_chips(chips):
        arrived = [chips[0]]
        for pair in range(1, half // 2):
            moves = [(d, d ^ (2 * pair)) for d in range(data_count)]
            arrived.append(lax.ppermute(chips[pair], "dp", moves))
        return arrived

    def between_cores(arrived):
        rows = arrived[0].shape[0] // 2
        mates = jnp.concatenate([part[rows:] for part in arrived], axis=0)
        mates = lax.ppermute(mates, "dp", [(d, d ^ 1) for d in range(data_count)])
        places = [
            (source // 2, 0) if source % 2 == 0 else (half // 2, source // 2 * rows)
            for source in range(half)
        ]
        return arrived + [mates], places

    def pairs(mirror, shift):
        moves = []
        for d in range(data_count):
            for s in range(space_count):
                target = data_count - 1 - d if mirror else d
                moves.append(
                    (d * space_count + s, target * space_count + (s + shift) % space_count)
                )
        return moves

    order = [(mirror, shift) for mirror in (1, 0) for shift in reversed(range(space_count))][:-1]

    def gathered(parts):
        held = [parts[0]]
        for mirror, shift in order:
            held.append(
                lax.ppermute(
                    parts[mirror * space_count + shift], ("dp", "space"), pairs(mirror, shift)
                )
            )
        return held

    tied = lax.optimization_barrier

    share = channels // half
    extra = extra_rows(channels, half)

    message = row_count * col_block
    y_table = y_basis(0)
    relative_table = y_basis(data_index % half)

    arrived = to_chips(input_call(sizes, field_in[0]))
    delta, delta_sums = delta_call(sizes, pre_act[0], cotangent[0], field_in[0])
    delta_sums, arrived = tied((delta_sums, arrived))
    delta_lines = exchange(delta_sums)
    lines, places = between_cores(arrived)
    input_parts = list(
        y_transform_call(
            relative_table, lines, places, message, blocks, space_count, col_block, 0
        )
    )
    for shift in range(1, space_count):
        input_parts[shift] = lax.ppermute(input_parts[shift], ("dp", "space"), pairs(0, shift))
    held_rows = kx_local * size
    mirrored = sum(part[held_rows:].astype(f32) for part in input_parts).astype(bf16)
    delta_lines, mirrored = tied((delta_lines, mirrored))

    message += extra
    delta_parts = y_transform_call(
        y_table,
        [delta_lines.reshape(half * message, channels)],
        [(0, source * message) for source in range(half)],
        message,
        blocks,
        blocks,
        col_block,
        extra,
    )
    delta_parts = list(delta_parts)
    rows = delta_parts[space_count].shape[0]
    delta_parts[space_count] = jnp.concatenate([delta_parts[space_count], mirrored], axis=0)
    weight, delta_parts = tied((spec_weight, delta_parts))
    weight = load_call(weight)
    delta_held = gathered(delta_parts)
    place = 1 + order.index((1, 0))
    input_held = [(part, 0) for part in input_parts] + [(delta_held[place][rows:], 0)]
    delta_held[place] = delta_held[place][:rows]
    back, delta_owned, share_rows = back_call(scale_rows, weight, delta_held, share)
    received = {(0, 0): back}
    for mirror, shift in order:
        received[(mirror, -shift % space_count)] = lax.ppermute(
            back, ("dp", "space"), pairs(mirror, shift)
        )
    modes = [received[(mirror, shift)] for mirror in (0, 1) for shift in range(space_count)]
    column_sums = y_inverse_call(relative_table, share_rows, modes, half, col_block)
    column_sums, delta_owned = tied((column_sums, delta_owned))
    columns = to_chips(column_sums)
    grad_spectral = outer_call(scale_rows, delta_owned, input_held)
    columns, grad_spectral = tied((columns, grad_spectral))
    lines, places = between_cores(columns)
    grad_input, grad_local, bias_rows = final_call(sizes, lines, places, delta, local_weight)
    return (grad_input[None], grad_spectral, grad_local, bias_rows.reshape(channels))


def solution(mesh):
    placed = (
        P(None, "space", "dp", None),
        P(None, "space", "dp", None),
        P(None, "space", "dp", None),
        P("dp", "space", None, None, None),
        P(),
    )
    return jax.shard_map(
        on_device,
        mesh=mesh,
        in_specs=placed,
        out_specs=(P(None, "space", "dp", None), P("dp", "space", None, None, None), P(), P()),
        check_vma=False,
    )
```

```python
import functools
import math

import jax
import jax.numpy as jnp
from jax import lax
from jax.experimental import pallas as pl
from jax.experimental.pallas import tpu as pltpu
from jax.sharding import PartitionSpec as P

root_two_pi = 0.7978845608028654
cubic_coef = 0.044715
f32 = jnp.float32
bf16 = jnp.bfloat16
mebi = 1024 * 1024


def gelu_slope(values):
    square = values * values
    cubic = root_two_pi * cubic_coef
    tangent = jnp.tanh(values * (root_two_pi + cubic * square))
    inner = values * (1.0 - tangent * tangent)
    return 0.5 * ((1.0 + tangent) + inner * (root_two_pi + (3.0 * cubic) * square))


def cosine_table(phases, period):
    quarter = period // 4
    if period & (period - 1) == 0:
        turns = (phases + quarter // 2) >> (quarter.bit_length() - 1)
    else:
        turns = (phases + quarter // 2) // quarter
    angle = (phases - turns * quarter).astype(f32) * (2.0 * math.pi / period)
    square = angle * angle
    cosine = 1.0 + square * (
        -0.5 + square * (1.0 / 24.0 + square * (-1.0 / 720.0 + square * (1.0 / 40320.0)))
    )
    sine = angle * (
        1.0
        + square
        * (-1.0 / 6.0 + square * (1.0 / 120.0 + square * (-1.0 / 5040.0 + square * (1.0 / 362880.0))))
    )
    turns = turns & 3
    magnitude = jnp.where((turns & 1) == 0, cosine, sine)
    return jnp.where((turns == 1) | (turns == 2), -magnitude, magnitude).astype(bf16)


def x_table(sizes, transposed=False, relative=False):
    half, kx_local, slab_rows, grid_rows = sizes
    row_count = 2 * (kx_local + 1)
    upper = (lax.axis_index("dp") >= half).astype(jnp.int32)
    shape = (half * row_count, slab_rows)
    if transposed:
        shape = shape[::-1]
    row = lax.broadcasted_iota(jnp.int32, shape, 1 if transposed else 0)
    position = lax.axis_index("space") * slab_rows + lax.broadcasted_iota(
        jnp.int32, shape, 0 if transposed else 1
    )
    member = sum((row >= i * row_count).astype(jnp.int32) for i in range(1, half))
    inner = row - member * row_count
    if relative:
        member = member ^ (lax.axis_index("dp") & (half - 1))
    ascending = member * kx_local + (inner >> 1)
    frequency = ascending + upper * (half * kx_local - 2 * ascending)
    quarter = grid_rows // 4
    return cosine_table(frequency * position - (inner & 1) * quarter, grid_rows)


def params(mebibytes=16):
    return pltpu.CompilerParams(vmem_limit_bytes=mebibytes * mebi)


def whole(shape):
    return pl.BlockSpec(shape, lambda *_: (0,) * len(shape))


def matrix_per_column(table, columns_of, rows=()):
    channels = columns_of[0].shape[1]
    results = []
    totals = [0.0] * len(rows)
    for y in range(0, len(columns_of), 2):
        pair = jnp.concatenate(columns_of[y : y + 2], axis=1)
        sums = jnp.dot(table, pair, preferred_element_type=f32)
        totals = [total + sums[row : row + 1] for total, row in zip(totals, rows)]
        sums = sums.astype(bf16)
        results += [sums[:, :channels], sums[:, channels:]]
    results = jnp.swapaxes(jnp.stack(results, axis=0), 0, 1)
    if rows:
        return results, [total[:, :channels] + total[:, channels:] for total in totals]
    return results


def two_terms(values):
    high = values.astype(bf16)
    return high, (values - high.astype(f32)).astype(bf16)


def extra_rows(channels, half):
    return -(-2 * (channels // half) // 16) * 16


def packed_rows(channels, half):
    return -(-(2 * (channels // half) + 2) // 16) * 16


def stacked(parts, rows):
    parts = list(parts)
    filled = sum(part.shape[0] for part in parts)
    if rows > filled:
        parts.append(jnp.zeros((rows - filled, parts[0].shape[1]), bf16))
    return jnp.concatenate([part.astype(f32) for part in parts], axis=0).astype(bf16)


def pack_share(share, bias):
    rows, channels = share.shape
    return stacked(two_terms(share) + two_terms(bias), packed_rows(channels, channels // rows))


def unpack_terms(rows, message):
    message = message.astype(f32)
    return message[:rows] + message[rows : 2 * rows]


def unpack_share(rows, message):
    return unpack_terms(rows, message), unpack_terms(1, message[2 * rows : 2 * rows + 2])


def bias_places(half, rows):
    return (0, 1), (half - 1, rows - 1)


def in_relative_order(pieces, half):
    place = lax.axis_index("dp")
    key = jnp.where(place >= half, 2 * half - 1 - place, place)
    step = 1
    while step < half:
        flag = (key & step) != 0
        pieces = [jnp.where(flag, pieces[i ^ step], pieces[i]) for i in range(half)]
        step *= 2
    return pieces


def delta_kernel(
    sizes,
    pre_ref,
    cot_ref,
    field_ref,
    delta_ref,
    out_ref,
    lines,
    local,
    bias,
    table,
    field,
    semaphores,
):
    grid_rows, columns, channels = pre_ref.shape
    half = out_ref.shape[0]
    block = pl.program_id(0)
    all_columns = columns * pl.num_programs(0)
    step = 16
    blocks = field.shape[0]

    def arriving(i):
        return pltpu.make_async_copy(
            field_ref.at[:, pl.ds(i * columns, columns)], field.at[i], semaphores.at[i]
        )

    @pl.when(block == 0)
    def _():
        for i in range(blocks):
            arriving(i).start()
        local[...] = jnp.zeros_like(local)
        bias[...] = jnp.zeros_like(bias)
        table[...] = x_table(sizes)

    def slab(i, carry):
        rows = pl.ds(pl.multiple_of(i * step, step), step)
        slope = gelu_slope(pre_ref[rows].astype(f32))
        delta = (cot_ref[rows].astype(f32) * slope).astype(bf16)
        delta_ref[rows] = delta
        lines[:, rows, :] = jnp.swapaxes(delta, 0, 1)
        return carry

    lax.fori_loop(0, grid_rows // step, slab, 0)
    sums, totals = matrix_per_column(
        table[...], [lines[y] for y in range(columns)], (0, table.shape[0] - 2)
    )
    upper = lax.axis_index("dp") >= half
    bias[...] += jnp.where(upper, totals[1], totals[0])
    for i in range(blocks):

        @pl.when(block == i)
        def _(i=i):
            arriving(i).wait()

    local[...] += lax.dot_general(
        field[block].reshape(grid_rows * columns, channels),
        delta_ref[...].reshape(grid_rows * columns, channels),
        (((0,), (0,)), ((), ())),
        preferred_element_type=f32,
    )
    per_target = sums.shape[0] // half
    first = pl.multiple_of(block * columns, columns)
    for target in range(half):
        for row in range(per_target):
            out_ref[target, pl.ds(row * all_columns + first, columns), :] = sums[
                target * per_target + row
            ]

    @pl.when(block == pl.num_programs(0) - 1)
    def _():
        share = channels // half
        for target in range(half):
            mine = local[target * share : (target + 1) * share]
            mirrored = local[(half - 1 - target) * share : (half - target) * share]
            rows = two_terms(jnp.where(upper, mirrored, mine))
            out_ref[target, per_target * all_columns :] = stacked(
                rows, out_ref.shape[1] - per_target * all_columns
            )
        terms = stacked(two_terms(bias[...]), columns).astype(f32)
        for in_upper, (member, row) in enumerate(bias_places(half, per_target)):
            here = slice(row * all_columns, row * all_columns + columns)
            old = out_ref[member, here].astype(f32)
            ours = upper if in_upper else jnp.logical_not(upper)
            out_ref[member, here] = jnp.where(ours, terms, old).astype(bf16)


def delta_call(sizes, pre_act, cotangent, field_in):
    grid_rows, columns, channels = pre_act.shape
    half = sizes[0]
    rows = 2 * half * (sizes[1] + 1)
    block = min(16, columns)
    field = pl.BlockSpec((grid_rows, block, channels), lambda i: (0, i, 0))
    message = (half, rows // half * columns + extra_rows(channels, half), channels)
    return pl.pallas_call(
        functools.partial(delta_kernel, sizes),
        grid=(columns // block,),
        in_specs=[field, field, pl.BlockSpec(memory_space=pl.ANY)],
        out_specs=[field, whole(message)],
        out_shape=[
            jax.ShapeDtypeStruct(pre_act.shape, bf16),
            jax.ShapeDtypeStruct(message, bf16),
        ],
        scratch_shapes=[
            pltpu.VMEM((block, grid_rows, channels), bf16),
            pltpu.VMEM((channels, channels), f32),
            pltpu.VMEM((1, channels), f32),
            pltpu.VMEM((rows, grid_rows), bf16),
            pltpu.VMEM((columns // block, grid_rows, block, channels), bf16),
            pltpu.SemaphoreType.DMA((columns // block,)),
        ],
        compiler_params=params(60),
        cost_estimate=pl.CostEstimate(
            flops=4 * rows * pre_act.size, bytes_accessed=8 * pre_act.size, transcendentals=pre_act.size
        ),
        name="delta_and_x_sums",
    )(pre_act, cotangent, field_in)


def input_kernel(sizes, pieces, *refs):
    field_refs, out_refs, table = refs[:pieces], refs[pieces:-1], refs[-1]
    columns, channels = field_refs[0].shape[1:]
    block = pl.program_id(0)
    all_columns = columns * pl.num_programs(0)

    @pl.when(block == 0)
    def _():
        table[...] = x_table(sizes, relative=True)

    lines = [jnp.swapaxes(ref[...], 0, 1) for ref in field_refs]
    sums = matrix_per_column(
        table[...],
        [jnp.concatenate([part[y] for part in lines], axis=0) for y in range(columns)],
    )
    first = pl.multiple_of(block * columns, columns)
    rows = sums.shape[0] // len(out_refs)
    for pair, out_ref in enumerate(out_refs):
        for row in range(rows):
            out_ref[pl.ds(row * all_columns + first, columns), :] = sums[pair * rows + row]


def input_call(sizes, field_in):
    grid_rows, columns, channels = field_in.shape
    half = sizes[0]
    rows = 2 * half * (sizes[1] + 1)
    block = min(16, columns)
    pieces = 4
    message = (2 * rows // half * columns, channels)
    return pl.pallas_call(
        functools.partial(input_kernel, sizes, pieces),
        grid=(columns // block,),
        in_specs=[
            pl.BlockSpec(
                (grid_rows // pieces, block, channels), lambda i, piece=piece: (piece, i, 0)
            )
            for piece in range(pieces)
        ],
        out_specs=[whole(message)] * (half // 2),
        out_shape=[jax.ShapeDtypeStruct(message, bf16)] * (half // 2),
        scratch_shapes=[pltpu.VMEM((rows, grid_rows), bf16)],
        compiler_params=params(60),
        cost_estimate=pl.CostEstimate(
            flops=2 * rows * field_in.size, bytes_accessed=4 * field_in.size, transcendentals=0
        ),
        name="input_x_sums",
    )(*[field_in] * pieces)


def y_transform_kernel(columns, extra, blocks, total_rows, places, arrays, table_ref, *refs):
    line_refs, out_refs = refs[:arrays], refs[arrays:]
    sources, channels = len(places), line_refs[0].shape[-1]

    def rows_of(source, first, last):
        array, at = places[source]
        return line_refs[array][at + first : at + last]

    frequencies = (total_rows - extra) // columns // 2
    own = blocks // 2
    size = table_ref.shape[0] // blocks
    table = table_ref[...]
    place = lax.axis_index("dp")
    for t in range(frequencies):
        pieces = [
            rows_of(source, row * columns, (row + 1) * columns)
            for row in (2 * t, 2 * t + 1)
            for source in range(sources)
        ]
        for in_upper, (member, row) in enumerate(bias_places(sources, 2 * frequencies)):
            if extra and row == 2 * t + 1:
                keep = jnp.where(place == in_upper * (2 * sources - 1), 0.0, 1.0).astype(f32)
                pieces[sources:] = [
                    (piece.astype(f32) * keep).astype(bf16) for piece in pieces[sources:]
                ]
        lines = jnp.concatenate(pieces, axis=0)
        sums = jnp.dot(table, lines, preferred_element_type=f32).astype(bf16)
        for block in range(blocks):
            held = t if block < own else frequencies - 1 - t
            if 0 <= held < frequencies - 1:
                first = (block // len(out_refs)) * (frequencies - 1) + held
                out_refs[block % len(out_refs)][first * size : (first + 1) * size] = sums[
                    block * size : (block + 1) * size
                ]
    if extra:
        share = channels // sources
        shares = [
            unpack_terms(share, rows_of(i, total_rows - extra, total_rows)) for i in range(sources)
        ]
        bias = 0.0
        for in_upper, (member, row) in enumerate(bias_places(sources, 2 * frequencies)):
            first = row * columns
            total = sum(
                unpack_terms(1, rows_of(i, first, first + min(16, columns))) for i in range(sources)
            )
            bias = bias + jnp.where(place == in_upper * (2 * sources - 1), total, 0.0)
        packed = pack_share(sum(shares), bias)
        for out_ref in out_refs:
            out_ref[out_ref.shape[0] - packed.shape[0] :] = packed


def y_transform_call(table, lines, places, total_rows, blocks, outputs, columns, extra):
    channels = lines[0].shape[-1]
    held = (total_rows - extra) // columns // 2 - 1
    size = table.shape[0] // blocks
    rows = blocks // outputs * held * size
    if extra:
        rows += packed_rows(channels, len(places))
    return pl.pallas_call(
        functools.partial(
            y_transform_kernel, columns, extra, blocks, total_rows, places, len(lines)
        ),
        out_shape=[jax.ShapeDtypeStruct((rows, channels), bf16)] * outputs,
        compiler_params=params(),
        cost_estimate=pl.CostEstimate(
            flops=2 * (held + 1) * table.size * channels,
            bytes_accessed=4 * len(places) * total_rows * channels,
            transcendentals=0,
        ),
        name="y_sums",
    )(table, *lines)


def turned(values):
    rows = values.shape[0]
    even = lax.broadcasted_iota(jnp.int32, values.shape, 0) % 2 == 0
    up = pltpu.roll(values, rows - 1, 0)
    down = pltpu.roll(values, 1, 0)
    return jnp.concatenate([values, jnp.where(even, up, -down)], axis=1)


def load_kernel(source_ref, target_ref, semaphores):
    held, modes = source_ref.shape[:2]
    pieces = semaphores.shape[1]
    rows = modes // pieces
    copies = [
        [
            pltpu.make_async_copy(
                source_ref.at[j, pl.ds(k * rows, rows)],
                target_ref.at[j, pl.ds(k * rows, rows)],
                semaphores.at[j, k],
            )
            for k in range(pieces)
        ]
        for j in range(held)
    ]
    for copy in sum(copies, []):
        copy.start()
    for j in range(held):
        for copy in copies[j]:
            copy.wait()
        if j >= turned_count(held):
            continue

        def turn(mode, carry, j=j):
            for part in range(2):
                target_ref[j, mode, part] = target_ref[j, mode, part].T
            return carry

        lax.fori_loop(0, modes, turn, 0, unroll=4)


def turned_count(held):
    return held // 2


def load_call(weight):
    held = weight.shape[0]
    return pl.pallas_call(
        load_kernel,
        in_specs=[pl.BlockSpec(memory_space=pl.ANY)],
        out_specs=pl.BlockSpec(memory_space=pltpu.VMEM),
        out_shape=pltpu.VMEM(weight.shape, bf16),
        scratch_shapes=[pltpu.SemaphoreType.DMA((held, 2))],
        compiler_params=params(50),
        cost_estimate=pl.CostEstimate(flops=0, bytes_accessed=4 * weight.size, transcendentals=0),
        name="weights_to_vmem",
    )(weight)


def back_kernel(share, scale_ref, weight_ref, *refs):
    part_refs, (back_ref, delta_ref, share_ref) = refs[:-3], refs[-3:]
    held, rows, channels = delta_ref.shape
    block = weight_ref.shape[1]
    j, k = pl.program_id(0), pl.program_id(1)
    first = pl.multiple_of((j * (rows // (2 * block)) + k) * 2 * block, 2 * block)
    here = pl.ds(first, 2 * block)
    inner = pl.ds(pl.multiple_of(k * 2 * block, 2 * block), 2 * block)
    total = part_refs[0][here].astype(f32)
    for ref in part_refs[1:]:
        total = total + ref[here].astype(f32)
    delta = total.astype(bf16)
    delta_ref[j, inner] = delta
    both = turned(delta.astype(f32)).astype(bf16)

    def products(is_turned):
        sums = []
        for mode in range(block):
            weight = jnp.concatenate(
                [weight_ref[0, mode, 0], weight_ref[0, mode, 1]], axis=0 if is_turned else 1
            )
            sums.append(
                lax.dot_general(
                    both[2 * mode : 2 * mode + 2],
                    weight,
                    (((1,), (0 if is_turned else 1,)), ((), ())),
                    preferred_element_type=f32,
                )
            )
        back_ref[j, inner] = (jnp.concatenate(sums, axis=0) * scale_ref[inner]).astype(bf16)

    pl.when(j < turned_count(held))(lambda: products(True))
    pl.when(j >= turned_count(held))(lambda: products(False))

    @pl.when((j == 0) & (k == 0))
    def _():
        extra = share_ref.shape[0]
        pieces = [unpack_share(share, ref[ref.shape[0] - extra :]) for ref in part_refs]
        share_ref[...] = pack_share(sum(p[0] for p in pieces), sum(p[1] for p in pieces))


def back_call(scale_rows, weight, parts, share):
    held, modes, _, channels, _ = weight.shape
    block = min(16, modes)
    shape = (held, 2 * modes, channels)
    extra = (parts[0].shape[0] - held * 2 * modes, channels)
    return pl.pallas_call(
        functools.partial(back_kernel, share),
        grid=(held, modes // block),
        in_specs=[
            whole(scale_rows.shape),
            pl.BlockSpec((1, block, 2, channels, channels), lambda j, k: (j, k, 0, 0, 0)),
        ]
        + [whole(part.shape) for part in parts],
        out_specs=[whole(shape), whole(shape), whole(extra)],
        out_shape=[
            jax.ShapeDtypeStruct(shape, bf16),
            jax.ShapeDtypeStruct(shape, bf16),
            jax.ShapeDtypeStruct(extra, bf16),
        ],
        compiler_params=params(),
        cost_estimate=pl.CostEstimate(
            flops=4 * weight.size, bytes_accessed=2 * weight.size, transcendentals=0
        ),
        name="mode_back",
    )(scale_rows, weight, *parts)


def outer_kernel(sizes, scale_ref, delta_ref, *refs):
    part_refs, (out_ref, table_ref) = refs[:-2], refs[-2:]

    @pl.when(pl.program_id(0) == 0)
    def _():
        table_ref[...] = x_table(sizes, transposed=True, relative=True)

    modes = out_ref.shape[1]
    channels = out_ref.shape[-1]
    total = part_refs[0][...].astype(f32)
    for ref in part_refs[1:]:
        total = total + ref[...].astype(f32)
    field = (total.astype(bf16).astype(f32) * scale_ref[...]).astype(bf16).astype(f32)
    delta = turned(delta_ref[0].astype(f32))
    group = 4
    mode_of_row = lax.broadcasted_iota(jnp.int32, (2 * group, 2 * channels), 0) // 2
    for first in range(0, modes, group):
        rows = slice(2 * first, 2 * (first + group))
        alone = [jnp.where(mode_of_row == i, delta[rows], 0.0) for i in range(group)]
        product = lax.dot_general(
            field[rows].astype(bf16),
            jnp.concatenate(alone, axis=1).astype(bf16),
            (((0,), (0,)), ((), ())),
            preferred_element_type=f32,
        ).astype(bf16)
        for i in range(2 * group):
            out_ref[0, first + i // 2, i % 2] = product[:, i * channels : (i + 1) * channels]


def outer_call(sizes, scale_rows, delta, parts):
    table = (sizes[2], 2 * sizes[0] * (sizes[1] + 1))
    held, rows, channels = delta.shape
    modes = rows // 2
    part = pl.BlockSpec((1, rows, channels), lambda j: (j, 0, 0))
    return pl.pallas_call(
        functools.partial(outer_kernel, sizes),
        grid=(held,),
        in_specs=[whole((rows, channels)), part]
        + [
            pl.BlockSpec((rows, channels), lambda j, first=first: (j + first, 0))
            for _, first in parts
        ],
        out_specs=[
            pl.BlockSpec((1, modes, 2, channels, channels), lambda j: (j, 0, 0, 0, 0)),
            whole(table),
        ],
        out_shape=[
            jax.ShapeDtypeStruct((held, modes, 2, channels, channels), bf16),
            jax.ShapeDtypeStruct(table, bf16),
        ],
        compiler_params=params(),
        cost_estimate=pl.CostEstimate(
            flops=6 * held * modes * channels * channels,
            bytes_accessed=4 * held * modes * channels * channels,
            transcendentals=0,
        ),
        name="grad_spectral",
    )(scale_rows, delta, *[part for part, _ in parts])


def y_inverse_kernel(columns, parts, table_ref, share_ref, *refs):
    part_refs, out_refs = refs[:parts], refs[parts:]
    channels = share_ref.shape[1]
    message = out_refs[0].shape[0] // 2
    targets = 2 * len(out_refs)
    extra = extra_rows(channels, targets)
    frequencies = (message - extra) // columns // 2
    own = parts // 2
    size = part_refs[0].shape[1]
    table = table_ref[...]
    for t in range(frequencies):
        first = 0 if t < frequencies - 1 else own
        last = 2 * own if t > 0 else own
        modes = jnp.concatenate(
            [
                part_refs[block][t if block < own else frequencies - 1 - t]
                for block in range(first, last)
            ],
            axis=0,
        )
        sums = lax.dot_general(
            table[first * size : last * size],
            modes,
            (((0,), (0,)), ((), ())),
            preferred_element_type=f32,
        ).astype(bf16)
        for part in range(2):
            for target in range(targets):
                at = target % 2 * message + (2 * t + part) * columns
                piece = part * targets + target
                out_refs[target // 2][at : at + columns] = sums[
                    piece * columns : (piece + 1) * columns
                ]
    for target in range(targets):
        last = (target % 2 + 1) * message
        out_refs[target // 2][last - extra : last] = share_ref[:extra]
    place = lax.axis_index("dp")
    height = min(16, columns)
    share = channels // targets
    terms = share_ref[2 * share : 2 * share + height].astype(f32)
    for in_upper, (member, row) in enumerate(bias_places(targets, 2 * frequencies)):
        ours = place == in_upper * (2 * targets - 1)
        for target in range(targets):
            first = target % 2 * message + row * columns
            old = out_refs[target // 2][first : first + height].astype(f32)
            out_refs[target // 2][first : first + height] = jnp.where(ours, terms, old).astype(bf16)


def y_inverse_call(table, share, parts, targets, columns):
    held, size, channels = parts[0].shape
    rows = 2 * (held + 1)
    message = (2 * (rows * columns + extra_rows(channels, targets)), channels)
    return pl.pallas_call(
        functools.partial(y_inverse_kernel, columns, len(parts)),
        out_shape=[jax.ShapeDtypeStruct(message, bf16)] * (targets // 2),
        compiler_params=params(),
        cost_estimate=pl.CostEstimate(
            flops=rows * table.size * channels,
            bytes_accessed=4 * targets * rows * columns * channels,
            transcendentals=0,
        ),
        name="y_inverse",
    )(table, share, *parts)


def final_kernel(places, arrays, *refs):
    line_refs, refs = refs[:arrays], refs[arrays:]
    delta_ref, weight_ref, table, out_ref, local_ref, bias_ref = refs
    grid_rows, columns, channels = out_ref.shape
    half = len(places)
    block = pl.program_id(0)
    all_columns = columns * pl.num_programs(0)
    per_source = table.shape[1] // half
    first = pl.multiple_of(block * columns, columns)

    lines = jnp.stack(
        [
            line_refs[array][pl.ds(at + row * all_columns + first, columns), :]
            for array, at in places
            for row in range(per_source)
        ],
        axis=0,
    )
    lines = jnp.swapaxes(lines, 0, 1)
    spectral = matrix_per_column(table[...], [lines[y] for y in range(columns)])
    local = lax.dot_general(
        delta_ref[...].reshape(grid_rows * columns, channels),
        weight_ref[...],
        (((1,), (1,)), ((), ())),
        preferred_element_type=f32,
    ).reshape(grid_rows, columns, channels)
    out_ref[...] = (spectral.astype(f32) + local).astype(bf16)

    @pl.when(block == 0)
    def _():
        share = channels // half
        extra = extra_rows(channels, half)
        upper = lax.axis_index("dp") >= half
        rows_low, rows_high = (row for _, row in bias_places(half, per_source))
        shares, biases = [], []
        for array, at in places:
            begin = at + per_source * all_columns
            shares.append(unpack_terms(share, line_refs[array][begin : begin + extra]))
            low, high = (
                unpack_terms(1, line_refs[array][at + row * all_columns : at + row * all_columns + columns])
                for row in (rows_low, rows_high)
            )
            biases.append(jnp.where(upper, high, low))
        for source, rows in enumerate(in_relative_order(shares, half)):
            local_ref[source * share : (source + 1) * share] = rows
        bias_ref[...] = in_relative_order(biases, half)[0]


def final_call(table, lines, places, delta, local_weight):
    grid_rows, columns, channels = delta.shape
    rows = table.shape[1]
    block = min(16, columns)
    field = pl.BlockSpec((grid_rows, block, channels), lambda i: (0, i, 0))
    return pl.pallas_call(
        functools.partial(final_kernel, places, len(lines)),
        grid=(columns // block,),
        in_specs=[whole(line.shape) for line in lines] + [field, whole(local_weight.shape), whole(table.shape)],
        out_specs=[field, whole((channels, channels)), whole((1, channels))],
        out_shape=[
            jax.ShapeDtypeStruct(delta.shape, bf16),
            jax.ShapeDtypeStruct((channels, channels), f32),
            jax.ShapeDtypeStruct((1, channels), f32),
        ],
        compiler_params=params(),
        cost_estimate=pl.CostEstimate(
            flops=2 * (rows + channels) * delta.size, bytes_accessed=5 * delta.size, transcendentals=0
        ),
        name="x_inverse_and_local",
    )(*lines, delta, local_weight, table)


def on_device(field_in, pre_act, cotangent, spec_weight, local_weight):
    batch_size, slab_rows, col_block, channels = field_in.shape
    space_count = lax.axis_size("space")
    data_count = lax.axis_size("dp")
    grid_rows = slab_rows * space_count
    grid_cols = col_block * data_count
    kx_local, ky_local = spec_weight.shape[:2]
    half = data_count // 2
    half_cols = half * col_block
    row_count = 2 * (kx_local + 1)
    data_index = lax.axis_index("dp")
    space_index = lax.axis_index("space")
    upper = data_index // half

    sizes = (half, kx_local, slab_rows, grid_rows)

    blocks = 2 * space_count
    size = 2 * ky_local
    row = jnp.arange(blocks * size, dtype=jnp.int32)
    block, inner = row // size, row % size
    shift = block % space_count
    ky_index = (space_index + shift) % space_count * ky_local + inner // 2
    quarter = grid_cols // 4
    cosine_turn = inner % 2
    sine_turn = jnp.where((block // space_count) == upper, 1 + inner % 2, 3 * (1 - inner % 2))
    turn = jnp.concatenate(
        [
            jnp.broadcast_to(cosine_turn[:, None], (blocks * size, half_cols)),
            jnp.broadcast_to(sine_turn[:, None], (blocks * size, half_cols)),
        ],
        axis=1,
    )

    def y_basis(flip):
        column = jnp.arange(half_cols, dtype=jnp.int32)
        member = (column // col_block) ^ flip
        positions = upper * half_cols + member * col_block + column % col_block
        positions = jnp.concatenate([positions, positions])
        return cosine_table(ky_index[:, None] * positions[None, :] + quarter * turn, grid_cols)

    ky_row = space_index * ky_local + jnp.arange(size, dtype=jnp.int32) // 2
    scale = jnp.where(ky_row == 0, 1.0, 2.0).astype(f32) / (grid_rows * grid_cols)
    scale_rows = jnp.broadcast_to(scale[:, None], (size, channels))

    halves = [list(range(half)), list(range(half, data_count))]

    def exchange(values):
        return lax.all_to_all(
            values, "dp", split_axis=0, concat_axis=0, tiled=True, axis_index_groups=halves
        )

    def to_chips(chips):
        arrived = [chips[0]]
        for pair in range(1, half // 2):
            moves = [(d, d ^ (2 * pair)) for d in range(data_count)]
            arrived.append(lax.ppermute(chips[pair], "dp", moves))
        return arrived

    def between_cores(arrived):
        rows = arrived[0].shape[0] // 2
        mates = jnp.concatenate([part[rows:] for part in arrived], axis=0)
        mates = lax.ppermute(mates, "dp", [(d, d ^ 1) for d in range(data_count)])
        places = [
            (source // 2, 0) if source % 2 == 0 else (half // 2, source // 2 * rows)
            for source in range(half)
        ]
        return arrived + [mates], places

    def pairs(mirror, shift):
        moves = []
        for d in range(data_count):
            for s in range(space_count):
                target = data_count - 1 - d if mirror else d
                moves.append(
                    (d * space_count + s, target * space_count + (s + shift) % space_count)
                )
        return moves

    order = [(mirror, shift) for mirror in (1, 0) for shift in reversed(range(space_count))][:-1]

    def gathered(parts):
        held = [parts[0]]
        for mirror, shift in order:
            held.append(
                lax.ppermute(
                    parts[mirror * space_count + shift], ("dp", "space"), pairs(mirror, shift)
                )
            )
        return held

    tied = lax.optimization_barrier

    share = channels // half
    extra = extra_rows(channels, half)

    message = row_count * col_block
    y_table = y_basis(0)
    relative_table = y_basis(data_index % half)

    arrived = to_chips(input_call(sizes, field_in[0]))
    delta, delta_sums = delta_call(sizes, pre_act[0], cotangent[0], field_in[0])
    delta_sums, arrived = tied((delta_sums, arrived))
    delta_lines = exchange(delta_sums)
    lines, places = between_cores(arrived)
    input_parts = list(
        y_transform_call(
            relative_table, lines, places, message, blocks, space_count, col_block, 0
        )
    )
    for shift in range(1, space_count):
        input_parts[shift] = lax.ppermute(input_parts[shift], ("dp", "space"), pairs(0, shift))
    held_rows = kx_local * size
    mirrored = sum(part[held_rows:].astype(f32) for part in input_parts).astype(bf16)
    delta_lines, mirrored = tied((delta_lines, mirrored))

    message += extra
    delta_parts = y_transform_call(
        y_table,
        [delta_lines.reshape(half * message, channels)],
        [(0, source * message) for source in range(half)],
        message,
        blocks,
        blocks,
        col_block,
        extra,
    )
    delta_parts = list(delta_parts)
    rows = delta_parts[space_count].shape[0]
    delta_parts[space_count] = jnp.concatenate([delta_parts[space_count], mirrored], axis=0)
    weight, delta_parts = tied((spec_weight, delta_parts))
    weight = load_call(weight)
    delta_held = gathered(delta_parts)
    place = 1 + order.index((1, 0))
    input_held = [(part, 0) for part in input_parts] + [(delta_held[place][rows:], 0)]
    delta_held[place] = delta_held[place][:rows]
    back, delta_owned, share_rows = back_call(scale_rows, weight, delta_held, share)
    received = {(0, 0): back}
    for mirror, shift in order:
        received[(mirror, -shift % space_count)] = lax.ppermute(
            back, ("dp", "space"), pairs(mirror, shift)
        )
    modes = [received[(mirror, shift)] for mirror in (0, 1) for shift in range(space_count)]
    column_sums = y_inverse_call(relative_table, share_rows, modes, half, col_block)
    column_sums, delta_owned = tied((column_sums, delta_owned))
    columns = to_chips(column_sums)
    grad_spectral, x_basis = outer_call(sizes, scale_rows, delta_owned, input_held)
    columns, grad_spectral = tied((columns, grad_spectral))
    lines, places = between_cores(columns)
    grad_input, grad_local, bias_rows = final_call(x_basis, lines, places, delta, local_weight)
    return (grad_input[None], grad_spectral, grad_local, bias_rows.reshape(channels))


def solution(mesh):
    placed = (
        P(None, "space", "dp", None),
        P(None, "space", "dp", None),
        P(None, "space", "dp", None),
        P("dp", "space", None, None, None),
        P(),
    )
    return jax.shard_map(
        on_device,
        mesh=mesh,
        in_specs=placed,
        out_specs=(P(None, "space", "dp", None), P("dp", "space", None, None, None), P(), P()),
        check_vma=False,
    )
```

```python
import functools
import math

import jax
import jax.numpy as jnp
from jax import lax
from jax.experimental import pallas as pl
from jax.experimental.pallas import tpu as pltpu
from jax.sharding import PartitionSpec as P

root_two_pi = 0.7978845608028654
cubic_coef = 0.044715
f32 = jnp.float32
bf16 = jnp.bfloat16
mebi = 1024 * 1024


def gelu_slope(values):
    square = values * values
    cubic = root_two_pi * cubic_coef
    tangent = jnp.tanh(values * (root_two_pi + cubic * square))
    inner = values * (1.0 - tangent * tangent)
    return 0.5 * ((1.0 + tangent) + inner * (root_two_pi + (3.0 * cubic) * square))


def cosine_table(phases, period):
    quarter = period // 4
    if period & (period - 1) == 0:
        turns = (phases + quarter // 2) >> (quarter.bit_length() - 1)
    else:
        turns = (phases + quarter // 2) // quarter
    angle = (phases - turns * quarter).astype(f32) * (2.0 * math.pi / period)
    square = angle * angle
    cosine = 1.0 + square * (
        -0.5 + square * (1.0 / 24.0 + square * (-1.0 / 720.0 + square * (1.0 / 40320.0)))
    )
    sine = angle * (
        1.0
        + square
        * (-1.0 / 6.0 + square * (1.0 / 120.0 + square * (-1.0 / 5040.0 + square * (1.0 / 362880.0))))
    )
    turns = turns & 3
    magnitude = jnp.where((turns & 1) == 0, cosine, sine)
    return jnp.where((turns == 1) | (turns == 2), -magnitude, magnitude).astype(bf16)


def x_table(sizes, transposed=False, relative=False):
    half, kx_local, slab_rows, grid_rows = sizes
    row_count = 2 * (kx_local + 1)
    upper = (lax.axis_index("dp") >= half).astype(jnp.int32)
    shape = (half * row_count, slab_rows)
    if transposed:
        shape = shape[::-1]
    row = lax.broadcasted_iota(jnp.int32, shape, 1 if transposed else 0)
    position = lax.axis_index("space") * slab_rows + lax.broadcasted_iota(
        jnp.int32, shape, 0 if transposed else 1
    )
    member = sum((row >= i * row_count).astype(jnp.int32) for i in range(1, half))
    inner = row - member * row_count
    if relative:
        member = member ^ (lax.axis_index("dp") & (half - 1))
    ascending = member * kx_local + (inner >> 1)
    frequency = ascending + upper * (half * kx_local - 2 * ascending)
    quarter = grid_rows // 4
    return cosine_table(frequency * position - (inner & 1) * quarter, grid_rows)


def params(mebibytes=16):
    return pltpu.CompilerParams(vmem_limit_bytes=mebibytes * mebi)


def whole(shape):
    return pl.BlockSpec(shape, lambda *_: (0,) * len(shape))


def matrix_per_column(table, columns_of, rows=()):
    channels = columns_of[0].shape[1]
    results = []
    totals = [0.0] * len(rows)
    for y in range(0, len(columns_of), 2):
        pair = jnp.concatenate(columns_of[y : y + 2], axis=1)
        sums = jnp.dot(table, pair, preferred_element_type=f32)
        totals = [total + sums[row : row + 1] for total, row in zip(totals, rows)]
        sums = sums.astype(bf16)
        results += [sums[:, :channels], sums[:, channels:]]
    results = jnp.swapaxes(jnp.stack(results, axis=0), 0, 1)
    if rows:
        return results, [total[:, :channels] + total[:, channels:] for total in totals]
    return results


def two_terms(values):
    high = values.astype(bf16)
    return high, (values - high.astype(f32)).astype(bf16)


def extra_rows(channels, half):
    return -(-2 * (channels // half) // 16) * 16


def packed_rows(channels, half):
    return -(-(2 * (channels // half) + 2) // 16) * 16


def stacked(parts, rows):
    parts = list(parts)
    filled = sum(part.shape[0] for part in parts)
    if rows > filled:
        parts.append(jnp.zeros((rows - filled, parts[0].shape[1]), bf16))
    return jnp.concatenate([part.astype(f32) for part in parts], axis=0).astype(bf16)


def pack_share(share, bias):
    rows, channels = share.shape
    return stacked(two_terms(share) + two_terms(bias), packed_rows(channels, channels // rows))


def unpack_terms(rows, message):
    message = message.astype(f32)
    return message[:rows] + message[rows : 2 * rows]


def unpack_share(rows, message):
    return unpack_terms(rows, message), unpack_terms(1, message[2 * rows : 2 * rows + 2])


def bias_places(half, rows):
    return (0, 1), (half - 1, rows - 1)


def in_relative_order(pieces, half):
    place = lax.axis_index("dp")
    key = jnp.where(place >= half, 2 * half - 1 - place, place)
    step = 1
    while step < half:
        flag = (key & step) != 0
        pieces = [jnp.where(flag, pieces[i ^ step], pieces[i]) for i in range(half)]
        step *= 2
    return pieces


def delta_kernel(
    sizes,
    pre_ref,
    cot_ref,
    field_ref,
    delta_ref,
    out_ref,
    lines,
    local,
    bias,
    table,
    field,
    semaphores,
):
    grid_rows, columns, channels = pre_ref.shape
    half = out_ref.shape[0]
    block = pl.program_id(0)
    all_columns = columns * pl.num_programs(0)
    step = 16
    blocks = field.shape[0]

    def arriving(i):
        return pltpu.make_async_copy(
            field_ref.at[:, pl.ds(i * columns, columns)], field.at[i], semaphores.at[i]
        )

    @pl.when(block == 0)
    def _():
        for i in range(blocks):
            arriving(i).start()
        local[...] = jnp.zeros_like(local)
        bias[...] = jnp.zeros_like(bias)
        table[...] = x_table(sizes)

    def slab(i, carry):
        rows = pl.ds(pl.multiple_of(i * step, step), step)
        slope = gelu_slope(pre_ref[rows].astype(f32))
        delta = (cot_ref[rows].astype(f32) * slope).astype(bf16)
        delta_ref[rows] = delta
        lines[:, rows, :] = jnp.swapaxes(delta, 0, 1)
        return carry

    lax.fori_loop(0, grid_rows // step, slab, 0)
    sums, totals = matrix_per_column(
        table[...], [lines[y] for y in range(columns)], (0, table.shape[0] - 2)
    )
    upper = lax.axis_index("dp") >= half
    bias[...] += jnp.where(upper, totals[1], totals[0])
    for i in range(blocks):

        @pl.when(block == i)
        def _(i=i):
            arriving(i).wait()

    local[...] += lax.dot_general(
        field[block].reshape(grid_rows * columns, channels),
        delta_ref[...].reshape(grid_rows * columns, channels),
        (((0,), (0,)), ((), ())),
        preferred_element_type=f32,
    )
    per_target = sums.shape[0] // half
    first = pl.multiple_of(block * columns, columns)
    for target in range(half):
        for row in range(per_target):
            out_ref[target, pl.ds(row * all_columns + first, columns), :] = sums[
                target * per_target + row
            ]

    @pl.when(block == pl.num_programs(0) - 1)
    def _():
        share = channels // half
        for target in range(half):
            mine = local[target * share : (target + 1) * share]
            mirrored = local[(half - 1 - target) * share : (half - target) * share]
            rows = two_terms(jnp.where(upper, mirrored, mine))
            out_ref[target, per_target * all_columns :] = stacked(
                rows, out_ref.shape[1] - per_target * all_columns
            )
        terms = stacked(two_terms(bias[...]), columns).astype(f32)
        for in_upper, (member, row) in enumerate(bias_places(half, per_target)):
            here = slice(row * all_columns, row * all_columns + columns)
            old = out_ref[member, here].astype(f32)
            ours = upper if in_upper else jnp.logical_not(upper)
            out_ref[member, here] = jnp.where(ours, terms, old).astype(bf16)


def delta_call(sizes, pre_act, cotangent, field_in):
    grid_rows, columns, channels = pre_act.shape
    half = sizes[0]
    rows = 2 * half * (sizes[1] + 1)
    block = min(16, columns)
    field = pl.BlockSpec((grid_rows, block, channels), lambda i: (0, i, 0))
    message = (half, rows // half * columns + extra_rows(channels, half), channels)
    return pl.pallas_call(
        functools.partial(delta_kernel, sizes),
        grid=(columns // block,),
        in_specs=[field, field, pl.BlockSpec(memory_space=pl.ANY)],
        out_specs=[field, whole(message)],
        out_shape=[
            jax.ShapeDtypeStruct(pre_act.shape, bf16),
            jax.ShapeDtypeStruct(message, bf16),
        ],
        scratch_shapes=[
            pltpu.VMEM((block, grid_rows, channels), bf16),
            pltpu.VMEM((channels, channels), f32),
            pltpu.VMEM((1, channels), f32),
            pltpu.VMEM((rows, grid_rows), bf16),
            pltpu.VMEM((columns // block, grid_rows, block, channels), bf16),
            pltpu.SemaphoreType.DMA((columns // block,)),
        ],
        compiler_params=params(60),
        cost_estimate=pl.CostEstimate(
            flops=4 * rows * pre_act.size, bytes_accessed=8 * pre_act.size, transcendentals=pre_act.size
        ),
        name="delta_and_x_sums",
    )(pre_act, cotangent, field_in)


def input_kernel(sizes, pieces, *refs):
    field_refs, out_refs, table = refs[:pieces], refs[pieces:-1], refs[-1]
    columns, channels = field_refs[0].shape[1:]
    block = pl.program_id(0)
    all_columns = columns * pl.num_programs(0)

    @pl.when(block == 0)
    def _():
        table[...] = x_table(sizes, relative=True)

    lines = [jnp.swapaxes(ref[...], 0, 1) for ref in field_refs]
    sums = matrix_per_column(
        table[...],
        [jnp.concatenate([part[y] for part in lines], axis=0) for y in range(columns)],
    )
    first = pl.multiple_of(block * columns, columns)
    rows = sums.shape[0] // len(out_refs)
    for pair, out_ref in enumerate(out_refs):
        for row in range(rows):
            out_ref[pl.ds(row * all_columns + first, columns), :] = sums[pair * rows + row]


def input_call(sizes, field_in):
    grid_rows, columns, channels = field_in.shape
    half = sizes[0]
    rows = 2 * half * (sizes[1] + 1)
    block = min(16, columns)
    pieces = 4
    message = (2 * rows // half * columns, channels)
    return pl.pallas_call(
        functools.partial(input_kernel, sizes, pieces),
        grid=(columns // block,),
        in_specs=[
            pl.BlockSpec(
                (grid_rows // pieces, block, channels), lambda i, piece=piece: (piece, i, 0)
            )
            for piece in range(pieces)
        ],
        out_specs=[whole(message)] * (half // 2),
        out_shape=[jax.ShapeDtypeStruct(message, bf16)] * (half // 2),
        scratch_shapes=[pltpu.VMEM((rows, grid_rows), bf16)],
        compiler_params=params(60),
        cost_estimate=pl.CostEstimate(
            flops=2 * rows * field_in.size, bytes_accessed=4 * field_in.size, transcendentals=0
        ),
        name="input_x_sums",
    )(*[field_in] * pieces)


def y_transform_kernel(columns, extra, blocks, total_rows, places, arrays, table_ref, *refs):
    line_refs, out_refs = refs[:arrays], refs[arrays:]
    sources, channels = len(places), line_refs[0].shape[-1]

    def rows_of(source, first, last):
        array, at = places[source]
        return line_refs[array][at + first : at + last]

    frequencies = (total_rows - extra) // columns // 2
    own = blocks // 2
    size = table_ref.shape[0] // blocks
    table = table_ref[...]
    place = lax.axis_index("dp")
    for t in range(frequencies):
        pieces = [
            rows_of(source, row * columns, (row + 1) * columns)
            for row in (2 * t, 2 * t + 1)
            for source in range(sources)
        ]
        for in_upper, (member, row) in enumerate(bias_places(sources, 2 * frequencies)):
            if extra and row == 2 * t + 1:
                keep = jnp.where(place == in_upper * (2 * sources - 1), 0.0, 1.0).astype(f32)
                pieces[sources:] = [
                    (piece.astype(f32) * keep).astype(bf16) for piece in pieces[sources:]
                ]
        lines = jnp.concatenate(pieces, axis=0)
        sums = jnp.dot(table, lines, preferred_element_type=f32).astype(bf16)
        for block in range(blocks):
            held = t if block < own else frequencies - 1 - t
            if 0 <= held < frequencies - 1:
                first = (block // len(out_refs)) * (frequencies - 1) + held
                out_refs[block % len(out_refs)][first * size : (first + 1) * size] = sums[
                    block * size : (block + 1) * size
                ]
    if extra:
        share = channels // sources
        shares = [
            unpack_terms(share, rows_of(i, total_rows - extra, total_rows)) for i in range(sources)
        ]
        bias = 0.0
        for in_upper, (member, row) in enumerate(bias_places(sources, 2 * frequencies)):
            first = row * columns
            total = sum(
                unpack_terms(1, rows_of(i, first, first + min(16, columns))) for i in range(sources)
            )
            bias = bias + jnp.where(place == in_upper * (2 * sources - 1), total, 0.0)
        packed = pack_share(sum(shares), bias)
        for out_ref in out_refs:
            out_ref[out_ref.shape[0] - packed.shape[0] :] = packed


def y_transform_call(table, lines, places, total_rows, blocks, outputs, columns, extra):
    channels = lines[0].shape[-1]
    held = (total_rows - extra) // columns // 2 - 1
    size = table.shape[0] // blocks
    rows = blocks // outputs * held * size
    if extra:
        rows += packed_rows(channels, len(places))
    return pl.pallas_call(
        functools.partial(
            y_transform_kernel, columns, extra, blocks, total_rows, places, len(lines)
        ),
        out_shape=[jax.ShapeDtypeStruct((rows, channels), bf16)] * outputs,
        compiler_params=params(),
        cost_estimate=pl.CostEstimate(
            flops=2 * (held + 1) * table.size * channels,
            bytes_accessed=4 * len(places) * total_rows * channels,
            transcendentals=0,
        ),
        name="y_sums",
    )(table, *lines)


def turned(values):
    rows = values.shape[0]
    even = lax.broadcasted_iota(jnp.int32, values.shape, 0) % 2 == 0
    up = pltpu.roll(values, rows - 1, 0)
    down = pltpu.roll(values, 1, 0)
    return jnp.concatenate([values, jnp.where(even, up, -down)], axis=1)


def load_kernel(source_ref, target_ref, semaphores):
    held, modes = source_ref.shape[:2]
    pieces = semaphores.shape[1]
    rows = modes // pieces
    copies = [
        [
            pltpu.make_async_copy(
                source_ref.at[j, pl.ds(k * rows, rows)],
                target_ref.at[j, pl.ds(k * rows, rows)],
                semaphores.at[j, k],
            )
            for k in range(pieces)
        ]
        for j in range(held)
    ]
    for copy in sum(copies, []):
        copy.start()
    for j in range(held):
        for copy in copies[j]:
            copy.wait()
        if j >= turned_count(held):
            continue

        def turn(mode, carry, j=j):
            for part in range(2):
                target_ref[j, mode, part] = target_ref[j, mode, part].T
            return carry

        lax.fori_loop(0, modes, turn, 0, unroll=4)


def turned_count(held):
    return held // 2


def load_call(weight):
    held = weight.shape[0]
    return pl.pallas_call(
        load_kernel,
        in_specs=[pl.BlockSpec(memory_space=pl.ANY)],
        out_specs=pl.BlockSpec(memory_space=pltpu.VMEM),
        out_shape=pltpu.VMEM(weight.shape, bf16),
        scratch_shapes=[pltpu.SemaphoreType.DMA((held, 2))],
        compiler_params=params(50),
        cost_estimate=pl.CostEstimate(flops=0, bytes_accessed=4 * weight.size, transcendentals=0),
        name="weights_to_vmem",
    )(weight)


def back_kernel(share, scale_ref, weight_ref, *refs):
    part_refs, (back_ref, delta_ref, share_ref) = refs[:-3], refs[-3:]
    held, rows, channels = delta_ref.shape
    block = weight_ref.shape[1]
    j, k = pl.program_id(0), pl.program_id(1)
    first = pl.multiple_of((j * (rows // (2 * block)) + k) * 2 * block, 2 * block)
    here = pl.ds(first, 2 * block)
    inner = pl.ds(pl.multiple_of(k * 2 * block, 2 * block), 2 * block)
    total = part_refs[0][here].astype(f32)
    for ref in part_refs[1:]:
        total = total + ref[here].astype(f32)
    delta = total.astype(bf16)
    delta_ref[j, inner] = delta
    both = turned(delta.astype(f32)).astype(bf16)

    def products(is_turned):
        sums = []
        for mode in range(block):
            weight = jnp.concatenate(
                [weight_ref[0, mode, 0], weight_ref[0, mode, 1]], axis=0 if is_turned else 1
            )
            sums.append(
                lax.dot_general(
                    both[2 * mode : 2 * mode + 2],
                    weight,
                    (((1,), (0 if is_turned else 1,)), ((), ())),
                    preferred_element_type=f32,
                )
            )
        back_ref[j, inner] = (jnp.concatenate(sums, axis=0) * scale_ref[inner]).astype(bf16)

    pl.when(j < turned_count(held))(lambda: products(True))
    pl.when(j >= turned_count(held))(lambda: products(False))

    @pl.when((j == 0) & (k == 0))
    def _():
        extra = share_ref.shape[0]
        pieces = [unpack_share(share, ref[ref.shape[0] - extra :]) for ref in part_refs]
        share_ref[...] = pack_share(sum(p[0] for p in pieces), sum(p[1] for p in pieces))


def back_call(scale_rows, weight, parts, share):
    held, modes, _, channels, _ = weight.shape
    block = min(16, modes)
    shape = (held, 2 * modes, channels)
    extra = (parts[0].shape[0] - held * 2 * modes, channels)
    return pl.pallas_call(
        functools.partial(back_kernel, share),
        grid=(held, modes // block),
        in_specs=[
            whole(scale_rows.shape),
            pl.BlockSpec((1, block, 2, channels, channels), lambda j, k: (j, k, 0, 0, 0)),
        ]
        + [whole(part.shape) for part in parts],
        out_specs=[whole(shape), whole(shape), whole(extra)],
        out_shape=[
            jax.ShapeDtypeStruct(shape, bf16),
            jax.ShapeDtypeStruct(shape, bf16),
            jax.ShapeDtypeStruct(extra, bf16),
        ],
        compiler_params=params(),
        cost_estimate=pl.CostEstimate(
            flops=4 * weight.size, bytes_accessed=2 * weight.size, transcendentals=0
        ),
        name="mode_back",
    )(scale_rows, weight, *parts)


def outer_kernel(sizes, scale_ref, delta_ref, *refs):
    part_refs, (out_ref, table_ref) = refs[:-2], refs[-2:]

    @pl.when(pl.program_id(0) == 0)
    def _():
        table_ref[...] = x_table(sizes, transposed=True, relative=True)

    modes = out_ref.shape[1]
    channels = out_ref.shape[-1]
    total = part_refs[0][...].astype(f32)
    for ref in part_refs[1:]:
        total = total + ref[...].astype(f32)
    field = (total.astype(bf16).astype(f32) * scale_ref[...]).astype(bf16).astype(f32)
    delta = turned(delta_ref[0].astype(f32))
    group = 4
    mode_of_row = lax.broadcasted_iota(jnp.int32, (2 * group, 2 * channels), 0) // 2
    for first in range(0, modes, group):
        rows = slice(2 * first, 2 * (first + group))
        alone = [jnp.where(mode_of_row == i, delta[rows], 0.0) for i in range(group)]
        product = lax.dot_general(
            field[rows].astype(bf16),
            jnp.concatenate(alone, axis=1).astype(bf16),
            (((0,), (0,)), ((), ())),
            preferred_element_type=f32,
        ).astype(bf16)
        for i in range(2 * group):
            out_ref[0, first + i // 2, i % 2] = product[:, i * channels : (i + 1) * channels]


def outer_call(sizes, scale_rows, delta, parts):
    table = (sizes[2], 2 * sizes[0] * (sizes[1] + 1))
    held, rows, channels = delta.shape
    modes = rows // 2
    part = pl.BlockSpec((1, rows, channels), lambda j: (j, 0, 0))
    return pl.pallas_call(
        functools.partial(outer_kernel, sizes),
        grid=(held,),
        in_specs=[whole((rows, channels)), part]
        + [
            pl.BlockSpec((rows, channels), lambda j, first=first: (j + first, 0))
            for _, first in parts
        ],
        out_specs=[
            pl.BlockSpec((1, modes, 2, channels, channels), lambda j: (j, 0, 0, 0, 0)),
            whole(table),
        ],
        out_shape=[
            jax.ShapeDtypeStruct((held, modes, 2, channels, channels), bf16),
            jax.ShapeDtypeStruct(table, bf16),
        ],
        compiler_params=params(),
        cost_estimate=pl.CostEstimate(
            flops=6 * held * modes * channels * channels,
            bytes_accessed=4 * held * modes * channels * channels,
            transcendentals=0,
        ),
        name="grad_spectral",
    )(scale_rows, delta, *[part for part, _ in parts])


def y_inverse_kernel(columns, parts, table_ref, share_ref, *refs):
    part_refs, out_refs = refs[:parts], refs[parts:]
    channels = share_ref.shape[1]
    message = out_refs[0].shape[0] // 2
    targets = 2 * len(out_refs)
    extra = extra_rows(channels, targets)
    frequencies = (message - extra) // columns // 2
    own = parts // 2
    size = part_refs[0].shape[1]
    table = table_ref[...]
    for t in range(frequencies):
        first = 0 if t < frequencies - 1 else own
        last = 2 * own if t > 0 else own
        modes = jnp.concatenate(
            [
                part_refs[block][t if block < own else frequencies - 1 - t]
                for block in range(first, last)
            ],
            axis=0,
        )
        sums = lax.dot_general(
            table[first * size : last * size],
            modes,
            (((0,), (0,)), ((), ())),
            preferred_element_type=f32,
        ).astype(bf16)
        for part in range(2):
            for target in range(targets):
                at = target % 2 * message + (2 * t + part) * columns
                piece = part * targets + target
                out_refs[target // 2][at : at + columns] = sums[
                    piece * columns : (piece + 1) * columns
                ]
    for target in range(targets):
        last = (target % 2 + 1) * message
        out_refs[target // 2][last - extra : last] = share_ref[:extra]
    place = lax.axis_index("dp")
    height = min(16, columns)
    share = channels // targets
    terms = share_ref[2 * share : 2 * share + height].astype(f32)
    for in_upper, (member, row) in enumerate(bias_places(targets, 2 * frequencies)):
        ours = place == in_upper * (2 * targets - 1)
        for target in range(targets):
            first = target % 2 * message + row * columns
            old = out_refs[target // 2][first : first + height].astype(f32)
            out_refs[target // 2][first : first + height] = jnp.where(ours, terms, old).astype(bf16)


def y_inverse_call(table, share, parts, targets, columns):
    held, size, channels = parts[0].shape
    rows = 2 * (held + 1)
    message = (2 * (rows * columns + extra_rows(channels, targets)), channels)
    return pl.pallas_call(
        functools.partial(y_inverse_kernel, columns, len(parts)),
        out_shape=[jax.ShapeDtypeStruct(message, bf16)] * (targets // 2),
        compiler_params=params(),
        cost_estimate=pl.CostEstimate(
            flops=rows * table.size * channels,
            bytes_accessed=4 * targets * rows * columns * channels,
            transcendentals=0,
        ),
        name="y_inverse",
    )(table, share, *parts)


def final_kernel(places, arrays, *refs):
    line_refs, refs = refs[:arrays], refs[arrays:]
    delta_ref, weight_ref, table, out_ref, local_ref, bias_ref = refs
    grid_rows, columns, channels = out_ref.shape
    half = len(places)
    block = pl.program_id(0)
    all_columns = columns * pl.num_programs(0)
    per_source = table.shape[1] // half
    first = pl.multiple_of(block * columns, columns)

    lines = jnp.stack(
        [
            line_refs[array][pl.ds(at + row * all_columns + first, columns), :]
            for array, at in places
            for row in range(per_source)
        ],
        axis=0,
    )
    lines = jnp.swapaxes(lines, 0, 1)
    spectral = matrix_per_column(table[...], [lines[y] for y in range(columns)])
    local = lax.dot_general(
        delta_ref[...].reshape(grid_rows * columns, channels),
        weight_ref[...],
        (((1,), (1,)), ((), ())),
        preferred_element_type=f32,
    ).reshape(grid_rows, columns, channels)
    out_ref[...] = (spectral.astype(f32) + local).astype(bf16)

    @pl.when(block == 0)
    def _():
        share = channels // half
        extra = extra_rows(channels, half)
        upper = lax.axis_index("dp") >= half
        rows_low, rows_high = (row for _, row in bias_places(half, per_source))
        shares, biases = [], []
        for array, at in places:
            begin = at + per_source * all_columns
            shares.append(unpack_terms(share, line_refs[array][begin : begin + extra]))
            low, high = (
                unpack_terms(1, line_refs[array][at + row * all_columns : at + row * all_columns + columns])
                for row in (rows_low, rows_high)
            )
            biases.append(jnp.where(upper, high, low))
        for source, rows in enumerate(in_relative_order(shares, half)):
            local_ref[source * share : (source + 1) * share] = rows
        bias_ref[...] = in_relative_order(biases, half)[0]


def final_call(table, lines, places, delta, local_weight):
    grid_rows, columns, channels = delta.shape
    rows = table.shape[1]
    block = min(16, columns)
    field = pl.BlockSpec((grid_rows, block, channels), lambda i: (0, i, 0))
    return pl.pallas_call(
        functools.partial(final_kernel, places, len(lines)),
        grid=(columns // block,),
        in_specs=[whole(line.shape) for line in lines] + [field, whole(local_weight.shape), whole(table.shape)],
        out_specs=[field, whole((channels, channels)), whole((1, channels))],
        out_shape=[
            jax.ShapeDtypeStruct(delta.shape, bf16),
            jax.ShapeDtypeStruct((channels, channels), f32),
            jax.ShapeDtypeStruct((1, channels), f32),
        ],
        compiler_params=params(),
        cost_estimate=pl.CostEstimate(
            flops=2 * (rows + channels) * delta.size, bytes_accessed=5 * delta.size, transcendentals=0
        ),
        name="x_inverse_and_local",
    )(*lines, delta, local_weight, table)


def on_device(field_in, pre_act, cotangent, spec_weight, local_weight):
    batch_size, slab_rows, col_block, channels = field_in.shape
    space_count = lax.axis_size("space")
    data_count = lax.axis_size("dp")
    grid_rows = slab_rows * space_count
    grid_cols = col_block * data_count
    kx_local, ky_local = spec_weight.shape[:2]
    half = data_count // 2
    half_cols = half * col_block
    row_count = 2 * (kx_local + 1)
    data_index = lax.axis_index("dp")
    space_index = lax.axis_index("space")
    upper = data_index // half

    sizes = (half, kx_local, slab_rows, grid_rows)

    blocks = 2 * space_count
    size = 2 * ky_local
    row = jnp.arange(blocks * size, dtype=jnp.int32)
    block, inner = row // size, row % size
    shift = block % space_count
    ky_index = (space_index + shift) % space_count * ky_local + inner // 2
    quarter = grid_cols // 4
    cosine_turn = inner % 2
    sine_turn = jnp.where((block // space_count) == upper, 1 + inner % 2, 3 * (1 - inner % 2))
    turn = jnp.concatenate(
        [
            jnp.broadcast_to(cosine_turn[:, None], (blocks * size, half_cols)),
            jnp.broadcast_to(sine_turn[:, None], (blocks * size, half_cols)),
        ],
        axis=1,
    )

    def y_basis(flip):
        column = jnp.arange(half_cols, dtype=jnp.int32)
        member = (column // col_block) ^ flip
        positions = upper * half_cols + member * col_block + column % col_block
        positions = jnp.concatenate([positions, positions])
        return cosine_table(ky_index[:, None] * positions[None, :] + quarter * turn, grid_cols)

    ky_row = space_index * ky_local + jnp.arange(size, dtype=jnp.int32) // 2
    scale = jnp.where(ky_row == 0, 1.0, 2.0).astype(f32) / (grid_rows * grid_cols)
    scale_rows = jnp.broadcast_to(scale[:, None], (size, channels))

    halves = [list(range(half)), list(range(half, data_count))]

    def exchange(values):
        return lax.all_to_all(
            values, "dp", split_axis=0, concat_axis=0, tiled=True, axis_index_groups=halves
        )

    def to_chips(chips):
        arrived = {0: chips[0]}
        for pair in reversed(range(1, half // 2)):
            moves = [(d, d ^ (2 * pair)) for d in range(data_count)]
            arrived[pair] = lax.ppermute(chips[pair], "dp", moves)
        return [arrived[pair] for pair in range(half // 2)]

    def between_cores(arrived):
        rows = arrived[0].shape[0] // 2
        mates = jnp.concatenate([part[rows:] for part in arrived], axis=0)
        mates = lax.ppermute(mates, "dp", [(d, d ^ 1) for d in range(data_count)])
        places = [
            (source // 2, 0) if source % 2 == 0 else (half // 2, source // 2 * rows)
            for source in range(half)
        ]
        return arrived + [mates], places

    def pairs(mirror, shift):
        moves = []
        for d in range(data_count):
            for s in range(space_count):
                target = data_count - 1 - d if mirror else d
                moves.append(
                    (d * space_count + s, target * space_count + (s + shift) % space_count)
                )
        return moves

    order = [(mirror, shift) for mirror in (1, 0) for shift in reversed(range(space_count))][:-1]

    def gathered(parts):
        held = [parts[0]]
        for mirror, shift in order:
            held.append(
                lax.ppermute(
                    parts[mirror * space_count + shift], ("dp", "space"), pairs(mirror, shift)
                )
            )
        return held

    tied = lax.optimization_barrier

    share = channels // half
    extra = extra_rows(channels, half)

    message = row_count * col_block
    y_table = y_basis(0)
    relative_table = y_basis(data_index % half)

    arrived = to_chips(input_call(sizes, field_in[0]))
    delta, delta_sums = delta_call(sizes, pre_act[0], cotangent[0], field_in[0])
    delta_sums, arrived = tied((delta_sums, arrived))
    delta_lines = exchange(delta_sums)
    lines, places = between_cores(arrived)
    input_parts = list(
        y_transform_call(
            relative_table, lines, places, message, blocks, space_count, col_block, 0
        )
    )
    for shift in range(1, space_count):
        input_parts[shift] = lax.ppermute(input_parts[shift], ("dp", "space"), pairs(0, shift))
    held_rows = kx_local * size
    mirrored = sum(part[held_rows:].astype(f32) for part in input_parts).astype(bf16)
    delta_lines, mirrored = tied((delta_lines, mirrored))

    message += extra
    delta_parts = y_transform_call(
        y_table,
        [delta_lines.reshape(half * message, channels)],
        [(0, source * message) for source in range(half)],
        message,
        blocks,
        blocks,
        col_block,
        extra,
    )
    delta_parts = list(delta_parts)
    rows = delta_parts[space_count].shape[0]
    delta_parts[space_count] = jnp.concatenate([delta_parts[space_count], mirrored], axis=0)
    weight, delta_parts = tied((spec_weight, delta_parts))
    weight = load_call(weight)
    delta_held = gathered(delta_parts)
    place = 1 + order.index((1, 0))
    input_held = [(part, 0) for part in input_parts] + [(delta_held[place][rows:], 0)]
    delta_held[place] = delta_held[place][:rows]
    back, delta_owned, share_rows = back_call(scale_rows, weight, delta_held, share)
    received = {(0, 0): back}
    for mirror, shift in order:
        received[(mirror, -shift % space_count)] = lax.ppermute(
            back, ("dp", "space"), pairs(mirror, shift)
        )
    modes = [received[(mirror, shift)] for mirror in (0, 1) for shift in range(space_count)]
    column_sums = y_inverse_call(relative_table, share_rows, modes, half, col_block)
    column_sums, delta_owned = tied((column_sums, delta_owned))
    columns = to_chips(column_sums)
    grad_spectral, x_basis = outer_call(sizes, scale_rows, delta_owned, input_held)
    columns, grad_spectral = tied((columns, grad_spectral))
    lines, places = between_cores(columns)
    grad_input, grad_local, bias_rows = final_call(x_basis, lines, places, delta, local_weight)
    return (grad_input[None], grad_spectral, grad_local, bias_rows.reshape(channels))


def solution(mesh):
    placed = (
        P(None, "space", "dp", None),
        P(None, "space", "dp", None),
        P(None, "space", "dp", None),
        P("dp", "space", None, None, None),
        P(),
    )
    return jax.shard_map(
        on_device,
        mesh=mesh,
        in_specs=placed,
        out_specs=(P(None, "space", "dp", None), P("dp", "space", None, None, None), P(), P()),
        check_vma=False,
    )
```
